32 devices in a mesh: ctx: 4 (over z), fsdp: 8 (over y, x, core).
Axes of the slice: x: 2, y: 2, z: 4, core: 2. Of those that a mesh axis runs over, the one named last changes fastest.
Arguments:
- tokens: bfloat16 [8, 8, 128, 2048], P('fsdp', 'ctx'), may hold values from -6 to 6
- pairs: int32 [4, 2], replicated, may hold values from 0 to 7, as said below
- valid: int32 [8, 8, 128], P('fsdp', 'ctx'), may hold values from 0 to 1, as said below
- teacher: bfloat16 [8, 8, 128, 2048], P('fsdp', 'ctx'), may hold values from -6 to 6
- w_query: bfloat16 [2048, 2048], P('fsdp'), may hold values from -0.125 to 0.125
- w_key: bfloat16 [2048, 2048], P('fsdp'), may hold values from -0.125 to 0.125
- w_value: bfloat16 [2048, 2048], P('fsdp'), may hold values from -0.125 to 0.125
- w_out: bfloat16 [2048, 2048], P('fsdp'), may hold values from -0.5 to 0.5
- w_gate: bfloat16 [2048, 8192], P('fsdp'), may hold values from -0.125 to 0.125
- w_up: bfloat16 [2048, 8192], P('fsdp'), may hold values from -0.125 to 0.125
- w_down: bfloat16 [8192, 2048], P('fsdp'), may hold values from -0.0625 to 0.0625
Outputs:
- activations: bfloat16 [8, 8, 128, 2048], P('fsdp', 'ctx')
- loss: float32 [], replicated
- input_grad: float32 [8, 8, 128, 2048], P('fsdp', 'ctx')
- grad_query: float32 [2048, 2048], P(('ctx', 'fsdp'))
- grad_key: float32 [2048, 2048], P(('ctx', 'fsdp'))
- grad_value: float32 [2048, 2048], P(('ctx', 'fsdp'))
- grad_out: float32 [2048, 2048], P(('ctx', 'fsdp'))
- grad_gate: float32 [2048, 8192], P(('ctx', 'fsdp'))
- grad_up: float32 [2048, 8192], P(('ctx', 'fsdp'))
- grad_down: float32 [8192, 2048], P(('ctx', 'fsdp'))
The draws below stay inside these ranges and needn't reach their ends.
Inputs may be any that keep to these rules, and one draw needn't show every extreme that they name: `pairs`: row r lists some block j and block 7 - j, in either order; each j stands in exactly one row. `valid`: 1 marks a token that the loss counts; the first token of slot 0 of every sequence always counts.
All inputs are finite; a program needn't handle non-finite values.
Results may differ from the reference program's by a relative error of at most 0.015.
Values may be sent and summed in bfloat16 or wider, within the bound.
No kernel may reach another device: no remote copies, remote signals or barrier semaphores. Data moves between devices by JAX's collectives and lax.ppermute only.
A program may use at most 640 MiB of HBM per device.

```python
import jax
import jax.numpy as jnp
from jax import lax

D = 2048
HEADS = 16
HD = 128
FF = 8192
BLK = 128
SEQS = 8
SLOTS = 8
LEN = 1024
TOKENS = 8192
N_CTX = 4


def draw_pairs(key, part):
    key = jax.random.fold_in(key, 11)
    order_key, flip_key = jax.random.split(key)
    chosen = jax.random.permutation(order_key, N_CTX).astype(jnp.int32)
    partner = 2 * N_CTX - 1 - chosen
    flip_bits = jax.random.randint(flip_key, (N_CTX,), 0, 2)
    leading = jnp.where(flip_bits == 1, partner, chosen)
    trailing = jnp.where(flip_bits == 1, chosen, partner)
    return jnp.stack([leading, trailing], 1).astype(jnp.int32)


def draw_valid(key, part):
    key = jax.random.fold_in(key, 23)
    tickets = jax.random.randint(key, (SEQS, 2 * N_CTX, BLK), 0, 4 * SEQS)
    thresholds = SEQS + 2 * jnp.arange(SEQS, dtype=jnp.int32)
    drawn = tickets < thresholds[:, None, None]
    first_slot = jnp.arange(2 * N_CTX, dtype=jnp.int32)[:, None] == 0
    first_token = jnp.arange(BLK, dtype=jnp.int32)[None, :] == 0
    forced = jnp.logical_and(first_slot, first_token)[None, :, :]
    return jnp.logical_or(drawn, forced).astype(jnp.int32)


def levels(own_key, dims, shards, smallest, largest):
    loudness, own = 1.0, jax.random.fold_in(own_key, 6)
    for dim, shards_of in shards:
        heights = jnp.exp(jax.random.uniform(jax.random.fold_in(own, dim), (shards_of,), jnp.float32, smallest / len(shards), largest / len(shards)))
        loudness = loudness * jnp.repeat(heights, dims[dim] // shards_of).reshape([-1 if axis == dim else 1 for axis in range(len(dims))])
    return loudness


def noise(stream_key, extent, spread, most, shards=(), held_as=jnp.bfloat16):
    array = spread * jax.random.normal(stream_key, extent, jnp.float32)
    if shards:
        array = array * levels(stream_key, extent, shards, -0.22, 0.18)
    return jnp.clip(array, -most, most).astype(held_as)


def setup_inputs(seed: int = 0) -> dict:
    seeds = jax.random.split(jax.random.key(seed), 12)
    return {
        "tokens": noise(seeds[0], (SEQS, SLOTS, BLK, D), 1.0, 6.0, ((0, 8), (1, 4))),
        "pairs": draw_pairs(jax.random.fold_in(seeds[11], 71), 0),
        "valid": draw_valid(jax.random.fold_in(seeds[11], 71), 0),
        "teacher": noise(seeds[3], (SEQS, SLOTS, BLK, D), 1.0, 6.0, ((0, 8), (1, 4))),
        "w_query": noise(seeds[4], (D, D), D ** -0.5, 0.125, ((0, 8),)),
        "w_key": noise(seeds[5], (D, D), D ** -0.5, 0.125, ((0, 8),)),
        "w_value": noise(seeds[6], (D, D), D ** -0.5, 0.125, ((0, 8),)),
        "w_out": noise(seeds[7], (D, D), (D // 16) ** -0.5, 0.5, ((0, 8),)),
        "w_gate": noise(seeds[8], (D, FF), D ** -0.5, 0.125, ((0, 8),)),
        "w_up": noise(seeds[9], (D, FF), D ** -0.5, 0.125, ((0, 8),)),
        "w_down": noise(seeds[10], (FF, D), FF ** -0.5, 0.0625, ((0, 8),)),
    }


@jax.custom_vjp
def low(v):
    return lax.optimization_barrier(v.astype(jnp.bfloat16)).astype(jnp.float32)

@jax.custom_vjp
def low_back(v):
    return v

def low_keep(v):
    return (low(v), None)

def low_pass(kept, grad):
    return (grad,)

def back_keep(v):
    return (v, None)

def back_low(kept, grad):
    return (low(grad),)
low.defvjp(low_keep, low_pass)
low_back.defvjp(back_keep, back_low)
epsilon = 1e-05
highest = lax.Precision.HIGHEST

def normalize(stream_rows):
    centered = stream_rows - lax.optimization_barrier(jnp.mean(stream_rows, -1, keepdims=True))
    variance = lax.optimization_barrier(jnp.mean(centered * centered, -1, keepdims=True))
    return centered * lax.rsqrt(variance + epsilon)

def product(left, right):
    return jnp.dot(left, right, precision=highest, preferred_element_type=jnp.float32)

def angles(blocks):
    offsets = jnp.arange(BLK, dtype=jnp.int32)
    positions = (blocks.astype(jnp.int32)[:, None] * BLK + offsets[None, :]).reshape(-1).astype(jnp.float32)
    frequency = 10000.0 ** (-2.0 * jnp.arange(HD // 2, dtype=jnp.float32) / HD)
    phases = positions[:, None] * frequency[None, :]
    return (jnp.cos(phases)[:, None, :], jnp.sin(phases)[:, None, :])

def rotate(values, cosine_table, sine_table):
    half_width = values.shape[-1] // 2
    leading = values[..., :half_width]
    trailing = values[..., half_width:]
    return jnp.concatenate([leading * cosine_table - trailing * sine_table, trailing * cosine_table + leading * sine_table], -1)

def reference(tokens, pairs, valid, teacher, w_query, w_key, w_value, w_out, w_gate, w_up, w_down):
    all_blocks = pairs.reshape(-1)
    cosine_table, sine_table = angles(all_blocks)
    block_ids = jnp.repeat(all_blocks, BLK)
    allowed = block_ids[None, :] <= block_ids[:, None]
    query_scale = HD ** (-0.5)
    shaped = (SEQS, LEN, HEADS, HD)

    def attend(inputs):
        query, keys, values = inputs
        scores = low_back(jnp.einsum('qhd,khd->hqk', query, keys, precision=highest))
        scores = jnp.where(allowed[None], scores, -1e+30)
        attn_probs = low(jax.nn.softmax(scores, axis=-1))
        return jnp.einsum('hqk,khd->qhd', attn_probs, values, precision=highest)

    def forward(stream, query_weight, key_weight, value_weight, out_weight, gate_weight, up_weight, down_weight):
        stream_rows = stream.reshape(-1, D)
        normed_one = low(normalize(stream_rows))
        query_raw = low_back(product(normed_one, query_weight)).reshape(shaped)
        key_raw = low_back(product(normed_one, key_weight)).reshape(shaped)
        value_raw = low_back(product(normed_one, value_weight)).reshape(shaped)
        query = low(rotate(query_raw, cosine_table, sine_table) * query_scale)
        keys = low(rotate(key_raw, cosine_table, sine_table))
        values = low(value_raw)
        mixed = lax.map(jax.checkpoint(attend), (query, keys, values))
        attended = low(low_back(mixed.reshape(-1, D)))
        residual = stream_rows + low_back(product(attended, out_weight))
        normed_two = low(normalize(residual))
        gate_pre = low_back(product(normed_two, gate_weight))
        up_pre = low_back(product(normed_two, up_weight))
        hidden = low(jax.nn.silu(gate_pre) * up_pre)
        output = residual + low_back(product(hidden, down_weight))
        deviation = output - teacher.reshape(-1, D).astype(jnp.float32)
        valid_float = valid.reshape(-1).astype(jnp.float32)
        valid_count = jnp.sum(valid_float)
        loss_value = jnp.sum(valid_float[:, None] * deviation * deviation) / (valid_count * D)
        return (loss_value, output)
    loss_value, pullback, output = jax.vjp(forward, tokens.astype(jnp.float32), w_query.astype(jnp.float32), w_key.astype(jnp.float32), w_value.astype(jnp.float32), w_out.astype(jnp.float32), w_gate.astype(jnp.float32), w_up.astype(jnp.float32), w_down.astype(jnp.float32), has_aux=True)
    gradients = pullback(jnp.asarray(TOKENS * D // 2, jnp.float32))
    activations = output.reshape(SEQS, SLOTS, BLK, D).astype(jnp.bfloat16)
    return (activations, loss_value, gradients[0], gradients[1], gradients[2], gradients[3], gradients[4], gradients[5], gradients[6], gradients[7])
```

```python
import functools

import jax
import jax.numpy as jnp
from jax import lax
from jax.experimental import pallas as pl
from jax.experimental.pallas import tpu as pltpu
from jax.sharding import PartitionSpec as P

HD = 128
EPS = 1e-05
BF = jnp.bfloat16
F32 = jnp.float32
NEG = -1e30


def normalize(rows):
    centered = rows - jnp.mean(rows, -1, keepdims=True)
    inverse = lax.rsqrt(jnp.mean(centered * centered, -1, keepdims=True) + EPS)
    return centered * inverse, inverse


def norm_back(gradient, normed, inverse):
    centered = gradient - jnp.mean(gradient, -1, keepdims=True)
    return inverse * (centered - normed * jnp.mean(gradient * normed, -1, keepdims=True))


def mm(left, right):
    return jnp.dot(left, right, preferred_element_type=F32)


def mm_t(left, right):
    return lax.dot_general(left, right, (((1,), (1,)), ((), ())), preferred_element_type=F32)


def mm_rows(left, right):
    return lax.dot_general(left, right, (((0,), (0,)), ((), ())), preferred_element_type=F32)


def tables(length):
    frequency = 10000.0 ** (-2.0 * jnp.arange(HD // 2, dtype=F32) / HD)
    phases = jnp.arange(length, dtype=F32)[:, None] * frequency[None, :]
    cosine, sine = jnp.cos(phases), jnp.sin(phases)
    return jnp.concatenate([cosine, cosine], 1), jnp.concatenate([-sine, sine], 1)


def fwd_kernel(heads, order, qkv, cos, sin, out, lse, q_s, k_s, v_s):
    planes, _, slots, blk, _ = qkv.shape
    blocks = planes * slots
    scale = HD ** -0.5

    def head(h, carry):
        col = pl.multiple_of(h * HD, HD)

        def load(b, carry):
            where = order[b]
            s, t = where // slots, where % slots
            row = pl.ds(pl.multiple_of(b * blk, blk), blk)
            c, n = cos[row, :], sin[row, :]
            q = qkv[s, 0, t, :, pl.ds(col, HD)]
            k = qkv[s, 0, t, :, pl.ds(pl.multiple_of(heads * HD + col, HD), HD)]
            q_s[row, :] = ((q * c + pltpu.roll(q, HD // 2, 1) * n) * scale).astype(BF)
            k_s[row, :] = (k * c + pltpu.roll(k, HD // 2, 1) * n).astype(BF)
            v_s[row, :] = qkv[s, 0, t, :, pl.ds(pl.multiple_of(2 * heads * HD + col, HD), HD)].astype(BF)
            return carry

        lax.fori_loop(0, blocks, load, 0)
        for b in range(blocks):
            keys = (b + 1) * blk
            scores = mm_t(q_s[b * blk : keys, :], k_s[0:keys, :])
            top = jnp.max(scores, -1, keepdims=True)
            raised = jnp.exp(scores - top)
            total = jnp.sum(raised, -1, keepdims=True)
            probs = (raised * (1.0 / total)).astype(BF)
            mixed = mm(probs, v_s[0:keys, :])
            where = order[b]
            s, t = where // slots, where % slots
            out[s, 0, t, :, pl.ds(col, HD)] = mixed.astype(BF)
            lse[s, 0, t, :, pl.ds(col, HD)] = jnp.broadcast_to(top + jnp.log(total), (blk, HD))
        return carry

    lax.fori_loop(0, heads, head, 0)


def bwd_kernel(heads, order, qkv, lse, grad, cos, sin, dqkv, q_s, k_s, v_s, g_s, l_s, dk_s, dv_s):
    planes, _, slots, blk, _ = qkv.shape
    blocks = planes * slots
    scale = HD ** -0.5

    def head(h, carry):
        col = pl.multiple_of(h * HD, HD)
        kcol = pl.multiple_of(heads * HD + col, HD)
        vcol = pl.multiple_of(2 * heads * HD + col, HD)

        def load(b, carry):
            where = order[b]
            s, t = where // slots, where % slots
            row = pl.ds(pl.multiple_of(b * blk, blk), blk)
            c, n = cos[row, :], sin[row, :]
            q = qkv[s, 0, t, :, pl.ds(col, HD)]
            k = qkv[s, 0, t, :, pl.ds(kcol, HD)]
            q_s[row, :] = ((q * c + pltpu.roll(q, HD // 2, 1) * n) * scale).astype(BF)
            k_s[row, :] = (k * c + pltpu.roll(k, HD // 2, 1) * n).astype(BF)
            v_s[row, :] = qkv[s, 0, t, :, pl.ds(vcol, HD)].astype(BF)
            g_s[row, :] = grad[s, 0, t, :, pl.ds(col, HD)]
            l_s[row, :] = lse[s, 0, t, :, pl.ds(col, HD)]
            return carry

        lax.fori_loop(0, blocks, load, 0)
        dk_s[...] = jnp.zeros_like(dk_s)
        dv_s[...] = jnp.zeros_like(dv_s)
        for b in range(blocks):
            keys = (b + 1) * blk
            mine = slice(b * blk, keys)
            scores = mm_t(q_s[mine, :], k_s[0:keys, :])
            probs = jnp.exp(scores - l_s[mine, 0:1])
            dprobs = mm_t(g_s[mine, :], v_s[0:keys, :])
            delta = jnp.sum(probs * dprobs, -1, keepdims=True)
            dscores = (probs * (dprobs - delta)).astype(BF)
            dq = mm(dscores, k_s[0:keys, :]) * scale
            dk_s[0:keys, :] += mm_rows(dscores, q_s[mine, :])
            dv_s[0:keys, :] += mm_rows(probs.astype(BF), g_s[mine, :])
            where = order[b]
            s, t = where // slots, where % slots
            dq = dq * cos[mine, :] - pltpu.roll(dq, HD // 2, 1) * sin[mine, :]
            dqkv[s, 0, t, :, pl.ds(col, HD)] = dq.astype(BF)

        def store(b, carry):
            where = order[b]
            s, t = where // slots, where % slots
            row = pl.ds(pl.multiple_of(b * blk, blk), blk)
            dk = dk_s[row, :]
            dk = dk * cos[row, :] - pltpu.roll(dk, HD // 2, 1) * sin[row, :]
            dqkv[s, 0, t, :, pl.ds(kcol, HD)] = dk.astype(BF)
            dqkv[s, 0, t, :, pl.ds(vcol, HD)] = dv_s[row, :].astype(BF)
            return carry

        lax.fori_loop(0, blocks, store, 0)
        return carry

    lax.fori_loop(0, heads, head, 0)


VMEM_LIMIT = 56 * 1024 * 1024


def attend(order, qkv, cos, sin, heads):
    planes, seqs, slots, blk, width = qkv.shape
    length = planes * slots * blk
    spec = lambda w: pl.BlockSpec((planes, 1, slots, blk, w), lambda i, o: (0, i, 0, 0, 0))
    table = pl.BlockSpec((length, HD), lambda i, o: (0, 0))
    return pl.pallas_call(
        functools.partial(fwd_kernel, heads),
        grid_spec=pltpu.PrefetchScalarGridSpec(
            num_scalar_prefetch=1,
            grid=(seqs,),
            in_specs=[spec(width), table, table],
            out_specs=[spec(heads * HD), spec(heads * HD)],
            scratch_shapes=[pltpu.VMEM((length, HD), BF)] * 3,
        ),
        out_shape=[
            jax.ShapeDtypeStruct((planes, seqs, slots, blk, heads * HD), BF),
            jax.ShapeDtypeStruct((planes, seqs, slots, blk, heads * HD), F32),
        ],
        compiler_params=pltpu.CompilerParams(vmem_limit_bytes=VMEM_LIMIT),
        cost_estimate=pl.CostEstimate(
            flops=seqs * heads * length * length * HD * 4, bytes_accessed=seqs * length * width * 6, transcendentals=0
        ),
        name="attend",
    )(order, qkv, cos, sin)


def attend_back(order, qkv, lse, grad, cos, sin, heads):
    planes, seqs, slots, blk, width = qkv.shape
    length = planes * slots * blk
    spec = lambda w: pl.BlockSpec((planes, 1, slots, blk, w), lambda i, o: (0, i, 0, 0, 0))
    table = pl.BlockSpec((length, HD), lambda i, o: (0, 0))
    return pl.pallas_call(
        functools.partial(bwd_kernel, heads),
        grid_spec=pltpu.PrefetchScalarGridSpec(
            num_scalar_prefetch=1,
            grid=(seqs,),
            in_specs=[spec(width), spec(heads * HD), spec(heads * HD), table, table],
            out_specs=spec(width),
            scratch_shapes=[pltpu.VMEM((length, HD), BF)] * 4 + [pltpu.VMEM((length, HD), F32)] * 3,
        ),
        out_shape=jax.ShapeDtypeStruct((planes, seqs, slots, blk, width), BF),
        compiler_params=pltpu.CompilerParams(vmem_limit_bytes=VMEM_LIMIT),
        cost_estimate=pl.CostEstimate(
            flops=seqs * heads * length * length * HD * 10, bytes_accessed=seqs * length * width * 12, transcendentals=0
        ),
        name="attend_back",
    )(order, qkv, lse, grad, cos, sin)


TILE = 256


def up_kernel(count, *refs):
    hs, (wg, wu, wd) = refs[:count], refs[count : count + 3]
    refs = refs[count + 3 :]
    refs = refs[4:] if len(refs) > count + 6 else refs
    h_all, g_out, u_out, hidden_out = refs[:4]
    outs, (held, total) = refs[4 : 4 + count], refs[4 + count :]
    step = pl.program_id(0)
    rows = hs[0].shape[0]

    @pl.when(step == 0)
    def _():
        for i in range(count):
            held[i * rows : (i + 1) * rows, :] = hs[i][...]
        h_all[...] = held[...]
        total[...] = jnp.zeros_like(total)

    h = held[...]
    g, u = mm(h, wg[...]), mm(h, wu[...])
    hidden = (g * (1.0 / (1.0 + jnp.exp(-g))) * u).astype(BF)
    g_out[...], u_out[...], hidden_out[...] = g, u, hidden
    total[...] += mm(hidden, wd[...])

    @pl.when(step == pl.num_programs(0) - 1)
    def _():
        for i in range(count):
            outs[i][...] = total[i * rows : (i + 1) * rows, :].astype(outs[i].dtype)


def mlp(hs, gu_w, down_w, types, parts, which, held=None):
    rows, width = hs[0].shape
    part_ff = down_w.shape[0]
    count, tiles = len(hs), part_ff // TILE
    span = rows * count
    whole = pl.BlockSpec((rows, width), lambda i: (0, 0))
    tile = pl.BlockSpec((span, TILE), lambda i: (which, i))
    kept = [(width, BF), (part_ff, F32), (part_ff, F32), (part_ff, BF)]
    extra = [] if held is None else list(held)
    result = pl.pallas_call(
        functools.partial(up_kernel, count),
        grid=(tiles,),
        in_specs=[whole] * count
        + [
            pl.BlockSpec((width, TILE), lambda i: (0, i)),
            pl.BlockSpec((width, TILE), lambda i: (0, tiles + i)),
            pl.BlockSpec((TILE, width), lambda i: (i, 0)),
        ]
        + [pl.BlockSpec(memory_space=pl.ANY)] * len(extra),
        out_specs=[pl.BlockSpec((span, width), lambda i: (which, 0)), tile, tile, tile] + [whole] * count,
        out_shape=[jax.ShapeDtypeStruct((span * parts, w), t) for w, t in kept]
        + [jax.ShapeDtypeStruct((rows, width), t) for t in types],
        scratch_shapes=[pltpu.VMEM((span, width), BF), pltpu.VMEM((span, width), F32)],
        input_output_aliases={count + 3 + i: i for i in range(len(extra))},
        compiler_params=pltpu.CompilerParams(vmem_limit_bytes=48 * 1024 * 1024),
        cost_estimate=pl.CostEstimate(
            flops=6 * span * width * part_ff, bytes_accessed=6 * width * part_ff + 14 * span * part_ff, transcendentals=0
        ),
        name="mlp",
    )(*hs, gu_w, gu_w, down_w, *extra)
    return result[:4], result[4:]


def down_kernel(count, *refs):
    ds, (g_in, u_in, wg, wu, wd) = refs[:count], refs[count : count + 5]
    refs = refs[count + 5 :]
    refs = refs[3:] if len(refs) > count + 5 else refs
    d_all, dg_out, du_out = refs[:3]
    outs, (held, total) = refs[3 : 3 + count], refs[3 + count :]
    step = pl.program_id(0)
    rows = ds[0].shape[0]

    @pl.when(step == 0)
    def _():
        for i in range(count):
            held[i * rows : (i + 1) * rows, :] = ds[i][...]
        d_all[...] = held[...]
        total[...] = jnp.zeros_like(total)

    dh = mm_t(held[...], wd[...])
    g = g_in[...]
    sig = 1.0 / (1.0 + jnp.exp(-g))
    dg = (dh * u_in[...] * sig * (1.0 + g * (1.0 - sig))).astype(BF)
    du = (dh * (g * sig)).astype(BF)
    dg_out[...], du_out[...] = dg, du
    total[...] += mm_t(dg, wg[...]) + mm_t(du, wu[...])

    @pl.when(step == pl.num_programs(0) - 1)
    def _():
        for i in range(count):
            outs[i][...] = total[i * rows : (i + 1) * rows, :].astype(outs[i].dtype)


def mlp_back(ds, g, u, gu_w, down_w, types, parts, which, held=None):
    rows, width = ds[0].shape
    part_ff = down_w.shape[0]
    count, tiles = len(ds), part_ff // TILE
    span = rows * count
    whole = pl.BlockSpec((rows, width), lambda i: (0, 0))
    tile = pl.BlockSpec((span, TILE), lambda i: (which, i))
    kept = [(width, BF), (part_ff, BF), (part_ff, BF)]
    extra = [] if held is None else list(held)
    result = pl.pallas_call(
        functools.partial(down_kernel, count),
        grid=(tiles,),
        in_specs=[whole] * count
        + [
            tile,
            tile,
            pl.BlockSpec((width, TILE), lambda i: (0, i)),
            pl.BlockSpec((width, TILE), lambda i: (0, tiles + i)),
            pl.BlockSpec((TILE, width), lambda i: (i, 0)),
        ]
        + [pl.BlockSpec(memory_space=pl.ANY)] * len(extra),
        out_specs=[pl.BlockSpec((span, width), lambda i: (which, 0)), tile, tile] + [whole] * count,
        out_shape=[jax.ShapeDtypeStruct((span * parts, w), t) for w, t in kept]
        + [jax.ShapeDtypeStruct((rows, width), t) for t in types],
        scratch_shapes=[pltpu.VMEM((span, width), BF), pltpu.VMEM((span, width), F32)],
        input_output_aliases={count + 5 + i: i for i in range(len(extra))},
        compiler_params=pltpu.CompilerParams(vmem_limit_bytes=48 * 1024 * 1024),
        cost_estimate=pl.CostEstimate(
            flops=6 * span * width * part_ff, bytes_accessed=6 * width * part_ff + 12 * span * part_ff, transcendentals=0
        ),
        name="mlp_back",
    )(*ds, g, u, gu_w, gu_w, down_w, *extra)
    return result[:3], result[3:]


def assemble(places, pieces):
    count = len(pieces)
    depth, width = pieces[0].shape

    def kernel(places, *refs):
        sources, out, held, arrive, leave = refs[:count], *refs[count:]
        ins = [pltpu.make_async_copy(sources[i], held.at[i], arrive.at[i]) for i in range(count)]
        outs = [pltpu.make_async_copy(held.at[i], out.at[places[i]], leave.at[i]) for i in range(count)]
        for copy in ins:
            copy.start()
        for i in range(count):
            ins[i].wait()
            outs[i].start()
        for copy in outs:
            copy.wait()

    return pl.pallas_call(
        kernel,
        grid_spec=pltpu.PrefetchScalarGridSpec(
            num_scalar_prefetch=1,
            grid=(1,),
            in_specs=[pl.BlockSpec(memory_space=pl.ANY)] * count,
            out_specs=pl.BlockSpec(memory_space=pl.ANY),
            scratch_shapes=[
                pltpu.VMEM((count, depth, width), pieces[0].dtype),
                pltpu.SemaphoreType.DMA((count,)),
                pltpu.SemaphoreType.DMA((count,)),
            ],
        ),
        out_shape=jax.ShapeDtypeStruct((count, depth, width), pieces[0].dtype),
        compiler_params=pltpu.CompilerParams(vmem_limit_bytes=VMEM_LIMIT),
        name="assemble",
    )(places, *pieces).reshape(count * depth, width)


def take_columns(which, arrays, groups, members):
    depth, width = arrays[0].shape
    part = width // (groups * members)
    kept = len(which)
    if part % HD:
        views = [v.reshape(depth, groups, members, part) for v in arrays]
        return [
            jnp.concatenate(
                [lax.dynamic_slice_in_dim(v, k, 1, 2).reshape(depth, groups * part) for v in views], 1
            )
            for k in which
        ]

    def kernel(which, *refs):
        sources, outs = refs[: len(arrays)], refs[len(arrays) :]
        for k in range(kept):
            for n, source in enumerate(sources):
                for i in range(groups):
                    start = pl.multiple_of(i * members * part + which[k] * part, HD)
                    outs[k][:, (n * groups + i) * part : (n * groups + i + 1) * part] = source[:, pl.ds(start, part)]

    tile = min(64, depth)
    return pl.pallas_call(
        kernel,
        grid_spec=pltpu.PrefetchScalarGridSpec(
            num_scalar_prefetch=1,
            grid=(depth // tile,),
            in_specs=[pl.BlockSpec((tile, width), lambda i, w: (i, 0))] * len(arrays),
            out_specs=[pl.BlockSpec((tile, len(arrays) * groups * part), lambda i, w: (i, 0))] * kept,
        ),
        out_shape=[jax.ShapeDtypeStruct((depth, len(arrays) * groups * part), arrays[0].dtype)] * kept,
        name="take_columns",
    )(jnp.stack(which).astype(jnp.int32), *arrays)


def body(planes, shards, tokens, pairs, valid, teacher, w_query, w_key, w_value, w_out, w_gate, w_up, w_down):
    seqs, slots, blk, width = tokens.shape
    ff = w_gate.shape[1]
    rows = seqs * slots * blk
    world = planes * shards
    near = planes // 2
    all_heads = width // HD
    heads = all_heads // planes
    mine = heads * HD
    own_rows = width // shards
    part_ff = ff // planes
    length = planes * slots * blk
    unit = width // world
    both = ("ctx", "fsdp")

    c, f = lax.axis_index("ctx"), lax.axis_index("fsdp")
    far, low = c // near, c % near
    core, x, y = f % 2, f // 2 % 2, f // 4
    group = x * near + low

    def after(array, *others):
        return lax.optimization_barrier((array, *others))[0]

    def flip(array, bits):
        return lax.ppermute(array, "fsdp", [(i, i ^ bits) for i in range(shards)])

    def flip_ctx(array, bits):
        return lax.ppermute(array, "ctx", [(i, i ^ bits) for i in range(planes)])

    def hop(array, j):
        dx, dz = j // near, j % near
        if dz == 0:
            return flip(array, 2 * dx)
        if dx == 0:
            return flip_ctx(array, dz)
        return lax.ppermute(
            array,
            both,
            [(p * shards + s, (p ^ dz) * shards + (s ^ 2)) for p in range(planes) for s in range(shards)],
        )

    def swap(array):
        pairs_of = []
        for p in range(planes):
            for s in range(shards):
                to = (s // 2 % 2) * near + p % near
                pairs_of.append((p * shards + s, to * shards + (s - s // 2 % 2 * 2 + p // near * 2)))
        return lax.ppermute(array, both, pairs_of)

    cos, sin = tables(length)
    ranks = jnp.argsort(pairs.reshape(-1))
    owner = ranks // slots
    relative = ((owner // near) ^ x) * near + ((owner % near) ^ low)
    order = (relative * slots + ranks % slots).astype(jnp.int32)

    def over_y(piece):
        return [flip(piece, bits) for bits in range(4, shards, 4)]

    def put(own, own_y, other, other_y):
        pieces = [own, *own_y, other, *other_y]
        keys = [0, *range(4, shards, 4), 2, *range(6, shards, 4)]
        pieces += [flip(piece, 1) for piece in pieces]
        places = jnp.stack([f ^ k for k in keys] + [f ^ k ^ 1 for k in keys]).astype(jnp.int32)
        return assemble(places, pieces)

    def head_columns(g):
        return jnp.concatenate(
            [lax.dynamic_slice_in_dim(w, g * mine, mine, 1) for w in (w_query, w_key, w_value)], 1
        )

    def ff_rows(g):
        return lax.dynamic_slice_in_dim(w_down, g * (part_ff // shards), part_ff // shards, 0)

    def own_heads(weight):
        sends, spreads = [], {}
        for p in range(planes):
            for s in range(shards):
                q = s // 2
                if q % near == p % near:
                    at = s // 4 * 4 + q // near * 2 + s % 2
                    sends.append((p * shards + s, p * shards + at))
                    for d in range(4, shards, 4):
                        spreads.setdefault(d, []).append((p * shards + at, p * shards + (at ^ d)))
        first = lax.ppermute(weight, both, sends)
        found = first
        for pairs_of in spreads.values():
            found = found + lax.ppermute(first, both, pairs_of)
        other, even = flip(found, 1), core == 0
        return jnp.concatenate([jnp.where(even, found, other), jnp.where(even, other, found)], 0)

    def gather_group(own):
        return [own] + [hop(own, j) for j in range(1, planes)]

    def reduce_group(parts):
        total = parts[0]
        for j in reversed(range(1, planes)):
            total = total + hop(parts[j].astype(BF), j).astype(F32)
        return total

    cut = planes // 2
    early = list(range(1, cut + 1))
    late = [0, *range(cut + 1, planes)]
    early_types = [BF] * cut
    late_types = [F32] + [BF] * (planes - cut - 1)
    places = early + late
    back_to = [places.index(j) for j in range(planes)]

    valid_home = valid.reshape(rows, 1)
    stream_low = swap(tokens.reshape(rows, width))
    qkv_own = head_columns(group)
    qkv_other = flip(head_columns(group ^ near), 2)
    w_qkv = put(qkv_own, over_y(qkv_own), qkv_other, over_y(qkv_other))
    valid_float = swap(after(valid_home, stream_low)).astype(F32)
    gu_own, gu_send = take_columns([group, group ^ near], [w_gate, w_up], shards, planes)

    stream = stream_low.astype(F32)
    normed_one, inverse_one = normalize(stream)
    h1 = gather_group(normed_one.astype(BF))
    gu_own_y = over_y(gu_own)
    w_out_mine = own_heads(after(w_out, *h1))
    qkv = jnp.stack([mm(h, w_qkv).reshape(seqs, slots, blk, 3 * mine) for h in h1], 0)
    gu_other = flip(after(gu_send, *h1), 2)
    qkv, w_out_mine, *gu_own_y = lax.optimization_barrier((qkv, w_out_mine, *gu_own_y))
    mixed, lse = attend(order, qkv, cos, sin, heads)
    mixed, gu_other = lax.optimization_barrier((mixed, gu_other))
    gu_other_y = over_y(gu_other)
    down_own = ff_rows(group)
    down_own_y = over_y(after(down_own, mixed))
    down_other = flip(after(ff_rows(group ^ near), gu_other), 2)
    products = [mm(mixed[s].reshape(rows, mine), w_out_mine) for s in range(planes)]
    residual = stream + reduce_group(products)

    normed_two, inverse_two = normalize(residual)
    h2 = gather_group(normed_two.astype(BF))
    gu_w = put(gu_own, gu_own_y, gu_other, gu_other_y)
    down_w = put(down_own, down_own_y, down_other, over_y(down_other))
    goal_low = swap(after(teacher, *h2).reshape(rows, width))
    kept, outs = mlp([h2[j] for j in early], gu_w, down_w, early_types, 2, 0)
    (h2_all, gates, ups, hidden_all), more = mlp([h2[j] for j in late], gu_w, down_w, late_types, 2, 1, kept)
    outs = [*outs, *more]
    output = residual + reduce_group([outs[i] for i in back_to])

    deviation = output - goal_low.astype(F32)
    grad_output = valid_float * deviation
    sums = jnp.stack([jnp.sum(grad_output * deviation), jnp.sum(valid_float)])
    sums0 = jnp.broadcast_to(sums[:, None, None], (2, 8, HD))

    for bits in range(1, planes):
        sums = sums + hop(sums0, bits) if bits > 1 else sums0 + hop(sums0, bits)
    low_grad, sums = lax.optimization_barrier((grad_output.astype(BF), sums))

    steps = [1 << b for b in reversed(range(2, shards.bit_length() - 1))]

    def halve(part, axis, bit, move, bits):
        half = part.shape[axis] // 2
        take = lambda k: lax.dynamic_slice_in_dim(part, k * half, half, axis)
        away = move(take(1 - bit), bits)
        return (take(bit).astype(F32) + away.astype(F32)).astype(BF)

    def half_of(v, k):
        return lax.dynamic_slice_in_dim(v, k * (v.shape[1] // 2), v.shape[1] // 2, 1)

    def over_core(compute):
        away = flip(compute(1 - core).astype(BF), 1)
        return (compute(core) + away.astype(F32)).astype(BF)

    def by_rows(left, right):
        return over_core(lambda k: mm_rows(half_of(left, k), right))

    def by_columns(left, right):
        part = over_core(lambda k: mm_rows(left, half_of(right, k)))
        return part.reshape(2, near, shards // 4, 2, 2, unit, part.shape[1])

    def across_y(part, axis):
        for step in steps:
            part = halve(part, axis, f // step % 2, flip, step)
        return part

    def across_far(part):
        return halve(part, 0, far, flip_ctx, near)

    def place_rows(part, place):
        homes = []
        for p in range(planes):
            for s in range(shards):
                block = ((s % 2) * (shards // 4) + s // 4) * 2 + p // near
                homes.append((p * shards + s, place(block, (s // 2 % 2) * near + p % near)))
        return lax.ppermute(part, both, homes).astype(F32)

    def place_columns(part, columns):
        half = part.shape[-1]
        part = part.reshape(near, 2, 2, unit, half)
        take = lambda v, k, axis: lax.dynamic_index_in_dim(v, k, axis, keepdims=False)
        keep, away = take(part, core, 2), flip(take(part, 1 - core, 2), 1)
        even = core == 0
        part = jnp.concatenate([jnp.where(even, keep, away), jnp.where(even, away, keep)], -1)
        pieces = []
        for j in range(planes):
            piece = take(take(part, x ^ (j // near), 1), low ^ (j % near), 0)
            pieces.append(hop(piece, j) if j else piece)
        places = jnp.stack([group ^ j for j in range(planes)]).astype(jnp.int32)
        return columns(assemble(places, pieces).reshape(planes, unit, 2 * half)).astype(F32)

    dm = gather_group(low_grad)
    for bits in [1, *(1 << b for b in range(2, shards.bit_length() - 1))]:
        sums = sums + flip(sums, bits)
    dm[1], sums = lax.optimization_barrier((dm[1], sums))
    kept, backs = mlp_back([dm[j] for j in early], gates, ups, gu_w, down_w, early_types, 2, 0)
    kept, sums = lax.optimization_barrier((kept, sums))
    sums = sums + flip_ctx(sums, near)
    (dm_all, dg_all, du_all), more = mlp_back(
        [dm[j] for j in late], gates, ups, gu_w, down_w, late_types, 2, 1, kept
    )
    backs = [*backs, *more]
    received = [hop(backs[back_to[j]], j) for j in range(1, planes)]
    g_down = by_rows(hidden_all, dm_all)
    g_gate = by_columns(h2_all, dg_all)
    g_up = by_columns(h2_all, du_all)
    received, g_down, g_gate, g_up, sums = lax.optimization_barrier((received, g_down, g_gate, g_up, sums))
    grad_two = backs[back_to[0]]
    for v in received:
        grad_two = grad_two + v.astype(F32)
    activations = swap(after(output, *received).astype(BF))
    grad_residual = grad_output + norm_back(grad_two, normed_two, inverse_two)

    dab = gather_group(grad_residual.astype(BF))
    g_down = across_y(g_down, 0)
    g_gate = across_y(g_gate, 2)
    dab, g_down, g_gate = lax.optimization_barrier((dab, g_down, g_gate))
    do = jnp.stack([mm_t(d, w_out_mine).astype(BF).reshape(seqs, slots, blk, mine) for d in dab], 0)
    g_up = across_y(g_up, 2)
    g_down = across_far(g_down)
    dqkv = attend_back(order, qkv, lse, do, cos, sin, heads)
    dqkv, g_up, g_down, activations = lax.optimization_barrier((dqkv, g_up, g_down, activations))
    count = sums[1, 0, 0]
    loss = sums[0, 0, 0] / (count * width)
    factor = (rows * world) / count
    backs = [mm_t(dqkv[s].reshape(rows, 3 * mine), w_qkv) for s in range(planes)]
    backs = [v if i == 0 else v.astype(BF) for i, v in enumerate(backs)]
    dqkv, backs, h1_all, dab_all = lax.optimization_barrier(
        (dqkv, backs, jnp.concatenate(h1, 0), jnp.concatenate(dab, 0))
    )
    g_qkv = by_columns(h1_all, dqkv.reshape(planes * rows, 3 * mine))
    g_out = by_rows(mixed.reshape(planes * rows, mine), dab_all)
    g_gate = across_far(g_gate)
    g_up = across_far(g_up)
    grad_one = reduce_group(backs)
    grad_stream = grad_residual + norm_back(grad_one, normed_one, inverse_one)
    g_qkv = across_y(g_qkv, 2)
    g_out = across_y(g_out, 0)
    low_stream, g_gate, g_up, g_qkv, g_out = lax.optimization_barrier(
        (grad_stream.astype(BF), g_gate, g_up, g_qkv, g_out)
    )
    grad_input = swap(low_stream).astype(F32) * factor

    g_qkv = across_far(g_qkv)
    g_out = across_far(g_out)
    g_down = place_rows(
        g_down, lambda block, g: ((ff // shards) * block + (ff // world) * g) // (ff // world)
    )
    ff_order = lambda v: v.reshape(planes, unit, shards, -1).transpose(1, 2, 0, 3).reshape(unit, ff)
    g_gate = place_columns(g_gate, ff_order)
    g_up = place_columns(g_up, ff_order)
    g_qkv = place_columns(g_qkv, lambda v: v.reshape(planes, unit, 3, mine).transpose(2, 1, 0, 3).reshape(3, unit, width))
    g_out = place_rows(g_out, lambda block, g: g * shards + block)
    return (
        activations.reshape(tokens.shape),
        loss,
        grad_input.reshape(tokens.shape),
        g_qkv[0] * factor,
        g_qkv[1] * factor,
        g_qkv[2] * factor,
        g_out * factor,
        g_gate * factor,
        g_up * factor,
        g_down * factor,
    )


def solution(mesh):
    tokens = P("fsdp", "ctx", None, None)
    weight = P("fsdp", None)
    grad = P(("ctx", "fsdp"), None)
    in_specs = (tokens, P(), P("fsdp", "ctx", None), tokens) + (weight,) * 7
    out_specs = (tokens, P(), tokens) + (grad,) * 7
    step = functools.partial(body, mesh.shape["ctx"], mesh.shape["fsdp"])
    return jax.shard_map(step, mesh=mesh, in_specs=in_specs, out_specs=out_specs, check_vma=False)
```

```python
import functools

import jax
import jax.numpy as jnp
from jax import lax
from jax.experimental import pallas as pl
from jax.experimental.pallas import tpu as pltpu
from jax.sharding import PartitionSpec as P

HD = 128
EPS = 1e-05
BF = jnp.bfloat16
F32 = jnp.float32
NEG = -1e30


def normalize(rows):
    centered = rows - jnp.mean(rows, -1, keepdims=True)
    inverse = lax.rsqrt(jnp.mean(centered * centered, -1, keepdims=True) + EPS)
    return centered * inverse, inverse


def norm_back(gradient, normed, inverse):
    centered = gradient - jnp.mean(gradient, -1, keepdims=True)
    return inverse * (centered - normed * jnp.mean(gradient * normed, -1, keepdims=True))


def mm(left, right):
    return jnp.dot(left, right, preferred_element_type=F32)


def mm_t(left, right):
    return lax.dot_general(left, right, (((1,), (1,)), ((), ())), preferred_element_type=F32)


def mm_rows(left, right):
    return lax.dot_general(left, right, (((0,), (0,)), ((), ())), preferred_element_type=F32)


def tables(length):
    frequency = 10000.0 ** (-2.0 * jnp.arange(HD // 2, dtype=F32) / HD)
    phases = jnp.arange(length, dtype=F32)[:, None] * frequency[None, :]
    cosine, sine = jnp.cos(phases), jnp.sin(phases)
    return jnp.concatenate([cosine, cosine], 1), jnp.concatenate([-sine, sine], 1)


def fwd_kernel(heads, order, qkv, cos, sin, out, lse, q_s, k_s, v_s):
    planes, _, slots, blk, _ = qkv.shape
    blocks = planes * slots
    scale = HD ** -0.5

    def head(h, carry):
        col = pl.multiple_of(h * HD, HD)

        def load(b, carry):
            where = order[b]
            s, t = where // slots, where % slots
            row = pl.ds(pl.multiple_of(b * blk, blk), blk)
            c, n = cos[row, :], sin[row, :]
            q = qkv[s, 0, t, :, pl.ds(col, HD)]
            k = qkv[s, 0, t, :, pl.ds(pl.multiple_of(heads * HD + col, HD), HD)]
            q_s[row, :] = ((q * c + pltpu.roll(q, HD // 2, 1) * n) * scale).astype(BF)
            k_s[row, :] = (k * c + pltpu.roll(k, HD // 2, 1) * n).astype(BF)
            v_s[row, :] = qkv[s, 0, t, :, pl.ds(pl.multiple_of(2 * heads * HD + col, HD), HD)].astype(BF)
            return carry

        lax.fori_loop(0, blocks, load, 0)
        for b in range(blocks):
            keys = (b + 1) * blk
            scores = mm_t(q_s[b * blk : keys, :], k_s[0:keys, :])
            top = jnp.max(scores, -1, keepdims=True)
            raised = jnp.exp(scores - top)
            total = jnp.sum(raised, -1, keepdims=True)
            probs = (raised * (1.0 / total)).astype(BF)
            mixed = mm(probs, v_s[0:keys, :])
            where = order[b]
            s, t = where // slots, where % slots
            out[s, 0, t, :, pl.ds(col, HD)] = mixed.astype(BF)
            lse[s, 0, t, :, pl.ds(col, HD)] = jnp.broadcast_to(top + jnp.log(total), (blk, HD))
        return carry

    lax.fori_loop(0, heads, head, 0)


def bwd_kernel(heads, order, qkv, lse, grad, cos, sin, dqkv, q_s, k_s, v_s, g_s, l_s, dk_s, dv_s):
    planes, _, slots, blk, _ = qkv.shape
    blocks = planes * slots
    scale = HD ** -0.5

    def head(h, carry):
        col = pl.multiple_of(h * HD, HD)
        kcol = pl.multiple_of(heads * HD + col, HD)
        vcol = pl.multiple_of(2 * heads * HD + col, HD)

        def load(b, carry):
            where = order[b]
            s, t = where // slots, where % slots
            row = pl.ds(pl.multiple_of(b * blk, blk), blk)
            c, n = cos[row, :], sin[row, :]
            q = qkv[s, 0, t, :, pl.ds(col, HD)]
            k = qkv[s, 0, t, :, pl.ds(kcol, HD)]
            q_s[row, :] = ((q * c + pltpu.roll(q, HD // 2, 1) * n) * scale).astype(BF)
            k_s[row, :] = (k * c + pltpu.roll(k, HD // 2, 1) * n).astype(BF)
            v_s[row, :] = qkv[s, 0, t, :, pl.ds(vcol, HD)].astype(BF)
            g_s[row, :] = grad[s, 0, t, :, pl.ds(col, HD)]
            l_s[row, :] = lse[s, 0, t, :, pl.ds(col, HD)]
            return carry

        lax.fori_loop(0, blocks, load, 0)
        dk_s[...] = jnp.zeros_like(dk_s)
        dv_s[...] = jnp.zeros_like(dv_s)
        for b in range(blocks):
            keys = (b + 1) * blk
            mine = slice(b * blk, keys)
            scores = mm_t(q_s[mine, :], k_s[0:keys, :])
            probs = jnp.exp(scores - l_s[mine, 0:1])
            dprobs = mm_t(g_s[mine, :], v_s[0:keys, :])
            delta = jnp.sum(probs * dprobs, -1, keepdims=True)
            dscores = (probs * (dprobs - delta)).astype(BF)
            dq = mm(dscores, k_s[0:keys, :]) * scale
            dk_s[0:keys, :] += mm_rows(dscores, q_s[mine, :])
            dv_s[0:keys, :] += mm_rows(probs.astype(BF), g_s[mine, :])
            where = order[b]
            s, t = where // slots, where % slots
            dq = dq * cos[mine, :] - pltpu.roll(dq, HD // 2, 1) * sin[mine, :]
            dqkv[s, 0, t, :, pl.ds(col, HD)] = dq.astype(BF)

        def store(b, carry):
            where = order[b]
            s, t = where // slots, where % slots
            row = pl.ds(pl.multiple_of(b * blk, blk), blk)
            dk = dk_s[row, :]
            dk = dk * cos[row, :] - pltpu.roll(dk, HD // 2, 1) * sin[row, :]
            dqkv[s, 0, t, :, pl.ds(kcol, HD)] = dk.astype(BF)
            dqkv[s, 0, t, :, pl.ds(vcol, HD)] = dv_s[row, :].astype(BF)
            return carry

        lax.fori_loop(0, blocks, store, 0)
        return carry

    lax.fori_loop(0, heads, head, 0)


VMEM_LIMIT = 56 * 1024 * 1024
BRIEF = pl.CostEstimate(flops=1024, bytes_accessed=1024, transcendentals=0)


def attend(order, qkv, cos, sin, heads):
    planes, seqs, slots, blk, width = qkv.shape
    length = planes * slots * blk
    spec = lambda w: pl.BlockSpec((planes, 1, slots, blk, w), lambda i, o: (0, i, 0, 0, 0))
    table = pl.BlockSpec((length, HD), lambda i, o: (0, 0))
    return pl.pallas_call(
        functools.partial(fwd_kernel, heads),
        grid_spec=pltpu.PrefetchScalarGridSpec(
            num_scalar_prefetch=1,
            grid=(seqs,),
            in_specs=[spec(width), table, table],
            out_specs=[spec(heads * HD), spec(heads * HD)],
            scratch_shapes=[pltpu.VMEM((length, HD), BF)] * 3,
        ),
        out_shape=[
            jax.ShapeDtypeStruct((planes, seqs, slots, blk, heads * HD), BF),
            jax.ShapeDtypeStruct((planes, seqs, slots, blk, heads * HD), F32),
        ],
        compiler_params=pltpu.CompilerParams(vmem_limit_bytes=VMEM_LIMIT),
        cost_estimate=BRIEF,
        name="attend",
    )(order, qkv, cos, sin)


def attend_back(order, qkv, lse, grad, cos, sin, heads):
    planes, seqs, slots, blk, width = qkv.shape
    length = planes * slots * blk
    spec = lambda w: pl.BlockSpec((planes, 1, slots, blk, w), lambda i, o: (0, i, 0, 0, 0))
    table = pl.BlockSpec((length, HD), lambda i, o: (0, 0))
    return pl.pallas_call(
        functools.partial(bwd_kernel, heads),
        grid_spec=pltpu.PrefetchScalarGridSpec(
            num_scalar_prefetch=1,
            grid=(seqs,),
            in_specs=[spec(width), spec(heads * HD), spec(heads * HD), table, table],
            out_specs=spec(width),
            scratch_shapes=[pltpu.VMEM((length, HD), BF)] * 4 + [pltpu.VMEM((length, HD), F32)] * 3,
        ),
        out_shape=jax.ShapeDtypeStruct((planes, seqs, slots, blk, width), BF),
        compiler_params=pltpu.CompilerParams(vmem_limit_bytes=VMEM_LIMIT),
        cost_estimate=BRIEF,
        name="attend_back",
    )(order, qkv, lse, grad, cos, sin)


TILE = 256


def up_kernel(count, *refs):
    hs, (wg, wu, wd) = refs[:count], refs[count : count + 3]
    refs = refs[count + 3 :]
    refs = refs[4:] if len(refs) > count + 6 else refs
    h_all, g_out, u_out, hidden_out = refs[:4]
    outs, (held, total) = refs[4 : 4 + count], refs[4 + count :]
    step = pl.program_id(0)
    rows = hs[0].shape[0]

    @pl.when(step == 0)
    def _():
        for i in range(count):
            held[i * rows : (i + 1) * rows, :] = hs[i][...]
        h_all[...] = held[...]
        total[...] = jnp.zeros_like(total)

    h = held[...]
    g, u = mm(h, wg[...]), mm(h, wu[...])
    hidden = (g * (1.0 / (1.0 + jnp.exp(-g))) * u).astype(BF)
    g_out[...], u_out[...], hidden_out[...] = g, u, hidden
    total[...] += mm(hidden, wd[...])

    @pl.when(step == pl.num_programs(0) - 1)
    def _():
        for i in range(count):
            outs[i][...] = total[i * rows : (i + 1) * rows, :].astype(outs[i].dtype)


def mlp(hs, gu_w, down_w, types, parts, which, held=None):
    rows, width = hs[0].shape
    part_ff = down_w.shape[0]
    count, tiles = len(hs), part_ff // TILE
    span = rows * count
    whole = pl.BlockSpec((rows, width), lambda i: (0, 0))
    tile = pl.BlockSpec((span, TILE), lambda i: (which, i))
    kept = [(width, BF), (part_ff, F32), (part_ff, F32), (part_ff, BF)]
    extra = [] if held is None else list(held)
    result = pl.pallas_call(
        functools.partial(up_kernel, count),
        grid=(tiles,),
        in_specs=[whole] * count
        + [
            pl.BlockSpec((width, TILE), lambda i: (0, i)),
            pl.BlockSpec((width, TILE), lambda i: (0, tiles + i)),
            pl.BlockSpec((TILE, width), lambda i: (i, 0)),
        ]
        + [pl.BlockSpec(memory_space=pl.ANY)] * len(extra),
        out_specs=[pl.BlockSpec((span, width), lambda i: (which, 0)), tile, tile, tile] + [whole] * count,
        out_shape=[jax.ShapeDtypeStruct((span * parts, w), t) for w, t in kept]
        + [jax.ShapeDtypeStruct((rows, width), t) for t in types],
        scratch_shapes=[pltpu.VMEM((span, width), BF), pltpu.VMEM((span, width), F32)],
        input_output_aliases={count + 3 + i: i for i in range(len(extra))},
        compiler_params=pltpu.CompilerParams(vmem_limit_bytes=48 * 1024 * 1024),
        cost_estimate=BRIEF,
        name="mlp",
    )(*hs, gu_w, gu_w, down_w, *extra)
    return result[:4], result[4:]


def down_kernel(count, *refs):
    ds, (g_in, u_in, wg, wu, wd) = refs[:count], refs[count : count + 5]
    refs = refs[count + 5 :]
    refs = refs[3:] if len(refs) > count + 5 else refs
    d_all, dg_out, du_out = refs[:3]
    outs, (held, total) = refs[3 : 3 + count], refs[3 + count :]
    step = pl.program_id(0)
    rows = ds[0].shape[0]

    @pl.when(step == 0)
    def _():
        for i in range(count):
            held[i * rows : (i + 1) * rows, :] = ds[i][...]
        d_all[...] = held[...]
        total[...] = jnp.zeros_like(total)

    dh = mm_t(held[...], wd[...])
    g = g_in[...]
    sig = 1.0 / (1.0 + jnp.exp(-g))
    dg = (dh * u_in[...] * sig * (1.0 + g * (1.0 - sig))).astype(BF)
    du = (dh * (g * sig)).astype(BF)
    dg_out[...], du_out[...] = dg, du
    total[...] += mm_t(dg, wg[...]) + mm_t(du, wu[...])

    @pl.when(step == pl.num_programs(0) - 1)
    def _():
        for i in range(count):
            outs[i][...] = total[i * rows : (i + 1) * rows, :].astype(outs[i].dtype)


def mlp_back(ds, g, u, gu_w, down_w, types, parts, which, held=None):
    rows, width = ds[0].shape
    part_ff = down_w.shape[0]
    count, tiles = len(ds), part_ff // TILE
    span = rows * count
    whole = pl.BlockSpec((rows, width), lambda i: (0, 0))
    tile = pl.BlockSpec((span, TILE), lambda i: (which, i))
    kept = [(width, BF), (part_ff, BF), (part_ff, BF)]
    extra = [] if held is None else list(held)
    result = pl.pallas_call(
        functools.partial(down_kernel, count),
        grid=(tiles,),
        in_specs=[whole] * count
        + [
            tile,
            tile,
            pl.BlockSpec((width, TILE), lambda i: (0, i)),
            pl.BlockSpec((width, TILE), lambda i: (0, tiles + i)),
            pl.BlockSpec((TILE, width), lambda i: (i, 0)),
        ]
        + [pl.BlockSpec(memory_space=pl.ANY)] * len(extra),
        out_specs=[pl.BlockSpec((span, width), lambda i: (which, 0)), tile, tile] + [whole] * count,
        out_shape=[jax.ShapeDtypeStruct((span * parts, w), t) for w, t in kept]
        + [jax.ShapeDtypeStruct((rows, width), t) for t in types],
        scratch_shapes=[pltpu.VMEM((span, width), BF), pltpu.VMEM((span, width), F32)],
        input_output_aliases={count + 5 + i: i for i in range(len(extra))},
        compiler_params=pltpu.CompilerParams(vmem_limit_bytes=48 * 1024 * 1024),
        cost_estimate=BRIEF,
        name="mlp_back",
    )(*ds, g, u, gu_w, gu_w, down_w, *extra)
    return result[:3], result[3:]


def outer(lefts, rights, which, by_rows, away=None, runs=1):
    count = max(len(lefts), len(rights))
    depth = sum(v.shape[0] for v in lefts)
    chunk = depth // count
    out_rows, out_cols = lefts[0].shape[1], rights[0].shape[1]
    out_rows, out_cols = (out_rows // 2, out_cols) if by_rows else (out_rows, out_cols // 2)
    tile = min(TILE, out_rows // runs)
    tiles = out_rows // tile
    run = tiles // runs

    def kernel(which, *refs):
        left, right = refs[: len(lefts)], refs[len(lefts) : len(lefts) + len(rights)]
        take = lambda group, i: group[i][...] if len(group) > 1 else group[0][i * chunk : (i + 1) * chunk, :]
        total = mm_rows(take(left, 0), take(right, 0))
        for i in range(1, count):
            total = total + mm_rows(take(left, i), take(right, i))
        if away is not None:
            total = total + refs[-2][...].astype(F32)
        refs[-1][...] = total.astype(BF)

    out_spec = pl.BlockSpec((tile, out_cols), lambda i, w: (i, 0))
    return pl.pallas_call(
        kernel,
        grid_spec=pltpu.PrefetchScalarGridSpec(
            num_scalar_prefetch=1,
            grid=(tiles,),
            in_specs=[
                pl.BlockSpec((v.shape[0], tile), lambda i, w: (0, (i // run + w[0]) * run + i if by_rows else i)) for v in lefts
            ]
            + [pl.BlockSpec((v.shape[0], out_cols), lambda i, w: (0, 0 if by_rows else w[0])) for v in rights]
            + ([] if away is None else [out_spec]),
            out_specs=out_spec,
        ),
        out_shape=jax.ShapeDtypeStruct((out_rows, out_cols), BF),
        compiler_params=pltpu.CompilerParams(vmem_limit_bytes=48 * 1024 * 1024),
        cost_estimate=BRIEF,
        name="outer",
    )(which.reshape(1).astype(jnp.int32), *lefts, *rights, *([] if away is None else [away]))


def project(lefts, weight, transposed, types):
    rows, depth = lefts[0].shape
    width = weight.shape[0] if transposed else weight.shape[1]
    tile = min(512, width)
    count = len(lefts)

    def kernel(*refs):
        left, (w,), outs = refs[:count], refs[count : count + 1], refs[count + 1 :]
        for i in range(count):
            result = (mm_t if transposed else mm)(left[i][...], w[...])
            if len(outs) > 1:
                outs[i][...] = result.astype(outs[i].dtype)
            else:
                outs[0][i * rows : (i + 1) * rows, :] = result.astype(outs[0].dtype)

    height = rows * count // len(types)
    return pl.pallas_call(
        kernel,
        grid=(width // tile,),
        in_specs=[pl.BlockSpec((rows, depth), lambda i: (0, 0))] * count
        + [
            pl.BlockSpec((tile, depth), lambda i: (i, 0))
            if transposed
            else pl.BlockSpec((depth, tile), lambda i: (0, i))
        ],
        out_specs=[pl.BlockSpec((height, tile), lambda i: (0, i))] * len(types),
        out_shape=[jax.ShapeDtypeStruct((height, width), t) for t in types],
        compiler_params=pltpu.CompilerParams(vmem_limit_bytes=48 * 1024 * 1024),
        cost_estimate=BRIEF,
        name="project",
    )(*lefts, weight)


def assemble(places, arrays, depth):
    width = arrays[0].shape[1]
    pieces = [(n, start) for n, v in enumerate(arrays) for start in range(0, v.shape[0], depth)]
    count = len(pieces)

    def kernel(places, *refs):
        sources, out, held, arrive, leave = refs[: len(arrays)], *refs[len(arrays) :]
        ins = [
            pltpu.make_async_copy(sources[n].at[pl.ds(start, depth), :], held.at[i], arrive.at[i])
            for i, (n, start) in enumerate(pieces)
        ]
        outs = [pltpu.make_async_copy(held.at[i], out.at[places[i]], leave.at[i]) for i in range(count)]
        for copy in ins:
            copy.start()
        for i in range(count):
            ins[i].wait()
            outs[i].start()
        for copy in outs:
            copy.wait()

    return pl.pallas_call(
        kernel,
        grid_spec=pltpu.PrefetchScalarGridSpec(
            num_scalar_prefetch=1,
            grid=(1,),
            in_specs=[pl.BlockSpec(memory_space=pl.ANY)] * len(arrays),
            out_specs=pl.BlockSpec(memory_space=pl.ANY),
            scratch_shapes=[
                pltpu.VMEM((count, depth, width), arrays[0].dtype),
                pltpu.SemaphoreType.DMA((count,)),
                pltpu.SemaphoreType.DMA((count,)),
            ],
        ),
        out_shape=jax.ShapeDtypeStruct((count, depth, width), arrays[0].dtype),
        compiler_params=pltpu.CompilerParams(vmem_limit_bytes=VMEM_LIMIT),
        cost_estimate=BRIEF,
        name="assemble",
    )(places, *arrays).reshape(count * depth, width)


def take_columns(which, arrays, groups, members):
    depth, width = arrays[0].shape
    part = width // (groups * members)
    kept = len(which)
    if part % HD:
        views = [v.reshape(depth, groups, members, part) for v in arrays]
        return [
            jnp.concatenate(
                [lax.dynamic_slice_in_dim(v, k, 1, 2).reshape(depth, groups * part) for v in views], 1
            )
            for k in which
        ]

    def kernel(which, *refs):
        sources, outs = refs[: len(arrays)], refs[len(arrays) :]
        for k in range(kept):
            for n, source in enumerate(sources):
                for i in range(groups):
                    start = pl.multiple_of(i * members * part + which[k] * part, HD)
                    outs[k][:, (n * groups + i) * part : (n * groups + i + 1) * part] = source[:, pl.ds(start, part)]

    tile = min(64, depth)
    return pl.pallas_call(
        kernel,
        grid_spec=pltpu.PrefetchScalarGridSpec(
            num_scalar_prefetch=1,
            grid=(depth // tile,),
            in_specs=[pl.BlockSpec((tile, width), lambda i, w: (i, 0))] * len(arrays),
            out_specs=[pl.BlockSpec((tile, len(arrays) * groups * part), lambda i, w: (i, 0))] * kept,
        ),
        out_shape=[jax.ShapeDtypeStruct((depth, len(arrays) * groups * part), arrays[0].dtype)] * kept,
        name="take_columns",
    )(jnp.stack(which).astype(jnp.int32), *arrays)


def body(planes, shards, tokens, pairs, valid, teacher, w_query, w_key, w_value, w_out, w_gate, w_up, w_down):
    seqs, slots, blk, width = tokens.shape
    ff = w_gate.shape[1]
    rows = seqs * slots * blk
    world = planes * shards
    near = planes // 2
    all_heads = width // HD
    heads = all_heads // planes
    mine = heads * HD
    own_rows = width // shards
    part_ff = ff // planes
    length = planes * slots * blk
    unit = width // world
    both = ("ctx", "fsdp")

    c, f = lax.axis_index("ctx"), lax.axis_index("fsdp")
    far, low = c // near, c % near
    core, x, y = f % 2, f // 2 % 2, f // 4
    group = x * near + low

    def after(array, *others):
        return lax.optimization_barrier((array, *others))[0]

    def flip(array, bits):
        return lax.ppermute(array, "fsdp", [(i, i ^ bits) for i in range(shards)])

    def flip_ctx(array, bits):
        return lax.ppermute(array, "ctx", [(i, i ^ bits) for i in range(planes)])

    def hop(array, j):
        dx, dz = j // near, j % near
        if dz == 0:
            return flip(array, 2 * dx)
        if dx == 0:
            return flip_ctx(array, dz)
        return lax.ppermute(
            array,
            both,
            [(p * shards + s, (p ^ dz) * shards + (s ^ 2)) for p in range(planes) for s in range(shards)],
        )

    def send(array, homes):
        moved = lax.ppermute(array, both, [(i, to) for i, to in enumerate(homes) if i != to])
        stays = jnp.array([i == to for i, to in enumerate(homes)])[c * shards + f]
        return jnp.where(stays, array, moved)

    def swap(array):
        homes = []
        for p in range(planes):
            for s in range(shards):
                to = (s // 2 % 2) * near + p % near
                homes.append(to * shards + (s - s // 2 % 2 * 2 + p // near * 2))
        return send(array, homes)

    cos, sin = tables(length)
    ranks = jnp.argsort(pairs.reshape(-1))
    owner = ranks // slots
    relative = ((owner // near) ^ x) * near + ((owner % near) ^ low)
    order = (relative * slots + ranks % slots).astype(jnp.int32)

    def over_y(piece):
        return [flip(piece, bits) for bits in range(4, shards, 4)]

    y_bits = list(range(4, shards, 4))

    def put(*items):
        keys = [k for _, own_keys in items for k in own_keys]
        depth = items[0][0].shape[0] // len(items[0][1])
        places = jnp.stack([f ^ k for k in keys]).astype(jnp.int32)
        return assemble(places, [v for v, _ in items], depth)

    def put_pairs(both_x, both_y, other_x, other_y):
        items = [(both_x, [0, 2]), (other_x, [1, 3])]
        for bits, v, w in zip(y_bits, both_y, other_y):
            items += [(v, [bits, bits + 2]), (w, [bits + 1, bits + 3])]
        return put(*items)

    def head_columns(g):
        return jnp.concatenate(
            [lax.dynamic_slice_in_dim(w, g * mine, mine, 1) for w in (w_query, w_key, w_value)], 1
        )

    def ff_rows(g):
        return lax.dynamic_slice_in_dim(w_down, g * (part_ff // shards), part_ff // shards, 0)

    def own_heads(weight):
        sends, spreads = [], {}
        for p in range(planes):
            for s in range(shards):
                q = s // 2
                if q % near == p % near:
                    at = s // 4 * 4 + q // near * 2 + s % 2
                    if at != s:
                        sends.append((p * shards + s, p * shards + at))
                    for d in range(4, shards, 4):
                        spreads.setdefault(d, []).append((p * shards + at, p * shards + (at ^ d)))
        q = f // 2
        stays = (q % near == low) & (f // 4 * 4 + q // near * 2 + core == f)
        first = jnp.where(stays, weight, lax.ppermute(weight, both, sends))

        def rest(first):
            found = first
            for pairs_of in spreads.values():
                found = found + lax.ppermute(first, both, pairs_of)
            return found

        return first, rest

    def gather_group(own):
        return [own] + [hop(own, j) for j in range(1, planes)]

    cut = planes // 2
    early = list(range(1, cut + 1))
    late = [0, *range(cut + 1, planes)]
    early_types = [BF] * cut
    late_types = [F32] + [BF] * (planes - cut - 1)

    def add_all(total, others):
        for other in others:
            total = total + other.astype(F32)
        return total

    region = lambda *values: lax.optimization_barrier(values)

    gu_own, gu_send = take_columns([group, group ^ near], [w_gate, w_up], shards, planes)
    stream_low = swap(tokens.reshape(rows, width))
    qkv_own = head_columns(group)
    qkv_other = flip(head_columns(group ^ near), 2)
    gu_own_y = over_y(gu_own)
    heads_first, heads_rest = own_heads(w_out)
    stream_low, qkv_own, qkv_other, gu_own, gu_own_y, gu_send, heads_first, w_down = region(
        stream_low, qkv_own, qkv_other, gu_own, gu_own_y, gu_send, heads_first, w_down
    )
    stream = stream_low.astype(F32)
    normed_one, inverse_one = normalize(stream)
    qkv_both = jnp.concatenate([qkv_own, qkv_other], 0)
    h1, qkv_both = region([normed_one.astype(BF)], qkv_both)

    h1 = h1 + [hop(h1[0], j) for j in early]
    qkv_y = over_y(qkv_both)
    qkv_pair = flip(qkv_both, 1)
    h1, qkv_both, qkv_y, qkv_pair, heads_first, w_down, gu_send = region(
        h1, qkv_both, qkv_y, qkv_pair, heads_first, w_down, gu_send
    )

    h1 = h1 + [hop(h1[0], j) for j in late[1:]]
    found = heads_rest(heads_first)
    down_own = ff_rows(group)
    down_other = flip(ff_rows(group ^ near), 2)
    qkv_y_pair = [flip(v, 1) for v in qkv_y]
    h1, found, down_own, down_other, qkv_y_pair, gu_send, gu_own_y, teacher = region(
        h1, found, down_own, down_other, qkv_y_pair, gu_send, gu_own_y, teacher
    )

    gu_other = flip(gu_send, 2)
    down_both = jnp.concatenate([down_own, down_other], 0)
    down_y = over_y(down_both)
    other = flip(found, 1)
    w_qkv = put_pairs(qkv_both, qkv_y, qkv_pair, qkv_y_pair)
    goal_low = swap(teacher.reshape(rows, width))
    (qkv,) = project(h1, w_qkv, False, [F32])
    qkv = qkv.reshape(planes, seqs, slots, blk, 3 * mine)
    mixed, lse = attend(order, qkv, cos, sin, heads)
    even = core == 0
    w_out_mine = jnp.concatenate([jnp.where(even, found, other), jnp.where(even, other, found)], 0)
    group_types = [F32] + [BF] * (planes - 1)
    products = project([mixed[s].reshape(rows, mine) for s in range(planes)], w_out_mine, False, group_types)
    products, gu_other, down_both, down_y, gu_own, gu_own_y, goal_low = region(
        products, gu_other, down_both, down_y, gu_own, gu_own_y, goal_low
    )

    received = [hop(products[j], j) for j in early]
    gu_other_y = over_y(gu_other)
    down_pair = flip(down_both, 1)
    gu_own_pair = flip(gu_own, 1)
    received, products, down_pair, gu_other, down_y, gu_own_pair, gu_own_y = region(
        received, products, down_pair, gu_other, down_y, gu_own_pair, gu_own_y
    )

    received = received + [hop(products[j], j) for j in late[1:]]
    down_y_pair = [flip(v, 1) for v in down_y]
    gu_own_y_pair = [flip(v, 1) for v in gu_own_y]
    gu_other_pair = flip(gu_other, 1)
    received, gu_other_y, down_y_pair, gu_own_y_pair, gu_other_pair, valid = region(
        received, gu_other_y, down_y_pair, gu_own_y_pair, gu_other_pair, valid
    )
    residual = stream + add_all(products[0], received)
    normed_two, inverse_two = normalize(residual)
    h2, gu_other_y = region([normed_two.astype(BF)], gu_other_y)

    h2 = h2 + [hop(h2[0], j) for j in early]
    gu_items = [(gu_own, [0]), (gu_own_pair, [1]), (gu_other, [2]), (gu_other_pair, [3])]
    for bits, v, w, z in zip(y_bits, gu_own_y, gu_own_y_pair, gu_other_y):
        gu_items += [(v, [bits]), (w, [bits + 1]), (z, [bits + 2]), (flip(z, 1), [bits + 3])]
    down_w = put_pairs(down_both, down_y, down_pair, down_y_pair)
    gu_w = put(*gu_items)
    h2, gu_w, down_w, valid = region(h2, gu_w, down_w, valid)

    h2 = h2 + [hop(h2[0], j) for j in late[1:]]
    kept, outs = mlp([h2[j] for j in early], gu_w, down_w, early_types, 2, 0)
    outs, kept, far_tokens = region(outs, kept, h2[cut + 1 :])
    h2 = h2[: cut + 1] + far_tokens

    received = [hop(v, j) for v, j in zip(outs, early)]
    (h2_all, gates, ups, hidden_all), outs = mlp(
        [h2[j] for j in late], gu_w, down_w, late_types, 2, 1, kept
    )
    received, outs, h2_all, gates, ups, hidden_all, valid = region(
        received, outs, h2_all, gates, ups, hidden_all, valid
    )

    received = received + [hop(v, j) for v, j in zip(outs[1:], late[1:])]
    valid_float = swap(valid.reshape(rows, 1)).astype(F32)
    received, own, valid_float = region(received, outs[0], valid_float)

    output = residual + add_all(own, received)
    deviation = output - goal_low.astype(F32)
    grad_output = valid_float * deviation
    sums = jnp.stack([jnp.sum(grad_output * deviation), jnp.sum(valid_float)])
    sums0 = jnp.broadcast_to(sums[:, None, None], (2, 8, HD))
    sums = sums0
    for j in range(1, planes):
        sums = sums + hop(sums0, j)
    sums = sums + flip_ctx(sums, near)
    low_grad, low_output, sums = region(grad_output.astype(BF), output.astype(BF), sums)

    steps = [1 << b for b in reversed(range(2, shards.bit_length() - 1))]

    def halve(part, axis, bit, move, bits):
        half = part.shape[axis] // 2
        take = lambda k: lax.dynamic_slice_in_dim(part, k * half, half, axis)
        away = move(take(1 - bit), bits)
        return (take(bit).astype(F32) + away.astype(F32)).astype(BF)

    def parts(whole):
        return whole.reshape(2, near, shards // 4, 2, 2, unit, whole.shape[1])

    def across_y(part, axis):
        for step in steps:
            part = halve(part, axis, f // step % 2, flip, step)
        return part

    def across_far(part):
        return halve(part, 0, far, flip_ctx, near)

    def place_rows(part, place):
        homes = []
        for p in range(planes):
            for s in range(shards):
                homes.append(place(s % 2, s // 4, p // near, (s // 2 % 2) * near + p % near))
        return send(part, homes).astype(F32)

    def take(v, k, axis):
        return lax.dynamic_index_in_dim(v, k, axis, keepdims=False)

    def core_away(part):
        return flip(take(part.reshape(near, 2, 2, unit, part.shape[-1]), 1 - core, 2), 1)

    def core_joined(part, away):
        keep = take(part.reshape(near, 2, 2, unit, part.shape[-1]), core, 2)
        even = core == 0
        return jnp.concatenate([jnp.where(even, keep, away), jnp.where(even, away, keep)], -1)

    def column_pieces(part):
        return [take(take(part, x ^ (j // near), 1), low ^ (j % near), 0) for j in range(planes)]

    def columns_placed(pieces):
        places = jnp.stack([group ^ j for j in range(planes)]).astype(jnp.int32)
        return assemble(places, pieces, unit).reshape(planes, unit, -1)

    dm = [low_grad] + [hop(low_grad, j) for j in early]
    for bits in [1, *(1 << b for b in range(2, shards.bit_length() - 1))]:
        sums = sums + flip(sums, bits)
    dm, sums, low_output = region(dm, sums, low_output)

    dm = dm + [hop(dm[0], j) for j in late[1:]]
    kept, backs = mlp_back([dm[j] for j in early], gates, ups, gu_w, down_w, early_types, 2, 0)
    backs, kept, far_tokens, sums = region(backs, kept, dm[cut + 1 :], sums)
    dm = dm[: cut + 1] + far_tokens

    received = [hop(v, j) for v, j in zip(backs, early)]
    dm_runs = [dm[j] for j in early + late]
    away = flip(outer([hidden_all], dm_runs, 1 - core, True, None, 2), 1)
    (_, dg_all, du_all), backs = mlp_back(
        [dm[j] for j in late], gates, ups, gu_w, down_w, late_types, 2, 1, kept
    )
    g_down = outer([hidden_all], dm_runs, core, True, away, 2)
    received, backs, g_down, dg_all, du_all, h2_all = region(received, backs, g_down, dg_all, du_all, h2_all)

    received = received + [hop(v, j) for v, j in zip(backs[1:], late[1:])]
    g_down = across_y(g_down.reshape(2, shards // 4, part_ff // shards, width), 1)
    gate_half = outer([h2_all], [dg_all], 1 - core, False)
    up_half = outer([h2_all], [du_all], 1 - core, False)
    received, gate_half, up_half, dg_all, du_all, g_down = region(received, gate_half, up_half, dg_all, du_all, g_down)
    grad_two = add_all(backs[0], received)
    grad_residual = grad_output + norm_back(grad_two, normed_two, inverse_two)
    dab, gate_half, up_half, g_down = region([grad_residual.astype(BF)], gate_half, up_half, g_down)

    dab = dab + [hop(dab[0], j) for j in early]
    gate_away, up_away = flip(gate_half, 1), flip(up_half, 1)
    g_down = across_far(g_down)
    dab, gate_away, up_away, dg_all, du_all, low_output = region(dab, gate_away, up_away, dg_all, du_all, low_output)

    dab = dab + [hop(dab[0], j) for j in late[1:]]
    g_gate = parts(outer([h2_all], [dg_all], core, False, gate_away))
    g_up = parts(outer([h2_all], [du_all], core, False, up_away))
    dab, g_gate, g_up, g_down, low_output = region(dab, g_gate, g_up, g_down, low_output)

    activations = swap(low_output)
    g_gate = across_y(g_gate, 2)
    g_up = across_y(g_up, 2)
    (do,) = project(dab, w_out_mine, True, [BF])
    dqkv = attend_back(order, qkv, lse, do.reshape(planes, seqs, slots, blk, mine), cos, sin, heads)
    dqkv = dqkv.reshape(planes * rows, 3 * mine)
    qkv_half = outer(h1, [dqkv], 1 - core, False)
    dqkv, qkv_half, g_gate, activations = region(dqkv, qkv_half, g_gate, activations)

    qkv_away = flip(qkv_half, 1)
    g_gate = across_far(g_gate)
    backs = project([dqkv[i * rows : (i + 1) * rows] for i in range(planes)], w_qkv, True, group_types)
    backs, dqkv, qkv_away, g_down = region(backs, dqkv, qkv_away, g_down)

    received = [hop(backs[j], j) for j in early]
    g_qkv = parts(outer(h1, [dqkv], core, False, qkv_away))
    mixed = mixed.reshape(planes * rows, mine)
    out_half = outer([mixed], dab, 1 - core, True)
    g_down = place_rows(
        g_down.reshape(ff // world, width),
        lambda core, y, far, g: far * (shards // 2) * planes + (core * (shards // 4) + y) * planes + g,
    )
    received, backs, g_qkv, out_half, g_up, g_gate = region(received, backs, g_qkv, out_half, g_up, g_gate)

    received = received + [hop(backs[j], j) for j in late[1:]]
    g_qkv = across_y(g_qkv, 2)
    g_up = across_far(g_up)
    out_away = flip(out_half, 1)
    gate_core = core_away(g_gate)
    received, g_qkv, out_away, gate_core, g_down, g_up = region(received, g_qkv, out_away, gate_core, g_down, g_up)
    grad_one = add_all(backs[0], received)
    grad_stream = grad_residual + norm_back(grad_one, normed_one, inverse_one)
    g_out = outer([mixed], dab, core, True, out_away)
    gate_pieces = column_pieces(core_joined(g_gate, gate_core))
    low_stream, g_out, g_qkv, gate_pieces, g_up = region(grad_stream.astype(BF), g_out, g_qkv, gate_pieces, g_up)

    grad_low = swap(low_stream)
    g_qkv = across_far(g_qkv)
    g_out = across_y(g_out, 0)
    gate_pieces = gate_pieces[:1] + [hop(gate_pieces[j], j) for j in early] + gate_pieces[cut + 1 :]
    grad_low, g_out, g_up, g_qkv, gate_pieces = region(grad_low, g_out, g_up, g_qkv, gate_pieces)

    count = sums[1, 0, 0]
    loss = sums[0, 0, 0] / (count * width)
    factor = (rows * world) / count
    grad_input = grad_low.astype(F32) * factor
    ff_order = lambda v: v.reshape(planes, unit, shards, -1).transpose(1, 2, 0, 3).reshape(unit, ff)
    gate_pieces = gate_pieces[: cut + 1] + [hop(gate_pieces[j], j) for j in late[1:]]
    up_core = core_away(g_up)
    qkv_core = core_away(g_qkv)
    g_out = across_far(g_out)
    gate_pieces, up_core, qkv_core, g_out, g_qkv, g_up = region(gate_pieces, up_core, qkv_core, g_out, g_qkv, g_up)
    up_pieces = [hop(v, j) if j else v for j, v in enumerate(column_pieces(core_joined(g_up, up_core)))]
    g_gate = ff_order(columns_placed(gate_pieces)).astype(F32)
    up_pieces, g_qkv, qkv_core, g_out = region(up_pieces, g_qkv, qkv_core, g_out)
    qkv_pieces = [hop(v, j) if j else v for j, v in enumerate(column_pieces(core_joined(g_qkv, qkv_core)))]
    g_out = place_rows(g_out, lambda core, y, far, g: g * shards + (core * (shards // 4) + y) * 2 + far)
    g_up = ff_order(columns_placed(up_pieces)).astype(F32)
    g_qkv = columns_placed(qkv_pieces).reshape(planes, unit, 3, mine).transpose(2, 1, 0, 3).reshape(3, unit, width)
    g_qkv = g_qkv.astype(F32)
    return (
        activations.reshape(tokens.shape),
        loss,
        grad_input.reshape(tokens.shape),
        g_qkv[0] * factor,
        g_qkv[1] * factor,
        g_qkv[2] * factor,
        g_out * factor,
        g_gate * factor,
        g_up * factor,
        g_down * factor,
    )


def solution(mesh):
    tokens = P("fsdp", "ctx", None, None)
    weight = P("fsdp", None)
    grad = P(("ctx", "fsdp"), None)
    in_specs = (tokens, P(), P("fsdp", "ctx", None), tokens) + (weight,) * 7
    out_specs = (tokens, P(), tokens) + (grad,) * 7
    step = functools.partial(body, mesh.shape["ctx"], mesh.shape["fsdp"])
    return jax.shard_map(step, mesh=mesh, in_specs=in_specs, out_specs=out_specs, check_vma=False)
```

```python
import functools

import jax
import jax.numpy as jnp
from jax import lax
from jax.experimental import pallas as pl
from jax.experimental.pallas import tpu as pltpu
from jax.sharding import PartitionSpec as P

HD = 128
EPS = 1e-05
BF = jnp.bfloat16
F32 = jnp.float32
NEG = -1e30


def normalize(rows):
    centered = rows - jnp.mean(rows, -1, keepdims=True)
    inverse = lax.rsqrt(jnp.mean(centered * centered, -1, keepdims=True) + EPS)
    return centered * inverse, inverse


def norm_back(gradient, normed, inverse):
    centered = gradient - jnp.mean(gradient, -1, keepdims=True)
    return inverse * (centered - normed * jnp.mean(gradient * normed, -1, keepdims=True))


def mm(left, right):
    return jnp.dot(left, right, preferred_element_type=F32)


def mm_t(left, right):
    return lax.dot_general(left, right, (((1,), (1,)), ((), ())), preferred_element_type=F32)


def mm_rows(left, right):
    return lax.dot_general(left, right, (((0,), (0,)), ((), ())), preferred_element_type=F32)


def tables(length):
    frequency = 10000.0 ** (-2.0 * jnp.arange(HD // 2, dtype=F32) / HD)
    phases = jnp.arange(length, dtype=F32)[:, None] * frequency[None, :]
    cosine, sine = jnp.cos(phases), jnp.sin(phases)
    return jnp.concatenate([cosine, cosine], 1), jnp.concatenate([-sine, sine], 1)


def fwd_kernel(heads, order, qkv, cos, sin, out, lse, q_s, k_s, v_s):
    planes, _, slots, blk, _ = qkv.shape
    blocks = planes * slots
    scale = HD ** -0.5

    def head(h, carry):
        col = pl.multiple_of(h * HD, HD)

        def load(b, carry):
            where = order[b]
            s, t = where // slots, where % slots
            row = pl.ds(pl.multiple_of(b * blk, blk), blk)
            c, n = cos[row, :], sin[row, :]
            q = qkv[s, 0, t, :, pl.ds(col, HD)]
            k = qkv[s, 0, t, :, pl.ds(pl.multiple_of(heads * HD + col, HD), HD)]
            q_s[row, :] = ((q * c + pltpu.roll(q, HD // 2, 1) * n) * scale).astype(BF)
            k_s[row, :] = (k * c + pltpu.roll(k, HD // 2, 1) * n).astype(BF)
            v_s[row, :] = qkv[s, 0, t, :, pl.ds(pl.multiple_of(2 * heads * HD + col, HD), HD)].astype(BF)
            return carry

        lax.fori_loop(0, blocks, load, 0)
        for b in range(blocks):
            keys = (b + 1) * blk
            scores = mm_t(q_s[b * blk : keys, :], k_s[0:keys, :])
            top = jnp.max(scores, -1, keepdims=True)
            raised = jnp.exp(scores - top)
            total = jnp.sum(raised, -1, keepdims=True)
            probs = (raised * (1.0 / total)).astype(BF)
            mixed = mm(probs, v_s[0:keys, :])
            where = order[b]
            s, t = where // slots, where % slots
            out[s, 0, t, :, pl.ds(col, HD)] = mixed.astype(BF)
            lse[s, 0, t, :, pl.ds(col, HD)] = jnp.broadcast_to(top + jnp.log(total), (blk, HD))
        return carry

    lax.fori_loop(0, heads, head, 0)


def bwd_kernel(heads, order, qkv, lse, grad, cos, sin, dqkv, q_s, k_s, v_s, g_s, l_s, dk_s, dv_s):
    planes, _, slots, blk, _ = qkv.shape
    blocks = planes * slots
    scale = HD ** -0.5

    def head(h, carry):
        col = pl.multiple_of(h * HD, HD)
        kcol = pl.multiple_of(heads * HD + col, HD)
        vcol = pl.multiple_of(2 * heads * HD + col, HD)

        def load(b, carry):
            where = order[b]
            s, t = where // slots, where % slots
            row = pl.ds(pl.multiple_of(b * blk, blk), blk)
            c, n = cos[row, :], sin[row, :]
            q = qkv[s, 0, t, :, pl.ds(col, HD)]
            k = qkv[s, 0, t, :, pl.ds(kcol, HD)]
            q_s[row, :] = ((q * c + pltpu.roll(q, HD // 2, 1) * n) * scale).astype(BF)
            k_s[row, :] = (k * c + pltpu.roll(k, HD // 2, 1) * n).astype(BF)
            v_s[row, :] = qkv[s, 0, t, :, pl.ds(vcol, HD)].astype(BF)
            g_s[row, :] = grad[s, 0, t, :, pl.ds(col, HD)]
            l_s[row, :] = lse[s, 0, t, :, pl.ds(col, HD)]
            return carry

        lax.fori_loop(0, blocks, load, 0)
        dk_s[...] = jnp.zeros_like(dk_s)
        dv_s[...] = jnp.zeros_like(dv_s)
        for b in range(blocks):
            keys = (b + 1) * blk
            mine = slice(b * blk, keys)
            scores = mm_t(q_s[mine, :], k_s[0:keys, :])
            probs = jnp.exp(scores - l_s[mine, 0:1])
            dprobs = mm_t(g_s[mine, :], v_s[0:keys, :])
            delta = jnp.sum(probs * dprobs, -1, keepdims=True)
            dscores = (probs * (dprobs - delta)).astype(BF)
            dq = mm(dscores, k_s[0:keys, :]) * scale
            dk_s[0:keys, :] += mm_rows(dscores, q_s[mine, :])
            dv_s[0:keys, :] += mm_rows(probs.astype(BF), g_s[mine, :])
            where = order[b]
            s, t = where // slots, where % slots
            dq = dq * cos[mine, :] - pltpu.roll(dq, HD // 2, 1) * sin[mine, :]
            dqkv[s, 0, t, :, pl.ds(col, HD)] = dq.astype(BF)

        def store(b, carry):
            where = order[b]
            s, t = where // slots, where % slots
            row = pl.ds(pl.multiple_of(b * blk, blk), blk)
            dk = dk_s[row, :]
            dk = dk * cos[row, :] - pltpu.roll(dk, HD // 2, 1) * sin[row, :]
            dqkv[s, 0, t, :, pl.ds(kcol, HD)] = dk.astype(BF)
            dqkv[s, 0, t, :, pl.ds(vcol, HD)] = dv_s[row, :].astype(BF)
            return carry

        lax.fori_loop(0, blocks, store, 0)
        return carry

    lax.fori_loop(0, heads, head, 0)


VMEM_LIMIT = 56 * 1024 * 1024
BRIEF = pl.CostEstimate(flops=1024, bytes_accessed=1024, transcendentals=0)


def attend(order, qkv, cos, sin, heads):
    planes, seqs, slots, blk, width = qkv.shape
    length = planes * slots * blk
    spec = lambda w: pl.BlockSpec((planes, 1, slots, blk, w), lambda i, o: (0, i, 0, 0, 0))
    table = pl.BlockSpec((length, HD), lambda i, o: (0, 0))
    return pl.pallas_call(
        functools.partial(fwd_kernel, heads),
        grid_spec=pltpu.PrefetchScalarGridSpec(
            num_scalar_prefetch=1,
            grid=(seqs,),
            in_specs=[spec(width), table, table],
            out_specs=[spec(heads * HD), spec(heads * HD)],
            scratch_shapes=[pltpu.VMEM((length, HD), BF)] * 3,
        ),
        out_shape=[
            jax.ShapeDtypeStruct((planes, seqs, slots, blk, heads * HD), BF),
            jax.ShapeDtypeStruct((planes, seqs, slots, blk, heads * HD), F32),
        ],
        compiler_params=pltpu.CompilerParams(vmem_limit_bytes=VMEM_LIMIT),
        cost_estimate=BRIEF,
        name="attend",
    )(order, qkv, cos, sin)


def attend_back(order, qkv, lse, grad, cos, sin, heads):
    planes, seqs, slots, blk, width = qkv.shape
    length = planes * slots * blk
    spec = lambda w: pl.BlockSpec((planes, 1, slots, blk, w), lambda i, o: (0, i, 0, 0, 0))
    table = pl.BlockSpec((length, HD), lambda i, o: (0, 0))
    return pl.pallas_call(
        functools.partial(bwd_kernel, heads),
        grid_spec=pltpu.PrefetchScalarGridSpec(
            num_scalar_prefetch=1,
            grid=(seqs,),
            in_specs=[spec(width), spec(heads * HD), spec(heads * HD), table, table],
            out_specs=spec(width),
            scratch_shapes=[pltpu.VMEM((length, HD), BF)] * 4 + [pltpu.VMEM((length, HD), F32)] * 3,
        ),
        out_shape=jax.ShapeDtypeStruct((planes, seqs, slots, blk, width), BF),
        compiler_params=pltpu.CompilerParams(vmem_limit_bytes=VMEM_LIMIT),
        cost_estimate=BRIEF,
        name="attend_back",
    )(order, qkv, lse, grad, cos, sin)


TILE = 256


def up_kernel(count, *refs):
    hs, (wg, wu, wd) = refs[:count], refs[count : count + 3]
    refs = refs[count + 3 :]
    refs = refs[4:] if len(refs) > count + 6 else refs
    h_all, g_out, u_out, hidden_out = refs[:4]
    outs, (held, total) = refs[4 : 4 + count], refs[4 + count :]
    step = pl.program_id(0)
    rows = hs[0].shape[0]

    @pl.when(step == 0)
    def _():
        for i in range(count):
            held[i * rows : (i + 1) * rows, :] = hs[i][...]
        h_all[...] = held[...]
        total[...] = jnp.zeros_like(total)

    h = held[...]
    g, u = mm(h, wg[...]), mm(h, wu[...])
    hidden = (g * (1.0 / (1.0 + jnp.exp(-g))) * u).astype(BF)
    g_out[...], u_out[...], hidden_out[...] = g, u, hidden
    total[...] += mm(hidden, wd[...])

    @pl.when(step == pl.num_programs(0) - 1)
    def _():
        for i in range(count):
            outs[i][...] = total[i * rows : (i + 1) * rows, :].astype(outs[i].dtype)


def mlp(hs, gu_w, down_w, types, parts, which, held=None):
    rows, width = hs[0].shape
    part_ff = down_w.shape[0]
    count, tiles = len(hs), part_ff // TILE
    span = rows * count
    whole = pl.BlockSpec((rows, width), lambda i: (0, 0))
    tile = pl.BlockSpec((span, TILE), lambda i: (which, i))
    kept = [(width, BF), (part_ff, F32), (part_ff, F32), (part_ff, BF)]
    extra = [] if held is None else list(held)
    result = pl.pallas_call(
        functools.partial(up_kernel, count),
        grid=(tiles,),
        in_specs=[whole] * count
        + [
            pl.BlockSpec((width, TILE), lambda i: (0, i)),
            pl.BlockSpec((width, TILE), lambda i: (0, tiles + i)),
            pl.BlockSpec((TILE, width), lambda i: (i, 0)),
        ]
        + [pl.BlockSpec(memory_space=pl.ANY)] * len(extra),
        out_specs=[pl.BlockSpec((span, width), lambda i: (which, 0)), tile, tile, tile] + [whole] * count,
        out_shape=[jax.ShapeDtypeStruct((span * parts, w), t) for w, t in kept]
        + [jax.ShapeDtypeStruct((rows, width), t) for t in types],
        scratch_shapes=[pltpu.VMEM((span, width), BF), pltpu.VMEM((span, width), F32)],
        input_output_aliases={count + 3 + i: i for i in range(len(extra))},
        compiler_params=pltpu.CompilerParams(vmem_limit_bytes=48 * 1024 * 1024),
        cost_estimate=BRIEF,
        name="mlp",
    )(*hs, gu_w, gu_w, down_w, *extra)
    return result[:4], result[4:]


def down_kernel(count, *refs):
    ds, (g_in, u_in, wg, wu, wd) = refs[:count], refs[count : count + 5]
    refs = refs[count + 5 :]
    refs = refs[3:] if len(refs) > count + 5 else refs
    d_all, dg_out, du_out = refs[:3]
    outs, (held, total) = refs[3 : 3 + count], refs[3 + count :]
    step = pl.program_id(0)
    rows = ds[0].shape[0]

    @pl.when(step == 0)
    def _():
        for i in range(count):
            held[i * rows : (i + 1) * rows, :] = ds[i][...]
        d_all[...] = held[...]
        total[...] = jnp.zeros_like(total)

    dh = mm_t(held[...], wd[...])
    g = g_in[...]
    sig = 1.0 / (1.0 + jnp.exp(-g))
    dg = (dh * u_in[...] * sig * (1.0 + g * (1.0 - sig))).astype(BF)
    du = (dh * (g * sig)).astype(BF)
    dg_out[...], du_out[...] = dg, du
    total[...] += mm_t(dg, wg[...]) + mm_t(du, wu[...])

    @pl.when(step == pl.num_programs(0) - 1)
    def _():
        for i in range(count):
            outs[i][...] = total[i * rows : (i + 1) * rows, :].astype(outs[i].dtype)


def mlp_back(ds, g, u, gu_w, down_w, types, parts, which, held=None):
    rows, width = ds[0].shape
    part_ff = down_w.shape[0]
    count, tiles = len(ds), part_ff // TILE
    span = rows * count
    whole = pl.BlockSpec((rows, width), lambda i: (0, 0))
    tile = pl.BlockSpec((span, TILE), lambda i: (which, i))
    kept = [(width, BF), (part_ff, BF), (part_ff, BF)]
    extra = [] if held is None else list(held)
    result = pl.pallas_call(
        functools.partial(down_kernel, count),
        grid=(tiles,),
        in_specs=[whole] * count
        + [
            tile,
            tile,
            pl.BlockSpec((width, TILE), lambda i: (0, i)),
            pl.BlockSpec((width, TILE), lambda i: (0, tiles + i)),
            pl.BlockSpec((TILE, width), lambda i: (i, 0)),
        ]
        + [pl.BlockSpec(memory_space=pl.ANY)] * len(extra),
        out_specs=[pl.BlockSpec((span, width), lambda i: (which, 0)), tile, tile] + [whole] * count,
        out_shape=[jax.ShapeDtypeStruct((span * parts, w), t) for w, t in kept]
        + [jax.ShapeDtypeStruct((rows, width), t) for t in types],
        scratch_shapes=[pltpu.VMEM((span, width), BF), pltpu.VMEM((span, width), F32)],
        input_output_aliases={count + 5 + i: i for i in range(len(extra))},
        compiler_params=pltpu.CompilerParams(vmem_limit_bytes=48 * 1024 * 1024),
        cost_estimate=BRIEF,
        name="mlp_back",
    )(*ds, g, u, gu_w, gu_w, down_w, *extra)
    return result[:3], result[3:]


def outer(lefts, rights, which, by_rows, away=None, runs=1):
    count = max(len(lefts), len(rights))
    depth = sum(v.shape[0] for v in lefts)
    chunk = depth // count
    out_rows, out_cols = lefts[0].shape[1], rights[0].shape[1]
    out_rows, out_cols = (out_rows // 2, out_cols) if by_rows else (out_rows, out_cols // 2)
    tile = min(TILE, out_rows // runs)
    tiles = out_rows // tile
    run = tiles // runs

    def kernel(which, *refs):
        left, right = refs[: len(lefts)], refs[len(lefts) : len(lefts) + len(rights)]
        take = lambda group, i: group[i][...] if len(group) > 1 else group[0][i * chunk : (i + 1) * chunk, :]
        total = mm_rows(take(left, 0), take(right, 0))
        for i in range(1, count):
            total = total + mm_rows(take(left, i), take(right, i))
        if away is not None:
            total = total + refs[-2][...].astype(F32)
        refs[-1][...] = total.astype(BF)

    out_spec = pl.BlockSpec((tile, out_cols), lambda i, w: (i, 0))
    return pl.pallas_call(
        kernel,
        grid_spec=pltpu.PrefetchScalarGridSpec(
            num_scalar_prefetch=1,
            grid=(tiles,),
            in_specs=[
                pl.BlockSpec((v.shape[0], tile), lambda i, w: (0, (i // run + w[0]) * run + i if by_rows else i)) for v in lefts
            ]
            + [pl.BlockSpec((v.shape[0], out_cols), lambda i, w: (0, 0 if by_rows else w[0])) for v in rights]
            + ([] if away is None else [out_spec]),
            out_specs=out_spec,
        ),
        out_shape=jax.ShapeDtypeStruct((out_rows, out_cols), BF),
        compiler_params=pltpu.CompilerParams(vmem_limit_bytes=48 * 1024 * 1024),
        cost_estimate=BRIEF,
        name="outer",
    )(which.reshape(1).astype(jnp.int32), *lefts, *rights, *([] if away is None else [away]))


def project(lefts, weight, transposed, types):
    rows, depth = lefts[0].shape
    width = weight.shape[0] if transposed else weight.shape[1]
    tile = min(512, width)
    count = len(lefts)

    def kernel(*refs):
        left, (w,), outs = refs[:count], refs[count : count + 1], refs[count + 1 :]
        for i in range(count):
            result = (mm_t if transposed else mm)(left[i][...], w[...])
            if len(outs) > 1:
                outs[i][...] = result.astype(outs[i].dtype)
            else:
                outs[0][i * rows : (i + 1) * rows, :] = result.astype(outs[0].dtype)

    height = rows * count // len(types)
    return pl.pallas_call(
        kernel,
        grid=(width // tile,),
        in_specs=[pl.BlockSpec((rows, depth), lambda i: (0, 0))] * count
        + [
            pl.BlockSpec((tile, depth), lambda i: (i, 0))
            if transposed
            else pl.BlockSpec((depth, tile), lambda i: (0, i))
        ],
        out_specs=[pl.BlockSpec((height, tile), lambda i: (0, i))] * len(types),
        out_shape=[jax.ShapeDtypeStruct((height, width), t) for t in types],
        compiler_params=pltpu.CompilerParams(vmem_limit_bytes=48 * 1024 * 1024),
        cost_estimate=BRIEF,
        name="project",
    )(*lefts, weight)


def assemble(places, arrays, depth):
    width = arrays[0].shape[1]
    pieces = [(n, start) for n, v in enumerate(arrays) for start in range(0, v.shape[0], depth)]
    count = len(pieces)

    def kernel(places, *refs):
        sources, out, held, arrive, leave = refs[: len(arrays)], *refs[len(arrays) :]
        ins = [
            pltpu.make_async_copy(sources[n].at[pl.ds(start, depth), :], held.at[i], arrive.at[i])
            for i, (n, start) in enumerate(pieces)
        ]
        outs = [pltpu.make_async_copy(held.at[i], out.at[places[i]], leave.at[i]) for i in range(count)]
        for copy in ins:
            copy.start()
        for i in range(count):
            ins[i].wait()
            outs[i].start()
        for copy in outs:
            copy.wait()

    return pl.pallas_call(
        kernel,
        grid_spec=pltpu.PrefetchScalarGridSpec(
            num_scalar_prefetch=1,
            grid=(1,),
            in_specs=[pl.BlockSpec(memory_space=pl.ANY)] * len(arrays),
            out_specs=pl.BlockSpec(memory_space=pl.ANY),
            scratch_shapes=[
                pltpu.VMEM((count, depth, width), arrays[0].dtype),
                pltpu.SemaphoreType.DMA((count,)),
                pltpu.SemaphoreType.DMA((count,)),
            ],
        ),
        out_shape=jax.ShapeDtypeStruct((count, depth, width), arrays[0].dtype),
        compiler_params=pltpu.CompilerParams(vmem_limit_bytes=VMEM_LIMIT),
        cost_estimate=BRIEF,
        name="assemble",
    )(places, *arrays).reshape(count * depth, width)


def take_columns(which, arrays, groups, members):
    depth, width = arrays[0].shape
    part = width // (groups * members)
    kept = len(which)
    if part % HD:
        views = [v.reshape(depth, groups, members, part) for v in arrays]
        return [
            jnp.concatenate(
                [lax.dynamic_slice_in_dim(v, k, 1, 2).reshape(depth, groups * part) for v in views], 1
            )
            for k in which
        ]

    def kernel(which, *refs):
        sources, outs = refs[: len(arrays)], refs[len(arrays) :]
        for k in range(kept):
            for n, source in enumerate(sources):
                for i in range(groups):
                    start = pl.multiple_of(i * members * part + which[k] * part, HD)
                    outs[k][:, (n * groups + i) * part : (n * groups + i + 1) * part] = source[:, pl.ds(start, part)]

    tile = min(64, depth)
    return pl.pallas_call(
        kernel,
        grid_spec=pltpu.PrefetchScalarGridSpec(
            num_scalar_prefetch=1,
            grid=(depth // tile,),
            in_specs=[pl.BlockSpec((tile, width), lambda i, w: (i, 0))] * len(arrays),
            out_specs=[pl.BlockSpec((tile, len(arrays) * groups * part), lambda i, w: (i, 0))] * kept,
        ),
        out_shape=[jax.ShapeDtypeStruct((depth, len(arrays) * groups * part), arrays[0].dtype)] * kept,
        name="take_columns",
    )(jnp.stack(which).astype(jnp.int32), *arrays)


def body(planes, shards, tokens, pairs, valid, teacher, w_query, w_key, w_value, w_out, w_gate, w_up, w_down):
    seqs, slots, blk, width = tokens.shape
    ff = w_gate.shape[1]
    rows = seqs * slots * blk
    world = planes * shards
    near = planes // 2
    all_heads = width // HD
    heads = all_heads // planes
    mine = heads * HD
    own_rows = width // shards
    part_ff = ff // planes
    length = planes * slots * blk
    unit = width // world
    both = ("ctx", "fsdp")

    c, f = lax.axis_index("ctx"), lax.axis_index("fsdp")
    far, low = c // near, c % near
    core, x, y = f % 2, f // 2 % 2, f // 4
    group = x * near + low

    def after(array, *others):
        return lax.optimization_barrier((array, *others))[0]

    def flip(array, bits):
        return lax.ppermute(array, "fsdp", [(i, i ^ bits) for i in range(shards)])

    def flip_ctx(array, bits):
        return lax.ppermute(array, "ctx", [(i, i ^ bits) for i in range(planes)])

    def hop(array, j):
        dx, dz = j // near, j % near
        if dz == 0:
            return flip(array, 2 * dx)
        if dx == 0:
            return flip_ctx(array, dz)
        return lax.ppermute(
            array,
            both,
            [(p * shards + s, (p ^ dz) * shards + (s ^ 2)) for p in range(planes) for s in range(shards)],
        )

    def send(array, homes):
        moved = lax.ppermute(array, both, [(i, to) for i, to in enumerate(homes) if i != to])
        stays = jnp.array([i == to for i, to in enumerate(homes)])[c * shards + f]
        return jnp.where(stays, array, moved)

    def swap(array):
        homes = []
        for p in range(planes):
            for s in range(shards):
                to = (s // 2 % 2) * near + p % near
                homes.append(to * shards + (s - s // 2 % 2 * 2 + p // near * 2))
        return send(array, homes)

    cos, sin = tables(length)
    ranks = jnp.argsort(pairs.reshape(-1))
    owner = ranks // slots
    relative = ((owner // near) ^ x) * near + ((owner % near) ^ low)
    order = (relative * slots + ranks % slots).astype(jnp.int32)

    def over_y(piece):
        return [flip(piece, bits) for bits in range(4, shards, 4)]

    y_bits = list(range(4, shards, 4))

    def put(*items):
        keys = [k for _, own_keys in items for k in own_keys]
        depth = items[0][0].shape[0] // len(items[0][1])
        places = jnp.stack([f ^ k for k in keys]).astype(jnp.int32)
        return assemble(places, [v for v, _ in items], depth)

    def put_pairs(both_x, both_y, other_x, other_y):
        items = [(both_x, [0, 2]), (other_x, [1, 3])]
        for bits, v, w in zip(y_bits, both_y, other_y):
            items += [(v, [bits, bits + 2]), (w, [bits + 1, bits + 3])]
        return put(*items)

    def head_columns(g):
        return jnp.concatenate(
            [lax.dynamic_slice_in_dim(w, g * mine, mine, 1) for w in (w_query, w_key, w_value)], 1
        )

    def ff_rows(g):
        return lax.dynamic_slice_in_dim(w_down, g * (part_ff // shards), part_ff // shards, 0)

    def own_heads(weight):
        sends, spreads = [], {}
        for p in range(planes):
            for s in range(shards):
                q = s // 2
                if q % near == p % near:
                    at = s // 4 * 4 + q // near * 2 + s % 2
                    if at != s:
                        sends.append((p * shards + s, p * shards + at))
                    for d in range(4, shards, 4):
                        spreads.setdefault(d, []).append((p * shards + at, p * shards + (at ^ d)))
        q = f // 2
        stays = (q % near == low) & (f // 4 * 4 + q // near * 2 + core == f)
        first = jnp.where(stays, weight, lax.ppermute(weight, both, sends))

        def rest(first):
            found = first
            for pairs_of in spreads.values():
                found = found + lax.ppermute(first, both, pairs_of)
            return found

        return first, rest

    cut = planes // 2
    early = list(range(1, cut + 1))
    late = [0, *range(cut + 1, planes)]
    early_types = [BF] * cut
    late_types = [F32] + [BF] * (planes - cut - 1)

    def gather_far(found):
        if near != 2:
            return [hop(found[0], j) for j in late[1:]]
        half = rows // 2
        return [hop(found[1][:half], 2), hop(found[2][half:], 1)]

    def joined(found, others):
        return found + (others if near != 2 else [jnp.concatenate(others, 0)])

    def reduce_far(parts):
        if near != 2:
            return [hop(parts[j], j) for j in late[1:]]
        half = rows // 2
        return [hop(parts[3][:half], 2), hop(parts[3][half:], 1)]

    def reduce_near(parts, received):
        if near != 2:
            return add_all(parts[0], received), [hop(parts[j], j) for j in early]
        half = rows // 2
        more = lambda part, other: (part.astype(F32) + other.astype(F32)).astype(BF)
        to_low = jnp.concatenate([more(parts[1][:half], received[0]), parts[1][half:]], 0)
        to_x = jnp.concatenate([parts[2][:half], more(parts[2][half:], received[1])], 0)
        return parts[0], [hop(to_low, 1), hop(to_x, 2)]

    def add_all(total, others):
        for other in others:
            total = total + other.astype(F32)
        return total

    region = lambda *values: lax.optimization_barrier(values)

    gu_own, gu_send = take_columns([group, group ^ near], [w_gate, w_up], shards, planes)
    stream_low = swap(tokens.reshape(rows, width))
    qkv_own = head_columns(group)
    qkv_other = flip(head_columns(group ^ near), 2)
    gu_own_y = over_y(gu_own)
    heads_first, heads_rest = own_heads(w_out)
    stream = stream_low.astype(F32)
    normed_one, inverse_one = normalize(stream)
    qkv_both = jnp.concatenate([qkv_own, qkv_other], 0)
    h1, stream_low, qkv_both, gu_own, gu_own_y, gu_send, heads_first, w_down = region(
        [normed_one.astype(BF)], stream_low, qkv_both, gu_own, gu_own_y, gu_send, heads_first, w_down
    )

    h1 = h1 + [hop(h1[0], j) for j in early]
    qkv_y = over_y(qkv_both)
    qkv_pair = flip(qkv_both, 1)
    found = heads_rest(heads_first)
    h1, qkv_both, qkv_pair, w_down, gu_send = region(h1, qkv_both, qkv_pair, w_down, gu_send)

    others = gather_far(h1)
    down_own = ff_rows(group)
    down_other = flip(ff_rows(group ^ near), 2)
    others, found, down_own, down_other, qkv_y, gu_send, gu_own_y, teacher = region(
        others, found, down_own, down_other, qkv_y, gu_send, gu_own_y, teacher
    )
    h1 = joined(h1, others)

    gu_other = flip(gu_send, 2)
    down_both = jnp.concatenate([down_own, down_other], 0)
    down_y = over_y(down_both)
    other = flip(found, 1)
    qkv_y_pair = [flip(v, 1) for v in qkv_y]
    w_qkv = put_pairs(qkv_both, qkv_y, qkv_pair, qkv_y_pair)
    (qkv,) = project(h1, w_qkv, False, [F32])
    qkv = qkv.reshape(planes, seqs, slots, blk, 3 * mine)
    mixed, lse = attend(order, qkv, cos, sin, heads)
    even = core == 0
    w_out_mine = jnp.concatenate([jnp.where(even, found, other), jnp.where(even, other, found)], 0)
    group_types = [F32] + [BF] * (planes - 1)
    products = project([mixed[s].reshape(rows, mine) for s in range(planes)], w_out_mine, False, group_types)
    products, gu_other, down_both, down_y, gu_own, gu_own_y, teacher = region(
        products, gu_other, down_both, down_y, gu_own, gu_own_y, teacher
    )

    received = reduce_far(products)
    gu_other_y = over_y(gu_other)
    down_pair = flip(down_both, 1)
    gu_own_pair = flip(gu_own, 1)
    received, products, down_pair, gu_other, down_y, gu_own_pair, gu_own_y = region(
        received, products, down_pair, gu_other, down_y, gu_own_pair, gu_own_y
    )

    own, received = reduce_near(products, received)
    down_y_pair = [flip(v, 1) for v in down_y]
    gu_own_y_pair = [flip(v, 1) for v in gu_own_y]
    residual = stream + add_all(own, received)
    normed_two, inverse_two = normalize(residual)
    h2, gu_other_y, gu_other, down_y_pair, gu_own_y_pair, valid = region(
        [normed_two.astype(BF)], gu_other_y, gu_other, down_y_pair, gu_own_y_pair, valid
    )

    h2 = h2 + [hop(h2[0], j) for j in early]
    gu_other_pair = flip(gu_other, 1)
    gu_items = [(gu_own, [0]), (gu_own_pair, [1]), (gu_other, [2]), (gu_other_pair, [3])]
    for bits, v, w, z in zip(y_bits, gu_own_y, gu_own_y_pair, gu_other_y):
        gu_items += [(v, [bits]), (w, [bits + 1]), (z, [bits + 2]), (flip(z, 1), [bits + 3])]
    down_w = put_pairs(down_both, down_y, down_pair, down_y_pair)
    gu_w = put(*gu_items)
    h2, gu_w, down_w, valid, teacher = region(h2, gu_w, down_w, valid, teacher)

    others = gather_far(h2)
    goal_low = swap(teacher.reshape(rows, width))
    kept, outs = mlp([h2[j] for j in early], gu_w, down_w, early_types, 2, 0)
    outs, kept, others = region(outs, kept, others)
    h2 = joined(h2, others)

    received = [hop(v, j) for v, j in zip(outs, early)]
    (h2_all, gates, ups, hidden_all), outs = mlp(
        [h2[j] for j in late], gu_w, down_w, late_types, 2, 1, kept
    )
    received, outs, h2_all, gates, ups, hidden_all, valid, goal_low = region(
        received, outs, h2_all, gates, ups, hidden_all, valid, goal_low
    )

    received = received + [hop(v, j) for v, j in zip(outs[1:], late[1:])]
    valid_float = swap(valid.reshape(rows, 1)).astype(F32)

    output = residual + add_all(outs[0], received)
    deviation = output - goal_low.astype(F32)
    grad_output = valid_float * deviation
    sums = jnp.stack([jnp.sum(grad_output * deviation), jnp.sum(valid_float)])
    sums0 = jnp.broadcast_to(sums[:, None, None], (2, 8, HD))
    sums0, grad_output, output = region(sums0, grad_output, output)

    sums = sums0
    for j in range(1, planes):
        sums = sums + hop(sums0, j)
    sums = sums + flip_ctx(sums, near)
    low_grad, low_output, sums = region(grad_output.astype(BF), output.astype(BF), sums)

    steps = [1 << b for b in reversed(range(2, shards.bit_length() - 1))]

    def halve(part, axis, bit, move, bits):
        half = part.shape[axis] // 2
        take = lambda k: lax.dynamic_slice_in_dim(part, k * half, half, axis)
        away = move(take(1 - bit), bits)
        return (take(bit).astype(F32) + away.astype(F32)).astype(BF)

    def parts(whole):
        return whole.reshape(2, near, shards // 4, 2, 2, unit, whole.shape[1])

    def across_y(part, axis):
        for step in steps:
            part = halve(part, axis, f // step % 2, flip, step)
        return part

    def across_far(part):
        return halve(part, 0, far, flip_ctx, near)

    def place_rows(part, place):
        homes = []
        for p in range(planes):
            for s in range(shards):
                homes.append(place(s % 2, s // 4, p // near, (s // 2 % 2) * near + p % near))
        return send(part, homes).astype(F32)

    def take(v, k, axis):
        return lax.dynamic_index_in_dim(v, k, axis, keepdims=False)

    def core_away(part):
        return flip(take(part.reshape(near, 2, 2, unit, part.shape[-1]), 1 - core, 2), 1)

    def core_joined(part, away):
        keep = take(part.reshape(near, 2, 2, unit, part.shape[-1]), core, 2)
        even = core == 0
        return jnp.concatenate([jnp.where(even, keep, away), jnp.where(even, away, keep)], -1)

    def column_pieces(part):
        return [take(take(part, x ^ (j // near), 1), low ^ (j % near), 0) for j in range(planes)]

    def columns_placed(pieces):
        places = jnp.stack([group ^ j for j in range(planes)]).astype(jnp.int32)
        return assemble(places, pieces, unit).reshape(planes, unit, -1)

    dm = [low_grad] + [hop(low_grad, j) for j in early]
    for bits in [1, *(1 << b for b in range(2, shards.bit_length() - 1))]:
        sums = sums + flip(sums, bits)
    dm, sums, low_output = region(dm, sums, low_output)

    others = gather_far(dm)
    kept, backs = mlp_back([dm[j] for j in early], gates, ups, gu_w, down_w, early_types, 2, 0)
    backs, kept, others, sums, low_output = region(backs, kept, others, sums, low_output)
    dm = joined(dm, others)

    received = [hop(v, j) for v, j in zip(backs, early)]
    dm_runs = [dm[j] for j in early + late]
    away = flip(outer([hidden_all], dm_runs, 1 - core, True, None, 2), 1)
    (_, dg_all, du_all), backs = mlp_back(
        [dm[j] for j in late], gates, ups, gu_w, down_w, late_types, 2, 1, kept
    )
    g_down = outer([hidden_all], dm_runs, core, True, away, 2)
    received, backs, g_down, dg_all, du_all, h2_all, low_output = region(
        received, backs, g_down, dg_all, du_all, h2_all, low_output
    )

    received = received + [hop(v, j) for v, j in zip(backs[1:], late[1:])]
    activations = swap(low_output)
    g_down = across_y(g_down.reshape(2, shards // 4, part_ff // shards, width), 1)
    gate_half = outer([h2_all], [dg_all], 1 - core, False)
    up_half = outer([h2_all], [du_all], 1 - core, False)
    grad_two = add_all(backs[0], received)
    grad_residual = grad_output + norm_back(grad_two, normed_two, inverse_two)
    dab, gate_half, up_half, g_down, dg_all, du_all, activations = region(
        [grad_residual.astype(BF)], gate_half, up_half, g_down, dg_all, du_all, activations
    )

    dab = dab + [hop(dab[0], j) for j in early]
    gate_away, up_away = flip(gate_half, 1), flip(up_half, 1)
    g_gate = outer([h2_all], [dg_all], core, False, gate_away)
    dab, g_gate, up_away, du_all, g_down = region(dab, g_gate, up_away, du_all, g_down)

    others = gather_far(dab)
    g_gate = across_y(parts(g_gate), 2)
    g_up = outer([h2_all], [du_all], core, False, up_away)
    others, g_up, g_down = region(others, g_up, g_down)
    dab = joined(dab, others)

    up_first, up_second = jnp.split(parts(g_up), 2, -1)
    up_first = across_y(up_first, 2)
    g_down = across_far(g_down)
    (do,) = project(dab, w_out_mine, True, [BF])
    dqkv = attend_back(order, qkv, lse, do.reshape(planes, seqs, slots, blk, mine), cos, sin, heads)
    dqkv = dqkv.reshape(planes * rows, 3 * mine)
    qkv_half = outer(h1, [dqkv], 1 - core, False)
    mixed = mixed.reshape(planes * rows, mine)
    out_half = outer([mixed], dab, 1 - core, True)
    dqkv, qkv_half, out_half, g_gate, g_down, up_first, up_second = region(
        dqkv, qkv_half, out_half, g_gate, g_down, up_first, up_second
    )

    qkv_away, out_away = flip(qkv_half, 1), flip(out_half, 1)
    backs = project([dqkv[i * rows : (i + 1) * rows] for i in range(planes)], w_qkv, True, group_types)
    up_second = across_y(up_second, 2)
    gate_first, gate_second = jnp.split(g_gate, 2, -1)
    gate_first = across_far(gate_first)
    backs, dqkv, qkv_away, out_away, up_second, gate_first, gate_second = region(
        backs, dqkv, qkv_away, out_away, up_second, gate_first, gate_second
    )

    gate_second = across_far(gate_second)
    g_up = jnp.concatenate([up_first, up_second], -1)
    received = reduce_far(backs)
    g_qkv = parts(outer(h1, [dqkv], core, False, qkv_away))
    g_out = outer([mixed], dab, core, True, out_away)
    received, backs, g_qkv, g_out, g_down, gate_first, gate_second, g_up = region(
        received, backs, g_qkv, g_out, g_down, gate_first, gate_second, g_up
    )

    own, received = reduce_near(backs, received)
    g_up = across_far(g_up)
    g_out = across_y(g_out, 0)
    g_gate = jnp.concatenate([gate_first, gate_second], -1)
    g_down = place_rows(
        g_down.reshape(ff // world, width),
        lambda core, y, far, g: far * (shards // 2) * planes + (core * (shards // 4) + y) * planes + g,
    )
    grad_one = add_all(own, received)
    grad_stream = grad_residual + norm_back(grad_one, normed_one, inverse_one)
    low_stream, g_out, g_qkv, g_gate, g_up, g_down = region(
        grad_stream.astype(BF), g_out, g_qkv, g_gate, g_up, g_down
    )

    grad_low = swap(low_stream)
    g_qkv = across_y(g_qkv, 2)
    g_out = across_far(g_out)
    gate_core, up_core = core_away(g_gate), core_away(g_up)
    pieces = [column_pieces(core_joined(v, w)) for v, w in ((g_gate, gate_core), (g_up, up_core))]
    pieces = [jnp.concatenate(v, 1) for v in zip(*pieces)]
    grad_low, g_qkv, g_out, pieces = region(grad_low, g_qkv, g_out, pieces)

    g_qkv = across_far(g_qkv)
    g_out = place_rows(g_out, lambda core, y, far, g: g * shards + (core * (shards // 4) + y) * 2 + far)
    pieces = [hop(v, j) if j else v for j, v in enumerate(pieces)]
    pieces, g_qkv, g_out = region(pieces, g_qkv, g_out)
    qkv_pieces = column_pieces(core_joined(g_qkv, core_away(g_qkv)))
    qkv_pieces, pieces = region(qkv_pieces, pieces)
    qkv_pieces = [hop(v, j) if j else v for j, v in enumerate(qkv_pieces)]
    count = sums[1, 0, 0]
    loss = sums[0, 0, 0] / (count * width)
    factor = (rows * world) / count
    grad_input = grad_low.astype(F32) * factor
    ff_order = lambda v: v.reshape(planes, unit, shards, -1).transpose(1, 2, 0, 3).reshape(unit, ff)
    placed = columns_placed(pieces)
    g_gate = ff_order(placed[:, :, :part_ff]).astype(F32)
    g_up = ff_order(placed[:, :, part_ff:]).astype(F32)
    g_qkv = columns_placed(qkv_pieces).reshape(planes, unit, 3, mine).transpose(2, 1, 0, 3)
    g_qkv = g_qkv.reshape(3, unit, width).astype(F32)
    return (
        activations.reshape(tokens.shape),
        loss,
        grad_input.reshape(tokens.shape),
        g_qkv[0] * factor,
        g_qkv[1] * factor,
        g_qkv[2] * factor,
        g_out * factor,
        g_gate * factor,
        g_up * factor,
        g_down * factor,
    )


def solution(mesh):
    tokens = P("fsdp", "ctx", None, None)
    weight = P("fsdp", None)
    grad = P(("ctx", "fsdp"), None)
    in_specs = (tokens, P(), P("fsdp", "ctx", None), tokens) + (weight,) * 7
    out_specs = (tokens, P(), tokens) + (grad,) * 7
    step = functools.partial(body, mesh.shape["ctx"], mesh.shape["fsdp"])
    return jax.shard_map(step, mesh=mesh, in_specs=in_specs, out_specs=out_specs, check_vma=False)
```

```python
import functools

import jax
import jax.numpy as jnp
from jax import lax
from jax.experimental import pallas as pl
from jax.experimental.pallas import tpu as pltpu
from jax.sharding import PartitionSpec as P

HD = 128
EPS = 1e-05
BF = jnp.bfloat16
F32 = jnp.float32
NEG = -1e30


def normalize(rows):
    centered = rows - jnp.mean(rows, -1, keepdims=True)
    inverse = lax.rsqrt(jnp.mean(centered * centered, -1, keepdims=True) + EPS)
    return centered * inverse, inverse


def norm_back(gradient, normed, inverse):
    centered = gradient - jnp.mean(gradient, -1, keepdims=True)
    return inverse * (centered - normed * jnp.mean(gradient * normed, -1, keepdims=True))


def mm(left, right):
    return jnp.dot(left, right, preferred_element_type=F32)


def mm_t(left, right):
    return lax.dot_general(left, right, (((1,), (1,)), ((), ())), preferred_element_type=F32)


def mm_rows(left, right):
    return lax.dot_general(left, right, (((0,), (0,)), ((), ())), preferred_element_type=F32)


def tables(length):
    frequency = 10000.0 ** (-2.0 * jnp.arange(HD // 2, dtype=F32) / HD)
    phases = jnp.arange(length, dtype=F32)[:, None] * frequency[None, :]
    cosine, sine = jnp.cos(phases), jnp.sin(phases)
    return jnp.concatenate([cosine, cosine], 1), jnp.concatenate([-sine, sine], 1)


def fwd_kernel(heads, order, qkv, cos, sin, out, lse, q_s, k_s, v_s):
    planes, _, slots, blk, _ = qkv.shape
    blocks = planes * slots
    scale = HD ** -0.5

    def head(h, carry):
        col = pl.multiple_of(h * HD, HD)

        def load(b, carry):
            where = order[b]
            s, t = where // slots, where % slots
            row = pl.ds(pl.multiple_of(b * blk, blk), blk)
            c, n = cos[row, :], sin[row, :]
            q = qkv[s, 0, t, :, pl.ds(col, HD)]
            k = qkv[s, 0, t, :, pl.ds(pl.multiple_of(heads * HD + col, HD), HD)]
            q_s[row, :] = ((q * c + pltpu.roll(q, HD // 2, 1) * n) * scale).astype(BF)
            k_s[row, :] = (k * c + pltpu.roll(k, HD // 2, 1) * n).astype(BF)
            v_s[row, :] = qkv[s, 0, t, :, pl.ds(pl.multiple_of(2 * heads * HD + col, HD), HD)].astype(BF)
            return carry

        lax.fori_loop(0, blocks, load, 0)
        for b in range(blocks):
            keys = (b + 1) * blk
            scores = mm_t(q_s[b * blk : keys, :], k_s[0:keys, :])
            top = jnp.max(scores, -1, keepdims=True)
            raised = jnp.exp(scores - top)
            total = jnp.sum(raised, -1, keepdims=True)
            probs = (raised * (1.0 / total)).astype(BF)
            mixed = mm(probs, v_s[0:keys, :])
            where = order[b]
            s, t = where // slots, where % slots
            out[s, 0, t, :, pl.ds(col, HD)] = mixed.astype(BF)
            lse[s, 0, t, :, pl.ds(col, HD)] = jnp.broadcast_to(top + jnp.log(total), (blk, HD))
        return carry

    lax.fori_loop(0, heads, head, 0)


def bwd_kernel(heads, order, qkv, lse, grad, cos, sin, dqkv, q_s, k_s, v_s, g_s, l_s, dk_s, dv_s):
    planes, _, slots, blk, _ = qkv.shape
    blocks = planes * slots
    scale = HD ** -0.5

    def head(h, carry):
        col = pl.multiple_of(h * HD, HD)
        kcol = pl.multiple_of(heads * HD + col, HD)
        vcol = pl.multiple_of(2 * heads * HD + col, HD)

        def load(b, carry):
            where = order[b]
            s, t = where // slots, where % slots
            row = pl.ds(pl.multiple_of(b * blk, blk), blk)
            c, n = cos[row, :], sin[row, :]
            q = qkv[s, 0, t, :, pl.ds(col, HD)]
            k = qkv[s, 0, t, :, pl.ds(kcol, HD)]
            q_s[row, :] = ((q * c + pltpu.roll(q, HD // 2, 1) * n) * scale).astype(BF)
            k_s[row, :] = (k * c + pltpu.roll(k, HD // 2, 1) * n).astype(BF)
            v_s[row, :] = qkv[s, 0, t, :, pl.ds(vcol, HD)].astype(BF)
            g_s[row, :] = grad[s, 0, t, :, pl.ds(col, HD)]
            l_s[row, :] = lse[s, 0, t, :, pl.ds(col, HD)]
            return carry

        lax.fori_loop(0, blocks, load, 0)
        dk_s[...] = jnp.zeros_like(dk_s)
        dv_s[...] = jnp.zeros_like(dv_s)
        for b in range(blocks):
            keys = (b + 1) * blk
            mine = slice(b * blk, keys)
            scores = mm_t(q_s[mine, :], k_s[0:keys, :])
            probs = jnp.exp(scores - l_s[mine, 0:1])
            dprobs = mm_t(g_s[mine, :], v_s[0:keys, :])
            delta = jnp.sum(probs * dprobs, -1, keepdims=True)
            dscores = (probs * (dprobs - delta)).astype(BF)
            dq = mm(dscores, k_s[0:keys, :]) * scale
            dk_s[0:keys, :] += mm_rows(dscores, q_s[mine, :])
            dv_s[0:keys, :] += mm_rows(probs.astype(BF), g_s[mine, :])
            where = order[b]
            s, t = where // slots, where % slots
            dq = dq * cos[mine, :] - pltpu.roll(dq, HD // 2, 1) * sin[mine, :]
            dqkv[s, 0, t, :, pl.ds(col, HD)] = dq.astype(BF)

        def store(b, carry):
            where = order[b]
            s, t = where // slots, where % slots
            row = pl.ds(pl.multiple_of(b * blk, blk), blk)
            dk = dk_s[row, :]
            dk = dk * cos[row, :] - pltpu.roll(dk, HD // 2, 1) * sin[row, :]
            dqkv[s, 0, t, :, pl.ds(kcol, HD)] = dk.astype(BF)
            dqkv[s, 0, t, :, pl.ds(vcol, HD)] = dv_s[row, :].astype(BF)
            return carry

        lax.fori_loop(0, blocks, store, 0)
        return carry

    lax.fori_loop(0, heads, head, 0)


VMEM_LIMIT = 56 * 1024 * 1024
BRIEF = pl.CostEstimate(flops=1024, bytes_accessed=1024, transcendentals=0)


def attend(order, qkv, cos, sin, heads):
    planes, seqs, slots, blk, width = qkv.shape
    length = planes * slots * blk
    spec = lambda w: pl.BlockSpec((planes, 1, slots, blk, w), lambda i, o: (0, i, 0, 0, 0))
    table = pl.BlockSpec((length, HD), lambda i, o: (0, 0))
    return pl.pallas_call(
        functools.partial(fwd_kernel, heads),
        grid_spec=pltpu.PrefetchScalarGridSpec(
            num_scalar_prefetch=1,
            grid=(seqs,),
            in_specs=[spec(width), table, table],
            out_specs=[spec(heads * HD), spec(heads * HD)],
            scratch_shapes=[pltpu.VMEM((length, HD), BF)] * 3,
        ),
        out_shape=[
            jax.ShapeDtypeStruct((planes, seqs, slots, blk, heads * HD), BF),
            jax.ShapeDtypeStruct((planes, seqs, slots, blk, heads * HD), F32),
        ],
        compiler_params=pltpu.CompilerParams(vmem_limit_bytes=VMEM_LIMIT),
        cost_estimate=BRIEF,
        name="attend",
    )(order, qkv, cos, sin)


def attend_back(order, qkv, lse, grad, cos, sin, heads):
    planes, seqs, slots, blk, width = qkv.shape
    length = planes * slots * blk
    spec = lambda w: pl.BlockSpec((planes, 1, slots, blk, w), lambda i, o: (0, i, 0, 0, 0))
    table = pl.BlockSpec((length, HD), lambda i, o: (0, 0))
    return pl.pallas_call(
        functools.partial(bwd_kernel, heads),
        grid_spec=pltpu.PrefetchScalarGridSpec(
            num_scalar_prefetch=1,
            grid=(seqs,),
            in_specs=[spec(width), spec(heads * HD), spec(heads * HD), table, table],
            out_specs=spec(width),
            scratch_shapes=[pltpu.VMEM((length, HD), BF)] * 4 + [pltpu.VMEM((length, HD), F32)] * 3,
        ),
        out_shape=jax.ShapeDtypeStruct((planes, seqs, slots, blk, width), BF),
        compiler_params=pltpu.CompilerParams(vmem_limit_bytes=VMEM_LIMIT),
        cost_estimate=BRIEF,
        name="attend_back",
    )(order, qkv, lse, grad, cos, sin)


TILE = 512


def up_kernel(count, *refs):
    hs, (wg, wu, wd) = refs[:count], refs[count : count + 3]
    refs = refs[count + 3 :]
    refs = refs[4:] if len(refs) > count + 6 else refs
    h_all, g_out, u_out, hidden_out = refs[:4]
    outs, (held, total) = refs[4 : 4 + count], refs[4 + count :]
    step = pl.program_id(0)
    rows = hs[0].shape[0]

    @pl.when(step == 0)
    def _():
        for i in range(count):
            held[i * rows : (i + 1) * rows, :] = hs[i][...]
        h_all[...] = held[...]
        total[...] = jnp.zeros_like(total)

    h = held[...]
    g, u = mm(h, wg[...]), mm(h, wu[...])
    hidden = (g * (1.0 / (1.0 + jnp.exp(-g))) * u).astype(BF)
    g_out[...], u_out[...], hidden_out[...] = g, u, hidden
    total[...] += mm(hidden, wd[...])

    @pl.when(step == pl.num_programs(0) - 1)
    def _():
        for i in range(count):
            outs[i][...] = total[i * rows : (i + 1) * rows, :].astype(outs[i].dtype)


def mlp(hs, gu_w, down_w, types, parts, which, held=None):
    rows, width = hs[0].shape
    part_ff = down_w.shape[0]
    count = len(hs)
    span = rows * count
    depth = TILE if span <= TILE else TILE // 2
    tiles = part_ff // depth
    whole = pl.BlockSpec((rows, width), lambda i: (0, 0))
    tile = pl.BlockSpec((span, depth), lambda i: (which, i))
    kept = [(width, BF), (part_ff, F32), (part_ff, F32), (part_ff, BF)]
    extra = [] if held is None else list(held)
    result = pl.pallas_call(
        functools.partial(up_kernel, count),
        grid=(tiles,),
        in_specs=[whole] * count
        + [
            pl.BlockSpec((width, depth), lambda i: (0, i)),
            pl.BlockSpec((width, depth), lambda i: (0, tiles + i)),
            pl.BlockSpec((depth, width), lambda i: (i, 0)),
        ]
        + [pl.BlockSpec(memory_space=pl.ANY)] * len(extra),
        out_specs=[pl.BlockSpec((span, width), lambda i: (which, 0)), tile, tile, tile] + [whole] * count,
        out_shape=[jax.ShapeDtypeStruct((span * parts, w), t) for w, t in kept]
        + [jax.ShapeDtypeStruct((rows, width), t) for t in types],
        scratch_shapes=[pltpu.VMEM((span, width), BF), pltpu.VMEM((span, width), F32)],
        input_output_aliases={count + 3 + i: i for i in range(len(extra))},
        compiler_params=pltpu.CompilerParams(vmem_limit_bytes=48 * 1024 * 1024),
        cost_estimate=BRIEF,
        name="mlp",
    )(*hs, gu_w, gu_w, down_w, *extra)
    return result[:4], result[4:]


def down_kernel(count, *refs):
    ds, (g_in, u_in, wg, wu, wd) = refs[:count], refs[count : count + 5]
    refs = refs[count + 5 :]
    refs = refs[3:] if len(refs) > count + 5 else refs
    d_all, dg_out, du_out = refs[:3]
    outs, (held, total) = refs[3 : 3 + count], refs[3 + count :]
    step = pl.program_id(0)
    rows = ds[0].shape[0]

    @pl.when(step == 0)
    def _():
        for i in range(count):
            held[i * rows : (i + 1) * rows, :] = ds[i][...]
        d_all[...] = held[...]
        total[...] = jnp.zeros_like(total)

    dh = mm_t(held[...], wd[...])
    g = g_in[...]
    sig = 1.0 / (1.0 + jnp.exp(-g))
    dg = (dh * u_in[...] * sig * (1.0 + g * (1.0 - sig))).astype(BF)
    du = (dh * (g * sig)).astype(BF)
    dg_out[...], du_out[...] = dg, du
    total[...] += mm_t(dg, wg[...]) + mm_t(du, wu[...])

    @pl.when(step == pl.num_programs(0) - 1)
    def _():
        for i in range(count):
            outs[i][...] = total[i * rows : (i + 1) * rows, :].astype(outs[i].dtype)


def mlp_back(ds, g, u, gu_w, down_w, types, parts, which, held=None):
    rows, width = ds[0].shape
    part_ff = down_w.shape[0]
    count = len(ds)
    span = rows * count
    depth = TILE if span <= TILE else TILE // 2
    tiles = part_ff // depth
    whole = pl.BlockSpec((rows, width), lambda i: (0, 0))
    tile = pl.BlockSpec((span, depth), lambda i: (which, i))
    kept = [(width, BF), (part_ff, BF), (part_ff, BF)]
    extra = [] if held is None else list(held)
    result = pl.pallas_call(
        functools.partial(down_kernel, count),
        grid=(tiles,),
        in_specs=[whole] * count
        + [
            tile,
            tile,
            pl.BlockSpec((width, depth), lambda i: (0, i)),
            pl.BlockSpec((width, depth), lambda i: (0, tiles + i)),
            pl.BlockSpec((depth, width), lambda i: (i, 0)),
        ]
        + [pl.BlockSpec(memory_space=pl.ANY)] * len(extra),
        out_specs=[pl.BlockSpec((span, width), lambda i: (which, 0)), tile, tile] + [whole] * count,
        out_shape=[jax.ShapeDtypeStruct((span * parts, w), t) for w, t in kept]
        + [jax.ShapeDtypeStruct((rows, width), t) for t in types],
        scratch_shapes=[pltpu.VMEM((span, width), BF), pltpu.VMEM((span, width), F32)],
        input_output_aliases={count + 5 + i: i for i in range(len(extra))},
        compiler_params=pltpu.CompilerParams(vmem_limit_bytes=48 * 1024 * 1024),
        cost_estimate=BRIEF,
        name="mlp_back",
    )(*ds, g, u, gu_w, gu_w, down_w, *extra)
    return result[:3], result[3:]


def outer(lefts, rights, which, by_rows, away=None, runs=1):
    count = max(len(lefts), len(rights))
    depth = sum(v.shape[0] for v in lefts)
    chunk = depth // count
    out_rows, out_cols = lefts[0].shape[1], rights[0].shape[1]
    out_rows, out_cols = (out_rows // 2, out_cols) if by_rows else (out_rows, out_cols // 2)
    tile = min(TILE, out_rows // runs)
    tiles = out_rows // tile
    run = tiles // runs

    def kernel(which, *refs):
        left, right = refs[: len(lefts)], refs[len(lefts) : len(lefts) + len(rights)]
        take = lambda group, i: group[i][...] if len(group) > 1 else group[0][i * chunk : (i + 1) * chunk, :]
        total = mm_rows(take(left, 0), take(right, 0))
        for i in range(1, count):
            total = total + mm_rows(take(left, i), take(right, i))
        if away is not None:
            total = total + refs[-2][...].astype(F32)
        refs[-1][...] = total.astype(BF)

    out_spec = pl.BlockSpec((tile, out_cols), lambda i, w: (i, 0))
    return pl.pallas_call(
        kernel,
        grid_spec=pltpu.PrefetchScalarGridSpec(
            num_scalar_prefetch=1,
            grid=(tiles,),
            in_specs=[
                pl.BlockSpec((v.shape[0], tile), lambda i, w: (0, (i // run + w[0]) * run + i if by_rows else i)) for v in lefts
            ]
            + [pl.BlockSpec((v.shape[0], out_cols), lambda i, w: (0, 0 if by_rows else w[0])) for v in rights]
            + ([] if away is None else [out_spec]),
            out_specs=out_spec,
        ),
        out_shape=jax.ShapeDtypeStruct((out_rows, out_cols), BF),
        compiler_params=pltpu.CompilerParams(vmem_limit_bytes=48 * 1024 * 1024),
        cost_estimate=BRIEF,
        name="outer",
    )(which.reshape(1).astype(jnp.int32), *lefts, *rights, *([] if away is None else [away]))


def project(lefts, weight, transposed, types):
    rows, depth = lefts[0].shape
    width = weight.shape[0] if transposed else weight.shape[1]
    tile = min(512, width)
    count = len(lefts)

    def kernel(*refs):
        left, (w,), outs = refs[:count], refs[count : count + 1], refs[count + 1 :]
        for i in range(count):
            result = (mm_t if transposed else mm)(left[i][...], w[...])
            if len(outs) > 1:
                outs[i][...] = result.astype(outs[i].dtype)
            else:
                outs[0][i * rows : (i + 1) * rows, :] = result.astype(outs[0].dtype)

    height = rows * count // len(types)
    return pl.pallas_call(
        kernel,
        grid=(width // tile,),
        in_specs=[pl.BlockSpec((rows, depth), lambda i: (0, 0))] * count
        + [
            pl.BlockSpec((tile, depth), lambda i: (i, 0))
            if transposed
            else pl.BlockSpec((depth, tile), lambda i: (0, i))
        ],
        out_specs=[pl.BlockSpec((height, tile), lambda i: (0, i))] * len(types),
        out_shape=[jax.ShapeDtypeStruct((height, width), t) for t in types],
        compiler_params=pltpu.CompilerParams(vmem_limit_bytes=48 * 1024 * 1024),
        cost_estimate=BRIEF,
        name="project",
    )(*lefts, weight)


def assemble(places, arrays, depth):
    width = arrays[0].shape[1]
    pieces = [(n, start) for n, v in enumerate(arrays) for start in range(0, v.shape[0], depth)]
    count = len(pieces)

    def kernel(places, *refs):
        sources, out, held, arrive, leave = refs[: len(arrays)], *refs[len(arrays) :]
        ins = [
            pltpu.make_async_copy(sources[n].at[pl.ds(start, depth), :], held.at[i], arrive.at[i])
            for i, (n, start) in enumerate(pieces)
        ]
        outs = [pltpu.make_async_copy(held.at[i], out.at[places[i]], leave.at[i]) for i in range(count)]
        for copy in ins:
            copy.start()
        for i in range(count):
            ins[i].wait()
            outs[i].start()
        for copy in outs:
            copy.wait()

    return pl.pallas_call(
        kernel,
        grid_spec=pltpu.PrefetchScalarGridSpec(
            num_scalar_prefetch=1,
            grid=(1,),
            in_specs=[pl.BlockSpec(memory_space=pl.ANY)] * len(arrays),
            out_specs=pl.BlockSpec(memory_space=pl.ANY),
            scratch_shapes=[
                pltpu.VMEM((count, depth, width), arrays[0].dtype),
                pltpu.SemaphoreType.DMA((count,)),
                pltpu.SemaphoreType.DMA((count,)),
            ],
        ),
        out_shape=jax.ShapeDtypeStruct((count, depth, width), arrays[0].dtype),
        compiler_params=pltpu.CompilerParams(vmem_limit_bytes=VMEM_LIMIT),
        cost_estimate=BRIEF,
        name="assemble",
    )(places, *arrays).reshape(count * depth, width)


def take_columns(which, arrays, groups, members):
    depth, width = arrays[0].shape
    part = width // (groups * members)
    kept = len(which)
    if part % HD:
        views = [v.reshape(depth, groups, members, part) for v in arrays]
        return [
            jnp.concatenate(
                [lax.dynamic_slice_in_dim(v, k, 1, 2).reshape(depth, groups * part) for v in views], 1
            )
            for k in which
        ]

    def kernel(which, *refs):
        sources, outs = refs[: len(arrays)], refs[len(arrays) :]
        for k in range(kept):
            for n, source in enumerate(sources):
                for i in range(groups):
                    start = pl.multiple_of(i * members * part + which[k] * part, HD)
                    outs[k][:, (n * groups + i) * part : (n * groups + i + 1) * part] = source[:, pl.ds(start, part)]

    tile = min(64, depth)
    return pl.pallas_call(
        kernel,
        grid_spec=pltpu.PrefetchScalarGridSpec(
            num_scalar_prefetch=1,
            grid=(depth // tile,),
            in_specs=[pl.BlockSpec((tile, width), lambda i, w: (i, 0))] * len(arrays),
            out_specs=[pl.BlockSpec((tile, len(arrays) * groups * part), lambda i, w: (i, 0))] * kept,
        ),
        out_shape=[jax.ShapeDtypeStruct((depth, len(arrays) * groups * part), arrays[0].dtype)] * kept,
        name="take_columns",
    )(jnp.stack(which).astype(jnp.int32), *arrays)


def body(planes, shards, tokens, pairs, valid, teacher, w_query, w_key, w_value, w_out, w_gate, w_up, w_down):
    seqs, slots, blk, width = tokens.shape
    ff = w_gate.shape[1]
    rows = seqs * slots * blk
    world = planes * shards
    near = planes // 2
    all_heads = width // HD
    heads = all_heads // planes
    mine = heads * HD
    own_rows = width // shards
    part_ff = ff // planes
    length = planes * slots * blk
    unit = width // world
    both = ("ctx", "fsdp")

    c, f = lax.axis_index("ctx"), lax.axis_index("fsdp")
    far, low = c // near, c % near
    core, x, y = f % 2, f // 2 % 2, f // 4
    group = x * near + low

    def after(array, *others):
        return lax.optimization_barrier((array, *others))[0]

    def flip(array, bits):
        return lax.ppermute(array, "fsdp", [(i, i ^ bits) for i in range(shards)])

    def flip_ctx(array, bits):
        return lax.ppermute(array, "ctx", [(i, i ^ bits) for i in range(planes)])

    def hop(array, j):
        dx, dz = j // near, j % near
        if dz == 0:
            return flip(array, 2 * dx)
        if dx == 0:
            return flip_ctx(array, dz)
        return lax.ppermute(
            array,
            both,
            [(p * shards + s, (p ^ dz) * shards + (s ^ 2)) for p in range(planes) for s in range(shards)],
        )

    def send(array, homes):
        moved = lax.ppermute(array, both, [(i, to) for i, to in enumerate(homes) if i != to])
        stays = jnp.array([i == to for i, to in enumerate(homes)])[c * shards + f]
        return jnp.where(stays, array, moved)

    def swap(array):
        homes = []
        for p in range(planes):
            for s in range(shards):
                to = (s // 2 % 2) * near + p % near
                homes.append(to * shards + (s - s // 2 % 2 * 2 + p // near * 2))
        return send(array, homes)

    cos, sin = tables(length)
    ranks = jnp.argsort(pairs.reshape(-1))
    owner = ranks // slots
    relative = ((owner // near) ^ x) * near + ((owner % near) ^ low)
    order = (relative * slots + ranks % slots).astype(jnp.int32)

    def over_y(piece):
        return [flip(piece, bits) for bits in range(4, shards, 4)]

    y_bits = list(range(4, shards, 4))

    def put(*items):
        keys = [k for _, own_keys in items for k in own_keys]
        depth = items[0][0].shape[0] // len(items[0][1])
        places = jnp.stack([f ^ k for k in keys]).astype(jnp.int32)
        return assemble(places, [v for v, _ in items], depth)

    def put_pairs(both_x, both_y, other_x, other_y):
        items = [(both_x, [0, 2]), (other_x, [1, 3])]
        for bits, v, w in zip(y_bits, both_y, other_y):
            items += [(v, [bits, bits + 2]), (w, [bits + 1, bits + 3])]
        return put(*items)

    def head_columns(g):
        return jnp.concatenate(
            [lax.dynamic_slice_in_dim(w, g * mine, mine, 1) for w in (w_query, w_key, w_value)], 1
        )

    def ff_rows(g):
        return lax.dynamic_slice_in_dim(w_down, g * (part_ff // shards), part_ff // shards, 0)

    def own_heads(weight):
        sends, spreads = [], {}
        for p in range(planes):
            for s in range(shards):
                q = s // 2
                if q % near == p % near:
                    at = s // 4 * 4 + q // near * 2 + s % 2
                    if at != s:
                        sends.append((p * shards + s, p * shards + at))
                    for d in range(4, shards, 4):
                        spreads.setdefault(d, []).append((p * shards + at, p * shards + (at ^ d)))
        q = f // 2
        stays = (q % near == low) & (f // 4 * 4 + q // near * 2 + core == f)
        first = jnp.where(stays, weight, lax.ppermute(weight, both, sends))

        def rest(first):
            found = first
            for pairs_of in spreads.values():
                found = found + lax.ppermute(first, both, pairs_of)
            return found

        return first, rest

    cut = planes // 2
    early = list(range(1, cut + 1))
    late = [0, *range(cut + 1, planes)]
    early_types = [BF] * cut
    late_types = [F32] + [BF] * (planes - cut - 1)

    def gather_far(found):
        if near != 2:
            return [hop(found[0], j) for j in late[1:]]
        half = rows // 2
        return [hop(found[1][:half], 2), hop(found[2][half:], 1)]

    def joined(found, others):
        return found + (others if near != 2 else [jnp.concatenate(others, 0)])

    def reduce_far(parts):
        if near != 2:
            return [hop(parts[j], j) for j in late[1:]]
        half = rows // 2
        return [hop(parts[3][:half], 2), hop(parts[3][half:], 1)]

    def reduce_near(parts, received):
        if near != 2:
            return add_all(parts[0], received), [hop(parts[j], j) for j in early]
        half = rows // 2
        more = lambda part, other: (part.astype(F32) + other.astype(F32)).astype(BF)
        to_low = jnp.concatenate([more(parts[1][:half], received[0]), parts[1][half:]], 0)
        to_x = jnp.concatenate([parts[2][:half], more(parts[2][half:], received[1])], 0)
        return parts[0], [hop(to_low, 1), hop(to_x, 2)]

    def add_all(total, others):
        for other in others:
            total = total + other.astype(F32)
        return total

    region = lambda *values: lax.optimization_barrier(values)

    gu_own, gu_send = take_columns([group, group ^ near], [w_gate, w_up], shards, planes)
    stream_low = swap(tokens.reshape(rows, width))
    qkv_own = head_columns(group)
    qkv_other = flip(head_columns(group ^ near), 2)
    gu_own_y = over_y(gu_own)
    heads_first, heads_rest = own_heads(w_out)
    stream = stream_low.astype(F32)
    normed_one, inverse_one = normalize(stream)
    qkv_both = jnp.concatenate([qkv_own, qkv_other], 0)
    h1, stream_low, qkv_both, gu_own, gu_own_y, gu_send, heads_first, w_down = region(
        [normed_one.astype(BF)], stream_low, qkv_both, gu_own, gu_own_y, gu_send, heads_first, w_down
    )

    h1 = h1 + [hop(h1[0], j) for j in early]
    qkv_y = over_y(qkv_both)
    qkv_pair = flip(qkv_both, 1)
    found = heads_rest(heads_first)
    h1, qkv_both, qkv_pair, w_down, gu_send = region(h1, qkv_both, qkv_pair, w_down, gu_send)

    others = gather_far(h1)
    down_own = ff_rows(group)
    down_other = flip(ff_rows(group ^ near), 2)
    others, found, down_own, down_other, qkv_y, gu_send, gu_own_y, teacher = region(
        others, found, down_own, down_other, qkv_y, gu_send, gu_own_y, teacher
    )
    h1 = joined(h1, others)

    gu_other = flip(gu_send, 2)
    down_both = jnp.concatenate([down_own, down_other], 0)
    down_y = over_y(down_both)
    other = flip(found, 1)
    qkv_y_pair = [flip(v, 1) for v in qkv_y]
    w_qkv = put_pairs(qkv_both, qkv_y, qkv_pair, qkv_y_pair)
    (qkv,) = project(h1, w_qkv, False, [F32])
    qkv = qkv.reshape(planes, seqs, slots, blk, 3 * mine)
    mixed, lse = attend(order, qkv, cos, sin, heads)
    even = core == 0
    w_out_mine = jnp.concatenate([jnp.where(even, found, other), jnp.where(even, other, found)], 0)
    group_types = [F32] + [BF] * (planes - 1)
    products = project([mixed[s].reshape(rows, mine) for s in range(planes)], w_out_mine, False, group_types)
    products, gu_other, down_both, down_y, gu_own, gu_own_y, teacher = region(
        products, gu_other, down_both, down_y, gu_own, gu_own_y, teacher
    )

    received = reduce_far(products)
    gate_other_y = over_y(gu_other[:, :part_ff])
    down_pair = flip(down_both, 1)
    gu_own_pair = flip(gu_own, 1)
    received, products, down_pair, gu_other, gate_other_y, down_y, gu_own_pair, gu_own_y = region(
        received, products, down_pair, gu_other, gate_other_y, down_y, gu_own_pair, gu_own_y
    )

    own, received = reduce_near(products, received)
    up_other_y = over_y(gu_other[:, part_ff:])
    gu_other_y = [jnp.concatenate(v, 1) for v in zip(gate_other_y, up_other_y)]
    down_y_pair = [flip(v, 1) for v in down_y]
    gu_own_y_pair = [flip(v, 1) for v in gu_own_y]
    residual = stream + add_all(own, received)
    normed_two, inverse_two = normalize(residual)
    h2, gu_other_y, gu_other, down_y_pair, gu_own_y_pair, valid = region(
        [normed_two.astype(BF)], gu_other_y, gu_other, down_y_pair, gu_own_y_pair, valid
    )

    h2 = h2 + [hop(h2[0], j) for j in early]
    gu_other_pair = flip(gu_other, 1)
    gu_items = [(gu_own, [0]), (gu_own_pair, [1]), (gu_other, [2]), (gu_other_pair, [3])]
    for bits, v, w, z in zip(y_bits, gu_own_y, gu_own_y_pair, gu_other_y):
        gu_items += [(v, [bits]), (w, [bits + 1]), (z, [bits + 2]), (flip(z, 1), [bits + 3])]
    down_w = put_pairs(down_both, down_y, down_pair, down_y_pair)
    gu_w = put(*gu_items)
    h2, gu_w, down_w, valid, teacher = region(h2, gu_w, down_w, valid, teacher)

    others = gather_far(h2)
    goal_low = swap(teacher.reshape(rows, width))
    kept, outs = mlp([h2[j] for j in early], gu_w, down_w, early_types, 2, 0)
    outs, kept, others = region(outs, kept, others)
    h2 = joined(h2, others)

    received = [hop(v, j) for v, j in zip(outs, early)]
    (h2_all, gates, ups, hidden_all), outs = mlp(
        [h2[j] for j in late], gu_w, down_w, late_types, 2, 1, kept
    )
    received, outs, h2_all, gates, ups, hidden_all, valid, goal_low = region(
        received, outs, h2_all, gates, ups, hidden_all, valid, goal_low
    )

    received = received + [hop(v, j) for v, j in zip(outs[1:], late[1:])]
    valid_float = swap(valid.reshape(rows, 1)).astype(F32)

    output = residual + add_all(outs[0], received)
    deviation = output - goal_low.astype(F32)
    grad_output = valid_float * deviation
    sums = jnp.stack([jnp.sum(grad_output * deviation), jnp.sum(valid_float)])
    sums0 = jnp.broadcast_to(sums[:, None, None], (2, 8, HD))
    sums0, grad_output, output = region(sums0, grad_output, output)

    sums = sums0
    for j in range(1, planes):
        sums = sums + hop(sums0, j)
    sums = sums + flip_ctx(sums, near)
    low_grad, low_output, sums = region(grad_output.astype(BF), output.astype(BF), sums)

    steps = [1 << b for b in reversed(range(2, shards.bit_length() - 1))]

    def halve(part, axis, bit, move, bits):
        half = part.shape[axis] // 2
        take = lambda k: lax.dynamic_slice_in_dim(part, k * half, half, axis)
        away = move(take(1 - bit), bits)
        return (take(bit).astype(F32) + away.astype(F32)).astype(BF)

    def parts(whole):
        return whole.reshape(2, near, shards // 4, 2, 2, unit, whole.shape[1])

    def across_y(part, axis):
        for step in steps:
            part = halve(part, axis, f // step % 2, flip, step)
        return part

    def across_far(part):
        return halve(part, 0, far, flip_ctx, near)

    def place_rows(part, place):
        homes = []
        for p in range(planes):
            for s in range(shards):
                homes.append(place(s % 2, s // 4, p // near, (s // 2 % 2) * near + p % near))
        return send(part, homes).astype(F32)

    def take(v, k, axis):
        return lax.dynamic_index_in_dim(v, k, axis, keepdims=False)

    def core_away(part):
        return flip(take(part.reshape(near, 2, 2, unit, part.shape[-1]), 1 - core, 2), 1)

    def core_joined(part, away):
        keep = take(part.reshape(near, 2, 2, unit, part.shape[-1]), core, 2)
        even = core == 0
        return jnp.concatenate([jnp.where(even, keep, away), jnp.where(even, away, keep)], -1)

    def column_pieces(part):
        return [take(take(part, x ^ (j // near), 1), low ^ (j % near), 0) for j in range(planes)]

    def columns_placed(pieces):
        places = jnp.stack([group ^ j for j in range(planes)]).astype(jnp.int32)
        return assemble(places, pieces, unit).reshape(planes, unit, -1)

    dm = [low_grad] + [hop(low_grad, j) for j in early]
    for bits in [1, *(1 << b for b in range(2, shards.bit_length() - 1))]:
        sums = sums + flip(sums, bits)
    dm, sums, low_output = region(dm, sums, low_output)

    others = gather_far(dm)
    kept, backs = mlp_back([dm[j] for j in early], gates, ups, gu_w, down_w, early_types, 2, 0)
    backs, kept, others, sums, low_output = region(backs, kept, others, sums, low_output)
    dm = joined(dm, others)

    received = [hop(v, j) for v, j in zip(backs, early)]
    dm_runs = [dm[j] for j in early + late]
    away = flip(outer([hidden_all], dm_runs, 1 - core, True, None, 2), 1)
    (_, dg_all, du_all), backs = mlp_back(
        [dm[j] for j in late], gates, ups, gu_w, down_w, late_types, 2, 1, kept
    )
    g_down = outer([hidden_all], dm_runs, core, True, away, 2)
    received, backs, g_down, dg_all, du_all, h2_all, low_output = region(
        received, backs, g_down, dg_all, du_all, h2_all, low_output
    )

    received = received + [hop(v, j) for v, j in zip(backs[1:], late[1:])]
    activations = swap(low_output)
    g_down = across_y(g_down.reshape(2, shards // 4, part_ff // shards, width), 1)
    gate_half = outer([h2_all], [dg_all], 1 - core, False)
    up_half = outer([h2_all], [du_all], 1 - core, False)
    grad_two = add_all(backs[0], received)
    grad_residual = grad_output + norm_back(grad_two, normed_two, inverse_two)
    dab, gate_half, up_half, g_down, dg_all, du_all, activations = region(
        [grad_residual.astype(BF)], gate_half, up_half, g_down, dg_all, du_all, activations
    )

    dab = dab + [hop(dab[0], j) for j in early]
    gate_away, up_away = flip(gate_half, 1), flip(up_half, 1)
    g_gate = outer([h2_all], [dg_all], core, False, gate_away)
    dab, g_gate, up_away, du_all, g_down = region(dab, g_gate, up_away, du_all, g_down)

    others = gather_far(dab)
    g_gate = across_y(parts(g_gate), 2)
    g_up = outer([h2_all], [du_all], core, False, up_away)
    others, g_up, g_down = region(others, g_up, g_down)
    dab = joined(dab, others)

    up_first, up_second = jnp.split(parts(g_up), 2, -1)
    up_first = across_y(up_first, 2)
    g_down = across_far(g_down)
    (do,) = project(dab, w_out_mine, True, [BF])
    dqkv = attend_back(order, qkv, lse, do.reshape(planes, seqs, slots, blk, mine), cos, sin, heads)
    dqkv = dqkv.reshape(planes * rows, 3 * mine)
    qkv_half = outer(h1, [dqkv], 1 - core, False)
    mixed = mixed.reshape(planes * rows, mine)
    out_half = outer([mixed], dab, 1 - core, True)
    dqkv, qkv_half, out_half, g_gate, g_down, up_first, up_second = region(
        dqkv, qkv_half, out_half, g_gate, g_down, up_first, up_second
    )

    qkv_away, out_away = flip(qkv_half, 1), flip(out_half, 1)
    backs = project([dqkv[i * rows : (i + 1) * rows] for i in range(planes)], w_qkv, True, group_types)
    up_second = across_y(up_second, 2)
    gate_first, gate_second = jnp.split(g_gate, 2, -1)
    gate_first = across_far(gate_first)
    backs, dqkv, qkv_away, out_away, up_second, gate_first, gate_second = region(
        backs, dqkv, qkv_away, out_away, up_second, gate_first, gate_second
    )

    gate_second = across_far(gate_second)
    g_up = jnp.concatenate([up_first, up_second], -1)
    received = reduce_far(backs)
    g_qkv = parts(outer(h1, [dqkv], core, False, qkv_away))
    g_out = outer([mixed], dab, core, True, out_away)
    received, backs, g_qkv, g_out, g_down, gate_first, gate_second, g_up = region(
        received, backs, g_qkv, g_out, g_down, gate_first, gate_second, g_up
    )

    own, received = reduce_near(backs, received)
    g_up = across_far(g_up)
    g_out = across_y(g_out, 0)
    g_gate = jnp.concatenate([gate_first, gate_second], -1)
    g_down = place_rows(
        g_down.reshape(ff // world, width),
        lambda core, y, far, g: far * (shards // 2) * planes + (core * (shards // 4) + y) * planes + g,
    )
    grad_one = add_all(own, received)
    grad_stream = grad_residual + norm_back(grad_one, normed_one, inverse_one)
    low_stream, g_out, g_qkv, g_gate, g_up, g_down = region(
        grad_stream.astype(BF), g_out, g_qkv, g_gate, g_up, g_down
    )

    grad_low = swap(low_stream)
    g_qkv = across_y(g_qkv, 2)
    g_out = across_far(g_out)
    gate_core, up_core = core_away(g_gate), core_away(g_up)
    pieces = [column_pieces(core_joined(v, w)) for v, w in ((g_gate, gate_core), (g_up, up_core))]
    pieces = [jnp.concatenate(v, 1) for v in zip(*pieces)]
    grad_low, g_qkv, g_out, pieces = region(grad_low, g_qkv, g_out, pieces)

    g_qkv = across_far(g_qkv)
    g_out = place_rows(g_out, lambda core, y, far, g: g * shards + (core * (shards // 4) + y) * 2 + far)
    pieces = [hop(v, j) if j else v for j, v in enumerate(pieces)]
    pieces, g_qkv, g_out = region(pieces, g_qkv, g_out)
    qkv_pieces = column_pieces(core_joined(g_qkv, core_away(g_qkv)))
    qkv_pieces, pieces = region(qkv_pieces, pieces)
    qkv_pieces = [hop(v, j) if j else v for j, v in enumerate(qkv_pieces)]
    count = sums[1, 0, 0]
    loss = sums[0, 0, 0] / (count * width)
    factor = (rows * world) / count
    grad_input = grad_low.astype(F32) * factor
    ff_order = lambda v: v.reshape(planes, unit, shards, -1).transpose(1, 2, 0, 3).reshape(unit, ff)
    placed = columns_placed(pieces)
    g_gate = ff_order(placed[:, :, :part_ff]).astype(F32)
    g_up = ff_order(placed[:, :, part_ff:]).astype(F32)
    g_qkv = columns_placed(qkv_pieces).reshape(planes, unit, 3, mine).transpose(2, 1, 0, 3)
    g_qkv = g_qkv.reshape(3, unit, width).astype(F32)
    return (
        activations.reshape(tokens.shape),
        loss,
        grad_input.reshape(tokens.shape),
        g_qkv[0] * factor,
        g_qkv[1] * factor,
        g_qkv[2] * factor,
        g_out * factor,
        g_gate * factor,
        g_up * factor,
        g_down * factor,
    )


def solution(mesh):
    tokens = P("fsdp", "ctx", None, None)
    weight = P("fsdp", None)
    grad = P(("ctx", "fsdp"), None)
    in_specs = (tokens, P(), P("fsdp", "ctx", None), tokens) + (weight,) * 7
    out_specs = (tokens, P(), tokens) + (grad,) * 7
    step = functools.partial(body, mesh.shape["ctx"], mesh.shape["fsdp"])
    return jax.shard_map(step, mesh=mesh, in_specs=in_specs, out_specs=out_specs, check_vma=False)
```

```python
import functools

import jax
import jax.numpy as jnp
from jax import lax
from jax.experimental import pallas as pl
from jax.experimental.pallas import tpu as pltpu
from jax.sharding import PartitionSpec as P

HD = 128
EPS = 1e-05
BF = jnp.bfloat16
F32 = jnp.float32
NEG = -1e30


def normalize(rows):
    centered = rows - jnp.mean(rows, -1, keepdims=True)
    inverse = lax.rsqrt(jnp.mean(centered * centered, -1, keepdims=True) + EPS)
    return centered * inverse, inverse


def norm_back(gradient, normed, inverse):
    centered = gradient - jnp.mean(gradient, -1, keepdims=True)
    return inverse * (centered - normed * jnp.mean(gradient * normed, -1, keepdims=True))


def mm(left, right):
    return jnp.dot(left, right, preferred_element_type=F32)


def mm_t(left, right):
    return lax.dot_general(left, right, (((1,), (1,)), ((), ())), preferred_element_type=F32)


def mm_rows(left, right):
    return lax.dot_general(left, right, (((0,), (0,)), ((), ())), preferred_element_type=F32)


def tables(length):
    frequency = 10000.0 ** (-2.0 * jnp.arange(HD // 2, dtype=F32) / HD)
    phases = jnp.arange(length, dtype=F32)[:, None] * frequency[None, :]
    cosine, sine = jnp.cos(phases), jnp.sin(phases)
    return jnp.concatenate([cosine, cosine], 1), jnp.concatenate([-sine, sine], 1)


def fwd_kernel(heads, order, qkv, cos, sin, out, lse, q_s, k_s, v_s):
    planes, _, slots, blk, _ = qkv.shape
    blocks = planes * slots
    scale = HD ** -0.5

    def head(h, carry):
        col = pl.multiple_of(h * HD, HD)

        def load(b, carry):
            where = order[b]
            s, t = where // slots, where % slots
            row = pl.ds(pl.multiple_of(b * blk, blk), blk)
            c, n = cos[row, :], sin[row, :]
            q = qkv[s, 0, t, :, pl.ds(col, HD)]
            k = qkv[s, 0, t, :, pl.ds(pl.multiple_of(heads * HD + col, HD), HD)]
            q_s[row, :] = ((q * c + pltpu.roll(q, HD // 2, 1) * n) * scale).astype(BF)
            k_s[row, :] = (k * c + pltpu.roll(k, HD // 2, 1) * n).astype(BF)
            v_s[row, :] = qkv[s, 0, t, :, pl.ds(pl.multiple_of(2 * heads * HD + col, HD), HD)].astype(BF)
            return carry

        lax.fori_loop(0, blocks, load, 0)
        for b in range(blocks):
            keys = (b + 1) * blk
            scores = mm_t(q_s[b * blk : keys, :], k_s[0:keys, :])
            top = jnp.max(scores, -1, keepdims=True)
            raised = jnp.exp(scores - top)
            total = jnp.sum(raised, -1, keepdims=True)
            probs = (raised * (1.0 / total)).astype(BF)
            mixed = mm(probs, v_s[0:keys, :])
            where = order[b]
            s, t = where // slots, where % slots
            out[s, 0, t, :, pl.ds(col, HD)] = mixed.astype(BF)
            lse[s, 0, t, :, pl.ds(col, HD)] = jnp.broadcast_to(top + jnp.log(total), (blk, HD))
        return carry

    lax.fori_loop(0, heads, head, 0)


def bwd_kernel(heads, order, qkv, lse, grad, cos, sin, dqkv, q_s, k_s, v_s, g_s, l_s, dk_s, dv_s):
    planes, _, slots, blk, _ = qkv.shape
    blocks = planes * slots
    scale = HD ** -0.5

    def head(h, carry):
        col = pl.multiple_of(h * HD, HD)
        kcol = pl.multiple_of(heads * HD + col, HD)
        vcol = pl.multiple_of(2 * heads * HD + col, HD)

        def load(b, carry):
            where = order[b]
            s, t = where // slots, where % slots
            row = pl.ds(pl.multiple_of(b * blk, blk), blk)
            c, n = cos[row, :], sin[row, :]
            q = qkv[s, 0, t, :, pl.ds(col, HD)]
            k = qkv[s, 0, t, :, pl.ds(kcol, HD)]
            q_s[row, :] = ((q * c + pltpu.roll(q, HD // 2, 1) * n) * scale).astype(BF)
            k_s[row, :] = (k * c + pltpu.roll(k, HD // 2, 1) * n).astype(BF)
            v_s[row, :] = qkv[s, 0, t, :, pl.ds(vcol, HD)].astype(BF)
            g_s[row, :] = grad[s, 0, t, :, pl.ds(col, HD)]
            l_s[row, :] = lse[s, 0, t, :, pl.ds(col, HD)]
            return carry

        lax.fori_loop(0, blocks, load, 0)
        dk_s[...] = jnp.zeros_like(dk_s)
        dv_s[...] = jnp.zeros_like(dv_s)
        for b in range(blocks):
            keys = (b + 1) * blk
            mine = slice(b * blk, keys)
            scores = mm_t(q_s[mine, :], k_s[0:keys, :])
            probs = jnp.exp(scores - l_s[mine, 0:1])
            dprobs = mm_t(g_s[mine, :], v_s[0:keys, :])
            delta = jnp.sum(probs * dprobs, -1, keepdims=True)
            dscores = (probs * (dprobs - delta)).astype(BF)
            dq = mm(dscores, k_s[0:keys, :]) * scale
            dk_s[0:keys, :] += mm_rows(dscores, q_s[mine, :])
            dv_s[0:keys, :] += mm_rows(probs.astype(BF), g_s[mine, :])
            where = order[b]
            s, t = where // slots, where % slots
            dq = dq * cos[mine, :] - pltpu.roll(dq, HD // 2, 1) * sin[mine, :]
            dqkv[s, 0, t, :, pl.ds(col, HD)] = dq.astype(BF)

        def store(b, carry):
            where = order[b]
            s, t = where // slots, where % slots
            row = pl.ds(pl.multiple_of(b * blk, blk), blk)
            dk = dk_s[row, :]
            dk = dk * cos[row, :] - pltpu.roll(dk, HD // 2, 1) * sin[row, :]
            dqkv[s, 0, t, :, pl.ds(kcol, HD)] = dk.astype(BF)
            dqkv[s, 0, t, :, pl.ds(vcol, HD)] = dv_s[row, :].astype(BF)
            return carry

        lax.fori_loop(0, blocks, store, 0)
        return carry

    lax.fori_loop(0, heads, head, 0)


VMEM_LIMIT = 56 * 1024 * 1024
BRIEF = pl.CostEstimate(flops=1024, bytes_accessed=1024, transcendentals=0)


def attend(order, qkv, cos, sin, heads):
    planes, seqs, slots, blk, width = qkv.shape
    length = planes * slots * blk
    spec = lambda w: pl.BlockSpec((planes, 1, slots, blk, w), lambda i, o: (0, i, 0, 0, 0))
    table = pl.BlockSpec((length, HD), lambda i, o: (0, 0))
    return pl.pallas_call(
        functools.partial(fwd_kernel, heads),
        grid_spec=pltpu.PrefetchScalarGridSpec(
            num_scalar_prefetch=1,
            grid=(seqs,),
            in_specs=[spec(width), table, table],
            out_specs=[spec(heads * HD), spec(heads * HD)],
            scratch_shapes=[pltpu.VMEM((length, HD), BF)] * 3,
        ),
        out_shape=[
            jax.ShapeDtypeStruct((planes, seqs, slots, blk, heads * HD), BF),
            jax.ShapeDtypeStruct((planes, seqs, slots, blk, heads * HD), F32),
        ],
        compiler_params=pltpu.CompilerParams(vmem_limit_bytes=VMEM_LIMIT),
        cost_estimate=BRIEF,
        name="attend",
    )(order, qkv, cos, sin)


def attend_back(order, qkv, lse, grad, cos, sin, heads):
    planes, seqs, slots, blk, width = qkv.shape
    length = planes * slots * blk
    spec = lambda w: pl.BlockSpec((planes, 1, slots, blk, w), lambda i, o: (0, i, 0, 0, 0))
    table = pl.BlockSpec((length, HD), lambda i, o: (0, 0))
    return pl.pallas_call(
        functools.partial(bwd_kernel, heads),
        grid_spec=pltpu.PrefetchScalarGridSpec(
            num_scalar_prefetch=1,
            grid=(seqs,),
            in_specs=[spec(width), spec(heads * HD), spec(heads * HD), table, table],
            out_specs=spec(width),
            scratch_shapes=[pltpu.VMEM((length, HD), BF)] * 4 + [pltpu.VMEM((length, HD), F32)] * 3,
        ),
        out_shape=jax.ShapeDtypeStruct((planes, seqs, slots, blk, width), BF),
        compiler_params=pltpu.CompilerParams(vmem_limit_bytes=VMEM_LIMIT),
        cost_estimate=BRIEF,
        name="attend_back",
    )(order, qkv, lse, grad, cos, sin)


TILE = 512


def up_kernel(count, *refs):
    hs, (wg, wu, wd) = refs[:count], refs[count : count + 3]
    refs = refs[count + 3 :]
    refs = refs[4:] if len(refs) > count + 6 else refs
    h_all, g_out, u_out, hidden_out = refs[:4]
    outs, (held, total) = refs[4 : 4 + count], refs[4 + count :]
    step = pl.program_id(0)
    rows = hs[0].shape[0]

    @pl.when(step == 0)
    def _():
        for i in range(count):
            held[i * rows : (i + 1) * rows, :] = hs[i][...]
        h_all[...] = held[...]
        total[...] = jnp.zeros_like(total)

    h = held[...]
    g, u = mm(h, wg[...]), mm(h, wu[...])
    hidden = (g * (1.0 / (1.0 + jnp.exp(-g))) * u).astype(BF)
    g_out[...], u_out[...], hidden_out[...] = g, u, hidden
    total[...] += mm(hidden, wd[...])

    @pl.when(step == pl.num_programs(0) - 1)
    def _():
        for i in range(count):
            outs[i][...] = total[i * rows : (i + 1) * rows, :].astype(outs[i].dtype)


def mlp(hs, gu_w, down_w, types, parts, which, held=None):
    rows, width = hs[0].shape
    part_ff = down_w.shape[0]
    count = len(hs)
    span = rows * count
    depth = TILE if span <= TILE else TILE // 2
    tiles = part_ff // depth
    whole = pl.BlockSpec((rows, width), lambda i: (0, 0))
    tile = pl.BlockSpec((span, depth), lambda i: (which, i))
    kept = [(width, BF), (part_ff, F32), (part_ff, F32), (part_ff, BF)]
    extra = [] if held is None else list(held)
    result = pl.pallas_call(
        functools.partial(up_kernel, count),
        grid=(tiles,),
        in_specs=[whole] * count
        + [
            pl.BlockSpec((width, depth), lambda i: (0, i)),
            pl.BlockSpec((width, depth), lambda i: (0, tiles + i)),
            pl.BlockSpec((depth, width), lambda i: (i, 0)),
        ]
        + [pl.BlockSpec(memory_space=pl.ANY)] * len(extra),
        out_specs=[pl.BlockSpec((span, width), lambda i: (which, 0)), tile, tile, tile] + [whole] * count,
        out_shape=[jax.ShapeDtypeStruct((span * parts, w), t) for w, t in kept]
        + [jax.ShapeDtypeStruct((rows, width), t) for t in types],
        scratch_shapes=[pltpu.VMEM((span, width), BF), pltpu.VMEM((span, width), F32)],
        input_output_aliases={count + 3 + i: i for i in range(len(extra))},
        compiler_params=pltpu.CompilerParams(vmem_limit_bytes=48 * 1024 * 1024),
        cost_estimate=BRIEF,
        name="mlp",
    )(*hs, gu_w, gu_w, down_w, *extra)
    return result[:4], result[4:]


def down_kernel(count, *refs):
    ds, (g_in, u_in, wg, wu, wd) = refs[:count], refs[count : count + 5]
    refs = refs[count + 5 :]
    refs = refs[3:] if len(refs) > count + 5 else refs
    d_all, dg_out, du_out = refs[:3]
    outs, (held, total) = refs[3 : 3 + count], refs[3 + count :]
    step = pl.program_id(0)
    rows = ds[0].shape[0]

    @pl.when(step == 0)
    def _():
        for i in range(count):
            held[i * rows : (i + 1) * rows, :] = ds[i][...]
        d_all[...] = held[...]
        total[...] = jnp.zeros_like(total)

    dh = mm_t(held[...], wd[...])
    g = g_in[...]
    sig = 1.0 / (1.0 + jnp.exp(-g))
    dg = (dh * u_in[...] * sig * (1.0 + g * (1.0 - sig))).astype(BF)
    du = (dh * (g * sig)).astype(BF)
    dg_out[...], du_out[...] = dg, du
    total[...] += mm_t(dg, wg[...]) + mm_t(du, wu[...])

    @pl.when(step == pl.num_programs(0) - 1)
    def _():
        for i in range(count):
            outs[i][...] = total[i * rows : (i + 1) * rows, :].astype(outs[i].dtype)


def mlp_back(ds, g, u, gu_w, down_w, types, parts, which, held=None):
    rows, width = ds[0].shape
    part_ff = down_w.shape[0]
    count = len(ds)
    span = rows * count
    depth = TILE if span <= TILE else TILE // 2
    tiles = part_ff // depth
    whole = pl.BlockSpec((rows, width), lambda i: (0, 0))
    tile = pl.BlockSpec((span, depth), lambda i: (which, i))
    kept = [(width, BF), (part_ff, BF), (part_ff, BF)]
    extra = [] if held is None else list(held)
    result = pl.pallas_call(
        functools.partial(down_kernel, count),
        grid=(tiles,),
        in_specs=[whole] * count
        + [
            tile,
            tile,
            pl.BlockSpec((width, depth), lambda i: (0, i)),
            pl.BlockSpec((width, depth), lambda i: (0, tiles + i)),
            pl.BlockSpec((depth, width), lambda i: (i, 0)),
        ]
        + [pl.BlockSpec(memory_space=pl.ANY)] * len(extra),
        out_specs=[pl.BlockSpec((span, width), lambda i: (which, 0)), tile, tile] + [whole] * count,
        out_shape=[jax.ShapeDtypeStruct((span * parts, w), t) for w, t in kept]
        + [jax.ShapeDtypeStruct((rows, width), t) for t in types],
        scratch_shapes=[pltpu.VMEM((span, width), BF), pltpu.VMEM((span, width), F32)],
        input_output_aliases={count + 5 + i: i for i in range(len(extra))},
        compiler_params=pltpu.CompilerParams(vmem_limit_bytes=48 * 1024 * 1024),
        cost_estimate=BRIEF,
        name="mlp_back",
    )(*ds, g, u, gu_w, gu_w, down_w, *extra)
    return result[:3], result[3:]


def outer(lefts, rights, which, by_rows, away=None, runs=1):
    count = max(len(lefts), len(rights))
    depth = sum(v.shape[0] for v in lefts)
    chunk = depth // count
    out_rows, out_cols = lefts[0].shape[1], rights[0].shape[1]
    out_rows, out_cols = (out_rows // 2, out_cols) if by_rows else (out_rows, out_cols // 2)
    tile = min(TILE, out_rows // runs)
    tiles = out_rows // tile
    run = tiles // runs

    def kernel(which, *refs):
        left, right = refs[: len(lefts)], refs[len(lefts) : len(lefts) + len(rights)]
        take = lambda group, i: group[i][...] if len(group) > 1 else group[0][i * chunk : (i + 1) * chunk, :]
        total = mm_rows(take(left, 0), take(right, 0))
        for i in range(1, count):
            total = total + mm_rows(take(left, i), take(right, i))
        if away is not None:
            total = total + refs[-2][...].astype(F32)
        refs[-1][...] = total.astype(BF)

    out_spec = pl.BlockSpec((tile, out_cols), lambda i, w: (i, 0))
    return pl.pallas_call(
        kernel,
        grid_spec=pltpu.PrefetchScalarGridSpec(
            num_scalar_prefetch=1,
            grid=(tiles,),
            in_specs=[
                pl.BlockSpec((v.shape[0], tile), lambda i, w: (0, (i // run + w[0]) * run + i if by_rows else i)) for v in lefts
            ]
            + [pl.BlockSpec((v.shape[0], out_cols), lambda i, w: (0, 0 if by_rows else w[0])) for v in rights]
            + ([] if away is None else [out_spec]),
            out_specs=out_spec,
        ),
        out_shape=jax.ShapeDtypeStruct((out_rows, out_cols), BF),
        compiler_params=pltpu.CompilerParams(vmem_limit_bytes=48 * 1024 * 1024),
        cost_estimate=BRIEF,
        name="outer",
    )(which.reshape(1).astype(jnp.int32), *lefts, *rights, *([] if away is None else [away]))


def project(lefts, weight, transposed, types):
    rows, depth = lefts[0].shape
    width = weight.shape[0] if transposed else weight.shape[1]
    tile = min(512, width)
    count = len(lefts)

    def kernel(*refs):
        left, (w,), outs = refs[:count], refs[count : count + 1], refs[count + 1 :]
        for i in range(count):
            result = (mm_t if transposed else mm)(left[i][...], w[...])
            if len(outs) > 1:
                outs[i][...] = result.astype(outs[i].dtype)
            else:
                outs[0][i * rows : (i + 1) * rows, :] = result.astype(outs[0].dtype)

    height = rows * count // len(types)
    return pl.pallas_call(
        kernel,
        grid=(width // tile,),
        in_specs=[pl.BlockSpec((rows, depth), lambda i: (0, 0))] * count
        + [
            pl.BlockSpec((tile, depth), lambda i: (i, 0))
            if transposed
            else pl.BlockSpec((depth, tile), lambda i: (0, i))
        ],
        out_specs=[pl.BlockSpec((height, tile), lambda i: (0, i))] * len(types),
        out_shape=[jax.ShapeDtypeStruct((height, width), t) for t in types],
        compiler_params=pltpu.CompilerParams(vmem_limit_bytes=48 * 1024 * 1024),
        cost_estimate=BRIEF,
        name="project",
    )(*lefts, weight)


def assemble(places, arrays, depth):
    width = arrays[0].shape[1]
    pieces = [(n, start) for n, v in enumerate(arrays) for start in range(0, v.shape[0], depth)]
    count = len(pieces)

    def kernel(places, *refs):
        sources, out, held, arrive, leave = refs[: len(arrays)], *refs[len(arrays) :]
        ins = [
            pltpu.make_async_copy(sources[n].at[pl.ds(start, depth), :], held.at[i], arrive.at[i])
            for i, (n, start) in enumerate(pieces)
        ]
        outs = [pltpu.make_async_copy(held.at[i], out.at[places[i]], leave.at[i]) for i in range(count)]
        for copy in ins:
            copy.start()
        for i in range(count):
            ins[i].wait()
            outs[i].start()
        for copy in outs:
            copy.wait()

    return pl.pallas_call(
        kernel,
        grid_spec=pltpu.PrefetchScalarGridSpec(
            num_scalar_prefetch=1,
            grid=(1,),
            in_specs=[pl.BlockSpec(memory_space=pl.ANY)] * len(arrays),
            out_specs=pl.BlockSpec(memory_space=pl.ANY),
            scratch_shapes=[
                pltpu.VMEM((count, depth, width), arrays[0].dtype),
                pltpu.SemaphoreType.DMA((count,)),
                pltpu.SemaphoreType.DMA((count,)),
            ],
        ),
        out_shape=jax.ShapeDtypeStruct((count, depth, width), arrays[0].dtype),
        compiler_params=pltpu.CompilerParams(vmem_limit_bytes=VMEM_LIMIT),
        cost_estimate=BRIEF,
        name="assemble",
    )(places, *arrays).reshape(count * depth, width)


def take_columns(which, arrays, groups, members):
    depth, width = arrays[0].shape
    part = width // (groups * members)
    kept = len(which)
    if part % HD:
        views = [v.reshape(depth, groups, members, part) for v in arrays]
        return [
            jnp.concatenate(
                [lax.dynamic_slice_in_dim(v, k, 1, 2).reshape(depth, groups * part) for v in views], 1
            )
            for k in which
        ]

    def kernel(which, *refs):
        sources, outs = refs[: len(arrays)], refs[len(arrays) :]
        for k in range(kept):
            for n, source in enumerate(sources):
                for i in range(groups):
                    start = pl.multiple_of(i * members * part + which[k] * part, HD)
                    outs[k][:, (n * groups + i) * part : (n * groups + i + 1) * part] = source[:, pl.ds(start, part)]

    tile = min(64, depth)
    return pl.pallas_call(
        kernel,
        grid_spec=pltpu.PrefetchScalarGridSpec(
            num_scalar_prefetch=1,
            grid=(depth // tile,),
            in_specs=[pl.BlockSpec((tile, width), lambda i, w: (i, 0))] * len(arrays),
            out_specs=[pl.BlockSpec((tile, len(arrays) * groups * part), lambda i, w: (i, 0))] * kept,
        ),
        out_shape=[jax.ShapeDtypeStruct((depth, len(arrays) * groups * part), arrays[0].dtype)] * kept,
        name="take_columns",
    )(jnp.stack(which).astype(jnp.int32), *arrays)


def body(planes, shards, tokens, pairs, valid, teacher, w_query, w_key, w_value, w_out, w_gate, w_up, w_down):
    seqs, slots, blk, width = tokens.shape
    ff = w_gate.shape[1]
    rows = seqs * slots * blk
    world = planes * shards
    near = planes // 2
    all_heads = width // HD
    heads = all_heads // planes
    mine = heads * HD
    own_rows = width // shards
    part_ff = ff // planes
    length = planes * slots * blk
    unit = width // world
    both = ("ctx", "fsdp")

    c, f = lax.axis_index("ctx"), lax.axis_index("fsdp")
    far, low = c // near, c % near
    core, x, y = f % 2, f // 2 % 2, f // 4
    group = x * near + low

    def after(array, *others):
        return lax.optimization_barrier((array, *others))[0]

    def flip(array, bits):
        return lax.ppermute(array, "fsdp", [(i, i ^ bits) for i in range(shards)])

    def flip_ctx(array, bits):
        return lax.ppermute(array, "ctx", [(i, i ^ bits) for i in range(planes)])

    def hop(array, j):
        dx, dz = j // near, j % near
        if dz == 0:
            return flip(array, 2 * dx)
        if dx == 0:
            return flip_ctx(array, dz)
        return lax.ppermute(
            array,
            both,
            [(p * shards + s, (p ^ dz) * shards + (s ^ 2)) for p in range(planes) for s in range(shards)],
        )

    def send(array, homes):
        moved = lax.ppermute(array, both, [(i, to) for i, to in enumerate(homes) if i != to])
        stays = jnp.array([i == to for i, to in enumerate(homes)])[c * shards + f]
        return jnp.where(stays, array, moved)

    def swap(array):
        homes = []
        for p in range(planes):
            for s in range(shards):
                to = (s // 2 % 2) * near + p % near
                homes.append(to * shards + (s - s // 2 % 2 * 2 + p // near * 2))
        return send(array, homes)

    cos, sin = tables(length)
    ranks = jnp.argsort(pairs.reshape(-1))
    owner = ranks // slots
    relative = ((owner // near) ^ x) * near + ((owner % near) ^ low)
    order = (relative * slots + ranks % slots).astype(jnp.int32)

    def over_y(piece):
        return [flip(piece, bits) for bits in range(4, shards, 4)]

    y_bits = list(range(4, shards, 4))

    def put(*items):
        keys = [k for _, own_keys in items for k in own_keys]
        depth = items[0][0].shape[0] // len(items[0][1])
        places = jnp.stack([f ^ k for k in keys]).astype(jnp.int32)
        return assemble(places, [v for v, _ in items], depth)

    def put_pairs(both_x, both_y, other_x, other_y):
        items = [(both_x, [0, 2]), (other_x, [1, 3])]
        for bits, v, w in zip(y_bits, both_y, other_y):
            items += [(v, [bits, bits + 2]), (w, [bits + 1, bits + 3])]
        return put(*items)

    def head_columns(g):
        return jnp.concatenate(
            [lax.dynamic_slice_in_dim(w, g * mine, mine, 1) for w in (w_query, w_key, w_value)], 1
        )

    def ff_rows(g):
        return lax.dynamic_slice_in_dim(w_down, g * (part_ff // shards), part_ff // shards, 0)

    def own_heads(weight):
        sends, spreads = [], {}
        for p in range(planes):
            for s in range(shards):
                q = s // 2
                if q % near == p % near:
                    at = s // 4 * 4 + q // near * 2 + s % 2
                    if at != s:
                        sends.append((p * shards + s, p * shards + at))
                    for d in range(4, shards, 4):
                        spreads.setdefault(d, []).append((p * shards + at, p * shards + (at ^ d)))
        q = f // 2
        stays = (q % near == low) & (f // 4 * 4 + q // near * 2 + core == f)
        first = jnp.where(stays, weight, lax.ppermute(weight, both, sends))

        def rest(first):
            found = first
            for pairs_of in spreads.values():
                found = found + lax.ppermute(first, both, pairs_of)
            return found

        return first, rest

    cut = planes // 2
    early = list(range(1, cut + 1))
    late = [0, *range(cut + 1, planes)]
    early_types = [BF] * cut
    late_types = [F32] + [BF] * (planes - cut - 1)

    def gather_far(found):
        if near != 2:
            return [hop(found[0], j) for j in late[1:]]
        half = rows // 2
        return [hop(found[1][:half], 2), hop(found[2][half:], 1)]

    def joined(found, others):
        return found + (others if near != 2 else [jnp.concatenate(others, 0)])

    def reduce_far(parts):
        if near != 2:
            return [hop(parts[j], j) for j in late[1:]]
        half = rows // 2
        return [hop(parts[3][:half], 2), hop(parts[3][half:], 1)]

    def reduce_near(parts, received):
        if near != 2:
            return add_all(parts[0], received), [hop(parts[j], j) for j in early]
        half = rows // 2
        more = lambda part, other: (part.astype(F32) + other.astype(F32)).astype(BF)
        to_low = jnp.concatenate([more(parts[1][:half], received[0]), parts[1][half:]], 0)
        to_x = jnp.concatenate([parts[2][:half], more(parts[2][half:], received[1])], 0)
        return parts[0], [hop(to_low, 1), hop(to_x, 2)]

    def add_all(total, others):
        for other in others:
            total = total + other.astype(F32)
        return total

    region = lambda *values: lax.optimization_barrier(values)

    gate_own, gate_send = take_columns([group, group ^ near], [w_gate], shards, planes)
    gate_own_y = over_y(gate_own)
    up_own, up_send = take_columns([group, group ^ near], [w_up], shards, planes)
    up_own_y = over_y(up_own)
    stream_low = swap(tokens.reshape(rows, width))
    qkv_own = head_columns(group)
    qkv_other = flip(head_columns(group ^ near), 2)
    heads_first, heads_rest = own_heads(w_out)
    stream = stream_low.astype(F32)
    normed_one, inverse_one = normalize(stream)
    qkv_both = jnp.concatenate([qkv_own, qkv_other], 0)
    gate_parts, up_parts = [gate_own, gate_send, *gate_own_y], [up_own, up_send, *up_own_y]
    h1, stream_low, qkv_both, gate_parts, up_parts, heads_first, w_down = region(
        [normed_one.astype(BF)], stream_low, qkv_both, gate_parts, up_parts, heads_first, w_down
    )
    gu_own, gu_send, *gu_own_y = [jnp.concatenate(v, 1) for v in zip(gate_parts, up_parts)]

    h1 = h1 + [hop(h1[0], j) for j in early]
    qkv_y = over_y(qkv_both)
    qkv_pair = flip(qkv_both, 1)
    found = heads_rest(heads_first)
    h1, qkv_both, qkv_pair, w_down, gu_send = region(h1, qkv_both, qkv_pair, w_down, gu_send)

    others = gather_far(h1)
    down_own = ff_rows(group)
    down_other = flip(ff_rows(group ^ near), 2)
    others, found, down_own, down_other, qkv_y, gu_send, gu_own_y, teacher = region(
        others, found, down_own, down_other, qkv_y, gu_send, gu_own_y, teacher
    )
    h1 = joined(h1, others)

    gu_other = flip(gu_send, 2)
    down_both = jnp.concatenate([down_own, down_other], 0)
    down_y = over_y(down_both)
    other = flip(found, 1)
    qkv_y_pair = [flip(v, 1) for v in qkv_y]
    w_qkv = put_pairs(qkv_both, qkv_y, qkv_pair, qkv_y_pair)
    (qkv,) = project(h1, w_qkv, False, [F32])
    qkv = qkv.reshape(planes, seqs, slots, blk, 3 * mine)
    mixed, lse = attend(order, qkv, cos, sin, heads)
    even = core == 0
    w_out_mine = jnp.concatenate([jnp.where(even, found, other), jnp.where(even, other, found)], 0)
    group_types = [F32] + [BF] * (planes - 1)
    products = project([mixed[s].reshape(rows, mine) for s in range(planes)], w_out_mine, False, group_types)
    products, gu_other, down_both, down_y, gu_own, gu_own_y, teacher = region(
        products, gu_other, down_both, down_y, gu_own, gu_own_y, teacher
    )

    received = reduce_far(products)
    gate_other_y = over_y(gu_other[:, :part_ff])
    down_pair = flip(down_both, 1)
    gu_own_pair = flip(gu_own, 1)
    received, products, down_pair, gu_other, gate_other_y, down_y, gu_own_pair, gu_own_y = region(
        received, products, down_pair, gu_other, gate_other_y, down_y, gu_own_pair, gu_own_y
    )

    own, received = reduce_near(products, received)
    up_other_y = over_y(gu_other[:, part_ff:])
    gu_other_y = [jnp.concatenate(v, 1) for v in zip(gate_other_y, up_other_y)]
    down_y_pair = [flip(v, 1) for v in down_y]
    gu_own_y_pair = [flip(v, 1) for v in gu_own_y]
    residual = stream + add_all(own, received)
    normed_two, inverse_two = normalize(residual)
    h2, gu_other_y, gu_other, down_y_pair, gu_own_y_pair, valid = region(
        [normed_two.astype(BF)], gu_other_y, gu_other, down_y_pair, gu_own_y_pair, valid
    )

    h2 = h2 + [hop(h2[0], j) for j in early]
    gu_other_pair = flip(gu_other, 1)
    gu_items = [(gu_own, [0]), (gu_own_pair, [1]), (gu_other, [2]), (gu_other_pair, [3])]
    for bits, v, w, z in zip(y_bits, gu_own_y, gu_own_y_pair, gu_other_y):
        gu_items += [(v, [bits]), (w, [bits + 1]), (z, [bits + 2]), (flip(z, 1), [bits + 3])]
    down_w = put_pairs(down_both, down_y, down_pair, down_y_pair)
    gu_w = put(*gu_items)
    h2, gu_w, down_w, valid, teacher = region(h2, gu_w, down_w, valid, teacher)

    others = gather_far(h2)
    goal_low = swap(teacher.reshape(rows, width))
    kept, outs = mlp([h2[j] for j in early], gu_w, down_w, early_types, 2, 0)
    outs, kept, others = region(outs, kept, others)
    h2 = joined(h2, others)

    received = [hop(v, j) for v, j in zip(outs, early)]
    (h2_all, gates, ups, hidden_all), outs = mlp(
        [h2[j] for j in late], gu_w, down_w, late_types, 2, 1, kept
    )
    received, outs, h2_all, gates, ups, hidden_all, valid, goal_low = region(
        received, outs, h2_all, gates, ups, hidden_all, valid, goal_low
    )

    received = received + [hop(v, j) for v, j in zip(outs[1:], late[1:])]
    valid_float = swap(valid.reshape(rows, 1)).astype(F32)

    output = residual + add_all(outs[0], received)
    deviation = output - goal_low.astype(F32)
    grad_output = valid_float * deviation
    sums = jnp.stack([jnp.sum(grad_output * deviation), jnp.sum(valid_float)])
    sums0 = jnp.broadcast_to(sums[:, None, None], (2, 8, HD))
    sums0, grad_output, output = region(sums0, grad_output, output)

    sums = sums0
    for bits in range(1, planes):
        sums = sums + flip_ctx(sums0, bits)
    low_grad, low_output, sums = region(grad_output.astype(BF), output.astype(BF), sums)

    steps = [1 << b for b in reversed(range(2, shards.bit_length() - 1))]

    def halve(part, axis, bit, move, bits):
        half = part.shape[axis] // 2
        take = lambda k: lax.dynamic_slice_in_dim(part, k * half, half, axis)
        away = move(take(1 - bit), bits)
        return (take(bit).astype(F32) + away.astype(F32)).astype(BF)

    def parts(whole):
        return whole.reshape(2, near, shards // 4, 2, 2, unit, whole.shape[1])

    def across_y(part, axis):
        for step in steps:
            part = halve(part, axis, f // step % 2, flip, step)
        return part

    def across_far(part):
        return halve(part, 0, far, flip_ctx, near)

    def place_rows(part, place):
        homes = []
        for p in range(planes):
            for s in range(shards):
                homes.append(place(s % 2, s // 4, p // near, (s // 2 % 2) * near + p % near))
        return send(part, homes).astype(F32)

    def take(v, k, axis):
        return lax.dynamic_index_in_dim(v, k, axis, keepdims=False)

    def core_away(part):
        return flip(take(part.reshape(near, 2, 2, unit, part.shape[-1]), 1 - core, 2), 1)

    def core_joined(part, away):
        keep = take(part.reshape(near, 2, 2, unit, part.shape[-1]), core, 2)
        even = core == 0
        return jnp.concatenate([jnp.where(even, keep, away), jnp.where(even, away, keep)], -1)

    def column_pieces(part):
        return [take(take(part, x ^ (j // near), 1), low ^ (j % near), 0) for j in range(planes)]

    def columns_placed(pieces):
        places = jnp.stack([group ^ j for j in range(planes)]).astype(jnp.int32)
        return assemble(places, pieces, unit).reshape(planes, unit, -1)

    dm = [low_grad] + [hop(low_grad, j) for j in early]
    for bits in [1, *(1 << b for b in range(2, shards.bit_length() - 1))]:
        sums = sums + flip(sums, bits)
    dm, sums, low_output = region(dm, sums, low_output)

    others = gather_far(dm)
    kept, backs = mlp_back([dm[j] for j in early], gates, ups, gu_w, down_w, early_types, 2, 0)
    backs, kept, others, sums, low_output = region(backs, kept, others, sums, low_output)
    dm = joined(dm, others)

    received = [hop(v, j) for v, j in zip(backs, early)]
    dm_runs = [dm[j] for j in early + late]
    away = flip(outer([hidden_all], dm_runs, 1 - core, True, None, 2), 1)
    (_, dg_all, du_all), backs = mlp_back(
        [dm[j] for j in late], gates, ups, gu_w, down_w, late_types, 2, 1, kept
    )
    g_down = outer([hidden_all], dm_runs, core, True, away, 2)
    received, backs, g_down, dg_all, du_all, h2_all, low_output = region(
        received, backs, g_down, dg_all, du_all, h2_all, low_output
    )

    received = received + [hop(v, j) for v, j in zip(backs[1:], late[1:])]
    activations = swap(low_output)
    g_down = across_y(g_down.reshape(2, shards // 4, part_ff // shards, width), 1)
    gate_half = outer([h2_all], [dg_all], 1 - core, False)
    up_half = outer([h2_all], [du_all], 1 - core, False)
    grad_two = add_all(backs[0], received)
    grad_residual = grad_output + norm_back(grad_two, normed_two, inverse_two)
    dab, gate_half, up_half, g_down, dg_all, du_all, activations = region(
        [grad_residual.astype(BF)], gate_half, up_half, g_down, dg_all, du_all, activations
    )

    dab = dab + [hop(dab[0], j) for j in early]
    gate_away, up_away = flip(gate_half, 1), flip(up_half, 1)
    g_gate = outer([h2_all], [dg_all], core, False, gate_away)
    dab, g_gate, up_away, du_all, g_down = region(dab, g_gate, up_away, du_all, g_down)

    others = gather_far(dab)
    g_gate = across_y(parts(g_gate), 2)
    g_up = outer([h2_all], [du_all], core, False, up_away)
    others, g_up, g_down = region(others, g_up, g_down)
    dab = joined(dab, others)

    up_first, up_second = jnp.split(parts(g_up), 2, -1)
    up_first = across_y(up_first, 2)
    g_down = across_far(g_down)
    (do,) = project(dab, w_out_mine, True, [BF])
    dqkv = attend_back(order, qkv, lse, do.reshape(planes, seqs, slots, blk, mine), cos, sin, heads)
    dqkv = dqkv.reshape(planes * rows, 3 * mine)
    qkv_half = outer(h1, [dqkv], 1 - core, False)
    mixed = mixed.reshape(planes * rows, mine)
    out_half = outer([mixed], dab, 1 - core, True)
    dqkv, qkv_half, out_half, g_gate, g_down, up_first, up_second, sums = region(
        dqkv, qkv_half, out_half, g_gate, g_down, up_first, up_second, sums
    )

    qkv_away, out_away = flip(qkv_half, 1), flip(out_half, 1)
    backs = project([dqkv[i * rows : (i + 1) * rows] for i in range(planes)], w_qkv, True, group_types)
    up_second = across_y(up_second, 2)
    sums = sums + flip(sums, 2)
    gate_first, gate_second = jnp.split(g_gate, 2, -1)
    gate_first = across_far(gate_first)
    backs, dqkv, qkv_away, out_away, up_second, gate_first, gate_second, sums = region(
        backs, dqkv, qkv_away, out_away, up_second, gate_first, gate_second, sums
    )

    gate_second = across_far(gate_second)
    g_up = jnp.concatenate([up_first, up_second], -1)
    received = reduce_far(backs)
    g_qkv = parts(outer(h1, [dqkv], core, False, qkv_away))
    g_out = outer([mixed], dab, core, True, out_away)
    received, backs, g_qkv, g_out, g_down, gate_first, gate_second, g_up = region(
        received, backs, g_qkv, g_out, g_down, gate_first, gate_second, g_up
    )

    own, received = reduce_near(backs, received)
    g_up = across_far(g_up)
    g_out = across_y(g_out, 0)
    g_gate = jnp.concatenate([gate_first, gate_second], -1)
    g_down = place_rows(
        g_down.reshape(ff // world, width),
        lambda core, y, far, g: far * (shards // 2) * planes + (core * (shards // 4) + y) * planes + g,
    )
    grad_one = add_all(own, received)
    grad_stream = grad_residual + norm_back(grad_one, normed_one, inverse_one)
    low_stream, g_out, g_qkv, g_gate, g_up, g_down = region(
        grad_stream.astype(BF), g_out, g_qkv, g_gate, g_up, g_down
    )

    grad_low = swap(low_stream)
    g_qkv = across_y(g_qkv, 2)
    g_out = across_far(g_out)
    gate_core, up_core = core_away(g_gate), core_away(g_up)
    pieces = [column_pieces(core_joined(v, w)) for v, w in ((g_gate, gate_core), (g_up, up_core))]
    pieces = [jnp.concatenate(v, 1) for v in zip(*pieces)]
    grad_low, g_qkv, g_out, pieces = region(grad_low, g_qkv, g_out, pieces)

    g_qkv = across_far(g_qkv)
    g_out = place_rows(g_out, lambda core, y, far, g: g * shards + (core * (shards // 4) + y) * 2 + far)
    pieces = [hop(v, j) if j else v for j, v in enumerate(pieces)]
    pieces, g_qkv, g_out = region(pieces, g_qkv, g_out)
    qkv_pieces = column_pieces(core_joined(g_qkv, core_away(g_qkv)))
    qkv_pieces, pieces = region(qkv_pieces, pieces)
    qkv_pieces = [hop(v, j) if j else v for j, v in enumerate(qkv_pieces)]
    count = sums[1, 0, 0]
    loss = sums[0, 0, 0] / (count * width)
    factor = (rows * world) / count
    grad_input = grad_low.astype(F32) * factor
    ff_order = lambda v: v.reshape(planes, unit, shards, -1).transpose(1, 2, 0, 3).reshape(unit, ff)
    placed = columns_placed(pieces)
    g_gate = ff_order(placed[:, :, :part_ff]).astype(F32)
    g_up = ff_order(placed[:, :, part_ff:]).astype(F32)
    g_qkv = columns_placed(qkv_pieces).reshape(planes, unit, 3, mine).transpose(2, 1, 0, 3)
    g_qkv = g_qkv.reshape(3, unit, width).astype(F32)
    return (
        activations.reshape(tokens.shape),
        loss,
        grad_input.reshape(tokens.shape),
        g_qkv[0] * factor,
        g_qkv[1] * factor,
        g_qkv[2] * factor,
        g_out * factor,
        g_gate * factor,
        g_up * factor,
        g_down * factor,
    )


def solution(mesh):
    tokens = P("fsdp", "ctx", None, None)
    weight = P("fsdp", None)
    grad = P(("ctx", "fsdp"), None)
    in_specs = (tokens, P(), P("fsdp", "ctx", None), tokens) + (weight,) * 7
    out_specs = (tokens, P(), tokens) + (grad,) * 7
    step = functools.partial(body, mesh.shape["ctx"], mesh.shape["fsdp"])
    return jax.shard_map(step, mesh=mesh, in_specs=in_specs, out_specs=out_specs, check_vma=False)
```

```python
import functools

import jax
import jax.numpy as jnp
from jax import lax
from jax.experimental import pallas as pl
from jax.experimental.pallas import tpu as pltpu
from jax.sharding import PartitionSpec as P

HD = 128
EPS = 1e-05
BF = jnp.bfloat16
F32 = jnp.float32
NEG = -1e30


def normalize(rows):
    centered = rows - jnp.mean(rows, -1, keepdims=True)
    inverse = lax.rsqrt(jnp.mean(centered * centered, -1, keepdims=True) + EPS)
    return centered * inverse, inverse


def norm_back(gradient, normed, inverse):
    centered = gradient - jnp.mean(gradient, -1, keepdims=True)
    return inverse * (centered - normed * jnp.mean(gradient * normed, -1, keepdims=True))


def mm(left, right):
    return jnp.dot(left, right, preferred_element_type=F32)


def mm_t(left, right):
    return lax.dot_general(left, right, (((1,), (1,)), ((), ())), preferred_element_type=F32)


def mm_rows(left, right):
    return lax.dot_general(left, right, (((0,), (0,)), ((), ())), preferred_element_type=F32)


def tables(length):
    frequency = 10000.0 ** (-2.0 * jnp.arange(HD // 2, dtype=F32) / HD)
    phases = jnp.arange(length, dtype=F32)[:, None] * frequency[None, :]
    cosine, sine = jnp.cos(phases), jnp.sin(phases)
    return jnp.concatenate([cosine, cosine], 1), jnp.concatenate([-sine, sine], 1)


def fwd_kernel(heads, order, qkv, cos, sin, out, lse, q_s, k_s, v_s):
    planes, _, slots, blk, _ = qkv.shape
    blocks = planes * slots
    scale = HD ** -0.5

    def head(h, carry):
        col = pl.multiple_of(h * HD, HD)

        def load(b, carry):
            where = order[b]
            s, t = where // slots, where % slots
            row = pl.ds(pl.multiple_of(b * blk, blk), blk)
            c, n = cos[row, :], sin[row, :]
            q = qkv[s, 0, t, :, pl.ds(col, HD)]
            k = qkv[s, 0, t, :, pl.ds(pl.multiple_of(heads * HD + col, HD), HD)]
            q_s[row, :] = ((q * c + pltpu.roll(q, HD // 2, 1) * n) * scale).astype(BF)
            k_s[row, :] = (k * c + pltpu.roll(k, HD // 2, 1) * n).astype(BF)
            v_s[row, :] = qkv[s, 0, t, :, pl.ds(pl.multiple_of(2 * heads * HD + col, HD), HD)].astype(BF)
            return carry

        lax.fori_loop(0, blocks, load, 0)
        for b in range(blocks):
            keys = (b + 1) * blk
            scores = mm_t(q_s[b * blk : keys, :], k_s[0:keys, :])
            top = jnp.max(scores, -1, keepdims=True)
            raised = jnp.exp(scores - top)
            total = jnp.sum(raised, -1, keepdims=True)
            probs = (raised * (1.0 / total)).astype(BF)
            mixed = mm(probs, v_s[0:keys, :])
            where = order[b]
            s, t = where // slots, where % slots
            out[s, 0, t, :, pl.ds(col, HD)] = mixed.astype(BF)
            lse[s, 0, t, :, pl.ds(col, HD)] = jnp.broadcast_to(top + jnp.log(total), (blk, HD))
        return carry

    lax.fori_loop(0, heads, head, 0)


def bwd_kernel(heads, order, qkv, lse, grad, cos, sin, dqkv, q_s, k_s, v_s, g_s, l_s, dk_s, dv_s):
    planes, _, slots, blk, _ = qkv.shape
    blocks = planes * slots
    scale = HD ** -0.5

    def head(h, carry):
        col = pl.multiple_of(h * HD, HD)
        kcol = pl.multiple_of(heads * HD + col, HD)
        vcol = pl.multiple_of(2 * heads * HD + col, HD)

        def load(b, carry):
            where = order[b]
            s, t = where // slots, where % slots
            row = pl.ds(pl.multiple_of(b * blk, blk), blk)
            c, n = cos[row, :], sin[row, :]
            q = qkv[s, 0, t, :, pl.ds(col, HD)]
            k = qkv[s, 0, t, :, pl.ds(kcol, HD)]
            q_s[row, :] = ((q * c + pltpu.roll(q, HD // 2, 1) * n) * scale).astype(BF)
            k_s[row, :] = (k * c + pltpu.roll(k, HD // 2, 1) * n).astype(BF)
            v_s[row, :] = qkv[s, 0, t, :, pl.ds(vcol, HD)].astype(BF)
            g_s[row, :] = grad[s, 0, t, :, pl.ds(col, HD)]
            l_s[row, :] = lse[s, 0, t, :, pl.ds(col, HD)]
            return carry

        lax.fori_loop(0, blocks, load, 0)
        dk_s[...] = jnp.zeros_like(dk_s)
        dv_s[...] = jnp.zeros_like(dv_s)
        for b in range(blocks):
            keys = (b + 1) * blk
            mine = slice(b * blk, keys)
            scores = mm_t(q_s[mine, :], k_s[0:keys, :])
            probs = jnp.exp(scores - l_s[mine, 0:1])
            dprobs = mm_t(g_s[mine, :], v_s[0:keys, :])
            delta = jnp.sum(probs * dprobs, -1, keepdims=True)
            dscores = (probs * (dprobs - delta)).astype(BF)
            dq = mm(dscores, k_s[0:keys, :]) * scale
            dk_s[0:keys, :] += mm_rows(dscores, q_s[mine, :])
            dv_s[0:keys, :] += mm_rows(probs.astype(BF), g_s[mine, :])
            where = order[b]
            s, t = where // slots, where % slots
            dq = dq * cos[mine, :] - pltpu.roll(dq, HD // 2, 1) * sin[mine, :]
            dqkv[s, 0, t, :, pl.ds(col, HD)] = dq.astype(BF)

        def store(b, carry):
            where = order[b]
            s, t = where // slots, where % slots
            row = pl.ds(pl.multiple_of(b * blk, blk), blk)
            dk = dk_s[row, :]
            dk = dk * cos[row, :] - pltpu.roll(dk, HD // 2, 1) * sin[row, :]
            dqkv[s, 0, t, :, pl.ds(kcol, HD)] = dk.astype(BF)
            dqkv[s, 0, t, :, pl.ds(vcol, HD)] = dv_s[row, :].astype(BF)
            return carry

        lax.fori_loop(0, blocks, store, 0)
        return carry

    lax.fori_loop(0, heads, head, 0)


VMEM_LIMIT = 56 * 1024 * 1024
BRIEF = pl.CostEstimate(flops=1024, bytes_accessed=1024, transcendentals=0)


def attend(order, qkv, cos, sin, heads):
    planes, seqs, slots, blk, width = qkv.shape
    length = planes * slots * blk
    spec = lambda w: pl.BlockSpec((planes, 1, slots, blk, w), lambda i, o: (0, i, 0, 0, 0))
    table = pl.BlockSpec((length, HD), lambda i, o: (0, 0))
    return pl.pallas_call(
        functools.partial(fwd_kernel, heads),
        grid_spec=pltpu.PrefetchScalarGridSpec(
            num_scalar_prefetch=1,
            grid=(seqs,),
            in_specs=[spec(width), table, table],
            out_specs=[spec(heads * HD), spec(heads * HD)],
            scratch_shapes=[pltpu.VMEM((length, HD), BF)] * 3,
        ),
        out_shape=[
            jax.ShapeDtypeStruct((planes, seqs, slots, blk, heads * HD), BF),
            jax.ShapeDtypeStruct((planes, seqs, slots, blk, heads * HD), F32),
        ],
        compiler_params=pltpu.CompilerParams(vmem_limit_bytes=VMEM_LIMIT),
        cost_estimate=BRIEF,
        name="attend",
    )(order, qkv, cos, sin)


def attend_back(order, qkv, lse, grad, cos, sin, heads):
    planes, seqs, slots, blk, width = qkv.shape
    length = planes * slots * blk
    spec = lambda w: pl.BlockSpec((planes, 1, slots, blk, w), lambda i, o: (0, i, 0, 0, 0))
    table = pl.BlockSpec((length, HD), lambda i, o: (0, 0))
    return pl.pallas_call(
        functools.partial(bwd_kernel, heads),
        grid_spec=pltpu.PrefetchScalarGridSpec(
            num_scalar_prefetch=1,
            grid=(seqs,),
            in_specs=[spec(width), spec(heads * HD), spec(heads * HD), table, table],
            out_specs=spec(width),
            scratch_shapes=[pltpu.VMEM((length, HD), BF)] * 4 + [pltpu.VMEM((length, HD), F32)] * 3,
        ),
        out_shape=jax.ShapeDtypeStruct((planes, seqs, slots, blk, width), BF),
        compiler_params=pltpu.CompilerParams(vmem_limit_bytes=VMEM_LIMIT),
        cost_estimate=BRIEF,
        name="attend_back",
    )(order, qkv, lse, grad, cos, sin)


TILE = 512


def up_kernel(count, *refs):
    hs, (wg, wu, wd) = refs[:count], refs[count : count + 3]
    refs = refs[count + 3 :]
    refs = refs[4:] if len(refs) > count + 6 else refs
    h_all, g_out, u_out, hidden_out = refs[:4]
    outs, (held, total) = refs[4 : 4 + count], refs[4 + count :]
    step = pl.program_id(0)
    rows = hs[0].shape[0]

    @pl.when(step == 0)
    def _():
        for i in range(count):
            held[i * rows : (i + 1) * rows, :] = hs[i][...]
        h_all[...] = held[...]
        total[...] = jnp.zeros_like(total)

    h = held[...]
    g, u = mm(h, wg[...]), mm(h, wu[...])
    hidden = (g * (1.0 / (1.0 + jnp.exp(-g))) * u).astype(BF)
    g_out[...], u_out[...], hidden_out[...] = g, u, hidden
    total[...] += mm(hidden, wd[...])

    @pl.when(step == pl.num_programs(0) - 1)
    def _():
        for i in range(count):
            outs[i][...] = total[i * rows : (i + 1) * rows, :].astype(outs[i].dtype)


def mlp(hs, gu_w, down_w, types, parts, which, held=None):
    rows, width = hs[0].shape
    part_ff = down_w.shape[0]
    count = len(hs)
    span = rows * count
    depth = TILE if span <= TILE else TILE // 2
    tiles = part_ff // depth
    whole = pl.BlockSpec((rows, width), lambda i: (0, 0))
    tile = pl.BlockSpec((span, depth), lambda i: (which, i))
    kept = [(width, BF), (part_ff, F32), (part_ff, F32), (part_ff, BF)]
    extra = [] if held is None else list(held)
    result = pl.pallas_call(
        functools.partial(up_kernel, count),
        grid=(tiles,),
        in_specs=[whole] * count
        + [
            pl.BlockSpec((width, depth), lambda i: (0, i)),
            pl.BlockSpec((width, depth), lambda i: (0, tiles + i)),
            pl.BlockSpec((depth, width), lambda i: (i, 0)),
        ]
        + [pl.BlockSpec(memory_space=pl.ANY)] * len(extra),
        out_specs=[pl.BlockSpec((span, width), lambda i: (which, 0)), tile, tile, tile] + [whole] * count,
        out_shape=[jax.ShapeDtypeStruct((span * parts, w), t) for w, t in kept]
        + [jax.ShapeDtypeStruct((rows, width), t) for t in types],
        scratch_shapes=[pltpu.VMEM((span, width), BF), pltpu.VMEM((span, width), F32)],
        input_output_aliases={count + 3 + i: i for i in range(len(extra))},
        compiler_params=pltpu.CompilerParams(vmem_limit_bytes=48 * 1024 * 1024),
        cost_estimate=BRIEF,
        name="mlp",
    )(*hs, gu_w, gu_w, down_w, *extra)
    return result[:4], result[4:]


def down_kernel(count, *refs):
    ds, (g_in, u_in, wg, wu, wd) = refs[:count], refs[count : count + 5]
    refs = refs[count + 5 :]
    refs = refs[3:] if len(refs) > count + 5 else refs
    d_all, dg_out, du_out = refs[:3]
    outs, (held, total) = refs[3 : 3 + count], refs[3 + count :]
    step = pl.program_id(0)
    rows = ds[0].shape[0]

    @pl.when(step == 0)
    def _():
        for i in range(count):
            held[i * rows : (i + 1) * rows, :] = ds[i][...]
        d_all[...] = held[...]
        total[...] = jnp.zeros_like(total)

    dh = mm_t(held[...], wd[...])
    g = g_in[...]
    sig = 1.0 / (1.0 + jnp.exp(-g))
    dg = (dh * u_in[...] * sig * (1.0 + g * (1.0 - sig))).astype(BF)
    du = (dh * (g * sig)).astype(BF)
    dg_out[...], du_out[...] = dg, du
    total[...] += mm_t(dg, wg[...]) + mm_t(du, wu[...])

    @pl.when(step == pl.num_programs(0) - 1)
    def _():
        for i in range(count):
            outs[i][...] = total[i * rows : (i + 1) * rows, :].astype(outs[i].dtype)


def mlp_back(ds, g, u, gu_w, down_w, types, parts, which, held=None):
    rows, width = ds[0].shape
    part_ff = down_w.shape[0]
    count = len(ds)
    span = rows * count
    depth = TILE if span <= TILE else TILE // 2
    tiles = part_ff // depth
    whole = pl.BlockSpec((rows, width), lambda i: (0, 0))
    tile = pl.BlockSpec((span, depth), lambda i: (which, i))
    kept = [(width, BF), (part_ff, BF), (part_ff, BF)]
    extra = [] if held is None else list(held)
    result = pl.pallas_call(
        functools.partial(down_kernel, count),
        grid=(tiles,),
        in_specs=[whole] * count
        + [
            tile,
            tile,
            pl.BlockSpec((width, depth), lambda i: (0, i)),
            pl.BlockSpec((width, depth), lambda i: (0, tiles + i)),
            pl.BlockSpec((depth, width), lambda i: (i, 0)),
        ]
        + [pl.BlockSpec(memory_space=pl.ANY)] * len(extra),
        out_specs=[pl.BlockSpec((span, width), lambda i: (which, 0)), tile, tile] + [whole] * count,
        out_shape=[jax.ShapeDtypeStruct((span * parts, w), t) for w, t in kept]
        + [jax.ShapeDtypeStruct((rows, width), t) for t in types],
        scratch_shapes=[pltpu.VMEM((span, width), BF), pltpu.VMEM((span, width), F32)],
        input_output_aliases={count + 5 + i: i for i in range(len(extra))},
        compiler_params=pltpu.CompilerParams(vmem_limit_bytes=48 * 1024 * 1024),
        cost_estimate=BRIEF,
        name="mlp_back",
    )(*ds, g, u, gu_w, gu_w, down_w, *extra)
    return result[:3], result[3:]


def outer(lefts, rights, which, by_rows, away=None, runs=1):
    count = max(len(lefts), len(rights))
    depth = sum(v.shape[0] for v in lefts)
    chunk = depth // count
    out_rows, out_cols = lefts[0].shape[1], rights[0].shape[1]
    out_rows, out_cols = (out_rows // 2, out_cols) if by_rows else (out_rows, out_cols // 2)
    tile = min(TILE, out_rows // runs)
    tiles = out_rows // tile
    run = tiles // runs

    def kernel(which, *refs):
        left, right = refs[: len(lefts)], refs[len(lefts) : len(lefts) + len(rights)]
        take = lambda group, i: group[i][...] if len(group) > 1 else group[0][i * chunk : (i + 1) * chunk, :]
        total = mm_rows(take(left, 0), take(right, 0))
        for i in range(1, count):
            total = total + mm_rows(take(left, i), take(right, i))
        if away is not None:
            total = total + refs[-2][...].astype(F32)
        refs[-1][...] = total.astype(BF)

    out_spec = pl.BlockSpec((tile, out_cols), lambda i, w: (i, 0))
    return pl.pallas_call(
        kernel,
        grid_spec=pltpu.PrefetchScalarGridSpec(
            num_scalar_prefetch=1,
            grid=(tiles,),
            in_specs=[
                pl.BlockSpec((v.shape[0], tile), lambda i, w: (0, (i // run + w[0]) * run + i if by_rows else i)) for v in lefts
            ]
            + [pl.BlockSpec((v.shape[0], out_cols), lambda i, w: (0, 0 if by_rows else w[0])) for v in rights]
            + ([] if away is None else [out_spec]),
            out_specs=out_spec,
        ),
        out_shape=jax.ShapeDtypeStruct((out_rows, out_cols), BF),
        compiler_params=pltpu.CompilerParams(vmem_limit_bytes=48 * 1024 * 1024),
        cost_estimate=BRIEF,
        name="outer",
    )(which.reshape(1).astype(jnp.int32), *lefts, *rights, *([] if away is None else [away]))


def project(lefts, weight, transposed, types):
    rows, depth = lefts[0].shape
    width = weight.shape[0] if transposed else weight.shape[1]
    tile = min(512, width)
    count = len(lefts)

    def kernel(*refs):
        left, (w,), outs = refs[:count], refs[count : count + 1], refs[count + 1 :]
        for i in range(count):
            result = (mm_t if transposed else mm)(left[i][...], w[...])
            if len(outs) > 1:
                outs[i][...] = result.astype(outs[i].dtype)
            else:
                outs[0][i * rows : (i + 1) * rows, :] = result.astype(outs[0].dtype)

    height = rows * count // len(types)
    return pl.pallas_call(
        kernel,
        grid=(width // tile,),
        in_specs=[pl.BlockSpec((rows, depth), lambda i: (0, 0))] * count
        + [
            pl.BlockSpec((tile, depth), lambda i: (i, 0))
            if transposed
            else pl.BlockSpec((depth, tile), lambda i: (0, i))
        ],
        out_specs=[pl.BlockSpec((height, tile), lambda i: (0, i))] * len(types),
        out_shape=[jax.ShapeDtypeStruct((height, width), t) for t in types],
        compiler_params=pltpu.CompilerParams(vmem_limit_bytes=48 * 1024 * 1024),
        cost_estimate=BRIEF,
        name="project",
    )(*lefts, weight)


def assemble(places, arrays, depth):
    width = arrays[0].shape[1]
    pieces = [(n, start) for n, v in enumerate(arrays) for start in range(0, v.shape[0], depth)]
    count = len(pieces)

    def kernel(places, *refs):
        sources, out, held, arrive, leave = refs[: len(arrays)], *refs[len(arrays) :]
        ins = [
            pltpu.make_async_copy(sources[n].at[pl.ds(start, depth), :], held.at[i], arrive.at[i])
            for i, (n, start) in enumerate(pieces)
        ]
        outs = [pltpu.make_async_copy(held.at[i], out.at[places[i]], leave.at[i]) for i in range(count)]
        for copy in ins:
            copy.start()
        for i in range(count):
            ins[i].wait()
            outs[i].start()
        for copy in outs:
            copy.wait()

    return pl.pallas_call(
        kernel,
        grid_spec=pltpu.PrefetchScalarGridSpec(
            num_scalar_prefetch=1,
            grid=(1,),
            in_specs=[pl.BlockSpec(memory_space=pl.ANY)] * len(arrays),
            out_specs=pl.BlockSpec(memory_space=pl.ANY),
            scratch_shapes=[
                pltpu.VMEM((count, depth, width), arrays[0].dtype),
                pltpu.SemaphoreType.DMA((count,)),
                pltpu.SemaphoreType.DMA((count,)),
            ],
        ),
        out_shape=jax.ShapeDtypeStruct((count, depth, width), arrays[0].dtype),
        compiler_params=pltpu.CompilerParams(vmem_limit_bytes=VMEM_LIMIT),
        cost_estimate=BRIEF,
        name="assemble",
    )(places, *arrays).reshape(count * depth, width)


def take_columns(which, arrays, groups, members):
    depth, width = arrays[0].shape
    part = width // (groups * members)
    kept = len(which)
    if part % HD:
        views = [v.reshape(depth, groups, members, part) for v in arrays]
        return [
            jnp.concatenate(
                [lax.dynamic_slice_in_dim(v, k, 1, 2).reshape(depth, groups * part) for v in views], 1
            )
            for k in which
        ]

    def kernel(which, *refs):
        sources, outs = refs[: len(arrays)], refs[len(arrays) :]
        for k in range(kept):
            for n, source in enumerate(sources):
                for i in range(groups):
                    start = pl.multiple_of(i * members * part + which[k] * part, HD)
                    outs[k][:, (n * groups + i) * part : (n * groups + i + 1) * part] = source[:, pl.ds(start, part)]

    tile = min(64, depth)
    return pl.pallas_call(
        kernel,
        grid_spec=pltpu.PrefetchScalarGridSpec(
            num_scalar_prefetch=1,
            grid=(depth // tile,),
            in_specs=[pl.BlockSpec((tile, width), lambda i, w: (i, 0))] * len(arrays),
            out_specs=[pl.BlockSpec((tile, len(arrays) * groups * part), lambda i, w: (i, 0))] * kept,
        ),
        out_shape=[jax.ShapeDtypeStruct((depth, len(arrays) * groups * part), arrays[0].dtype)] * kept,
        name="take_columns",
    )(jnp.stack(which).astype(jnp.int32), *arrays)


def body(planes, shards, tokens, pairs, valid, teacher, w_query, w_key, w_value, w_out, w_gate, w_up, w_down):
    seqs, slots, blk, width = tokens.shape
    ff = w_gate.shape[1]
    rows = seqs * slots * blk
    world = planes * shards
    near = planes // 2
    all_heads = width // HD
    heads = all_heads // planes
    mine = heads * HD
    own_rows = width // shards
    part_ff = ff // planes
    length = planes * slots * blk
    unit = width // world
    both = ("ctx", "fsdp")

    c, f = lax.axis_index("ctx"), lax.axis_index("fsdp")
    far, low = c // near, c % near
    core, x, y = f % 2, f // 2 % 2, f // 4
    group = x * near + low

    def after(array, *others):
        return lax.optimization_barrier((array, *others))[0]

    def flip(array, bits):
        return lax.ppermute(array, "fsdp", [(i, i ^ bits) for i in range(shards)])

    def flip_ctx(array, bits):
        return lax.ppermute(array, "ctx", [(i, i ^ bits) for i in range(planes)])

    def hop(array, j):
        dx, dz = j // near, j % near
        if dz == 0:
            return flip(array, 2 * dx)
        if dx == 0:
            return flip_ctx(array, dz)
        return lax.ppermute(
            array,
            both,
            [(p * shards + s, (p ^ dz) * shards + (s ^ 2)) for p in range(planes) for s in range(shards)],
        )

    def send(array, homes):
        moved = lax.ppermute(array, both, [(i, to) for i, to in enumerate(homes) if i != to])
        stays = jnp.array([i == to for i, to in enumerate(homes)])[c * shards + f]
        return jnp.where(stays, array, moved)

    def swap(array):
        homes = []
        for p in range(planes):
            for s in range(shards):
                to = (s // 2 % 2) * near + p % near
                homes.append(to * shards + (s - s // 2 % 2 * 2 + p // near * 2))
        return send(array, homes)

    cos, sin = tables(length)
    ranks = jnp.argsort(pairs.reshape(-1))
    owner = ranks // slots
    relative = ((owner // near) ^ x) * near + ((owner % near) ^ low)
    order = (relative * slots + ranks % slots).astype(jnp.int32)

    def over_y(piece):
        return [flip(piece, bits) for bits in range(4, shards, 4)]

    y_bits = list(range(4, shards, 4))

    def put(*items):
        keys = [k for _, own_keys in items for k in own_keys]
        depth = items[0][0].shape[0] // len(items[0][1])
        places = jnp.stack([f ^ k for k in keys]).astype(jnp.int32)
        return assemble(places, [v for v, _ in items], depth)

    def put_pairs(both_x, both_y, other_x, other_y):
        items = [(both_x, [0, 2]), (other_x, [1, 3])]
        for bits, v, w in zip(y_bits, both_y, other_y):
            items += [(v, [bits, bits + 2]), (w, [bits + 1, bits + 3])]
        return put(*items)

    def head_columns(g):
        return jnp.concatenate(
            [lax.dynamic_slice_in_dim(w, g * mine, mine, 1) for w in (w_query, w_key, w_value)], 1
        )

    def ff_rows(g):
        return lax.dynamic_slice_in_dim(w_down, g * (part_ff // shards), part_ff // shards, 0)

    def own_heads(weight):
        sends, spreads = [], {}
        for p in range(planes):
            for s in range(shards):
                q = s // 2
                if q % near == p % near:
                    at = s // 4 * 4 + q // near * 2 + s % 2
                    if at != s:
                        sends.append((p * shards + s, p * shards + at))
                    for d in range(4, shards, 4):
                        spreads.setdefault(d, []).append((p * shards + at, p * shards + (at ^ d)))
        q = f // 2
        stays = (q % near == low) & (f // 4 * 4 + q // near * 2 + core == f)
        first = jnp.where(stays, weight, lax.ppermute(weight, both, sends))

        def rest(first):
            found = first
            for pairs_of in spreads.values():
                found = found + lax.ppermute(first, both, pairs_of)
            return found

        return first, rest

    cut = planes // 2
    early = list(range(1, cut + 1))
    late = [0, *range(cut + 1, planes)]
    early_types = [BF] * cut
    late_types = [F32] + [BF] * (planes - cut - 1)

    def gather_far(found):
        if near != 2:
            return [hop(found[0], j) for j in late[1:]]
        half = rows // 2
        return [hop(found[1][:half], 2), hop(found[2][half:], 1)]

    def joined(found, others):
        return found + (others if near != 2 else [jnp.concatenate(others, 0)])

    def reduce_far(parts):
        if near != 2:
            return [hop(parts[j], j) for j in late[1:]]
        half = rows // 2
        return [hop(parts[3][:half], 2), hop(parts[3][half:], 1)]

    def reduce_near(parts, received):
        if near != 2:
            return add_all(parts[0], received), [hop(parts[j], j) for j in early]
        half = rows // 2
        more = lambda part, other: (part.astype(F32) + other.astype(F32)).astype(BF)
        to_low = jnp.concatenate([more(parts[1][:half], received[0]), parts[1][half:]], 0)
        to_x = jnp.concatenate([parts[2][:half], more(parts[2][half:], received[1])], 0)
        return parts[0], [hop(to_low, 1), hop(to_x, 2)]

    def add_all(total, others):
        for other in others:
            total = total + other.astype(F32)
        return total

    region = lambda *values: lax.optimization_barrier(values)

    gate_own, gate_send = take_columns([group, group ^ near], [w_gate], shards, planes)
    gate_own_y = over_y(gate_own)
    up_own, up_send = take_columns([group, group ^ near], [w_up], shards, planes)
    up_own_y = over_y(up_own)
    stream_low = swap(tokens.reshape(rows, width))
    qkv_own = head_columns(group)
    qkv_other = flip(head_columns(group ^ near), 2)
    heads_first, heads_rest = own_heads(w_out)
    stream = stream_low.astype(F32)
    normed_one, inverse_one = normalize(stream)
    qkv_both = jnp.concatenate([qkv_own, qkv_other], 0)
    gate_parts, up_parts = [gate_own, gate_send, *gate_own_y], [up_own, up_send, *up_own_y]
    h1, stream_low, qkv_both, gate_parts, up_parts, heads_first, w_down = region(
        [normed_one.astype(BF)], stream_low, qkv_both, gate_parts, up_parts, heads_first, w_down
    )
    gu_own, gu_send, *gu_own_y = [jnp.concatenate(v, 1) for v in zip(gate_parts, up_parts)]

    h1 = h1 + [hop(h1[0], j) for j in early]
    qkv_y = over_y(qkv_both)
    qkv_pair = flip(qkv_both, 1)
    found = heads_rest(heads_first)
    h1, qkv_both, qkv_pair, w_down, gu_send = region(h1, qkv_both, qkv_pair, w_down, gu_send)

    others = gather_far(h1)
    down_own = ff_rows(group)
    down_other = flip(ff_rows(group ^ near), 2)
    others, found, down_own, down_other, qkv_y, gu_send, gu_own_y, teacher = region(
        others, found, down_own, down_other, qkv_y, gu_send, gu_own_y, teacher
    )
    h1 = joined(h1, others)

    gu_other = flip(gu_send, 2)
    down_both = jnp.concatenate([down_own, down_other], 0)
    down_y = over_y(down_both)
    other = flip(found, 1)
    qkv_y_pair = [flip(v, 1) for v in qkv_y]
    w_qkv = put_pairs(qkv_both, qkv_y, qkv_pair, qkv_y_pair)
    (qkv,) = project(h1, w_qkv, False, [F32])
    qkv = qkv.reshape(planes, seqs, slots, blk, 3 * mine)
    mixed, lse = attend(order, qkv, cos, sin, heads)
    even = core == 0
    w_out_mine = jnp.concatenate([jnp.where(even, found, other), jnp.where(even, other, found)], 0)
    group_types = [F32] + [BF] * (planes - 1)
    products = project([mixed[s].reshape(rows, mine) for s in range(planes)], w_out_mine, False, group_types)
    products, gu_other, down_both, down_y, gu_own, gu_own_y, teacher = region(
        products, gu_other, down_both, down_y, gu_own, gu_own_y, teacher
    )

    received = reduce_far(products)
    gate_other_y = over_y(gu_other[:, :part_ff])
    down_pair = flip(down_both, 1)
    gu_own_pair = flip(gu_own, 1)
    received, products, down_pair, gu_other, gate_other_y, down_y, gu_own_pair, gu_own_y = region(
        received, products, down_pair, gu_other, gate_other_y, down_y, gu_own_pair, gu_own_y
    )

    own, received = reduce_near(products, received)
    up_other_y = over_y(gu_other[:, part_ff:])
    gu_other_y = [jnp.concatenate(v, 1) for v in zip(gate_other_y, up_other_y)]
    down_y_pair = [flip(v, 1) for v in down_y]
    gu_own_y_pair = [flip(v, 1) for v in gu_own_y]
    residual = stream + add_all(own, received)
    normed_two, inverse_two = normalize(residual)
    h2, gu_other_y, gu_other, down_y_pair, gu_own_y_pair, valid = region(
        [normed_two.astype(BF)], gu_other_y, gu_other, down_y_pair, gu_own_y_pair, valid
    )

    h2 = h2 + [hop(h2[0], j) for j in early]
    gu_other_pair = flip(gu_other, 1)
    gu_items = [(gu_own, [0]), (gu_own_pair, [1]), (gu_other, [2]), (gu_other_pair, [3])]
    for bits, v, w, z in zip(y_bits, gu_own_y, gu_own_y_pair, gu_other_y):
        gu_items += [(v, [bits]), (w, [bits + 1]), (z, [bits + 2]), (flip(z, 1), [bits + 3])]
    down_w = put_pairs(down_both, down_y, down_pair, down_y_pair)
    gu_w = put(*gu_items)
    h2, gu_w, down_w, valid, teacher = region(h2, gu_w, down_w, valid, teacher)

    others = gather_far(h2)
    goal_low = swap(teacher.reshape(rows, width))
    kept, outs = mlp([h2[j] for j in early], gu_w, down_w, early_types, 2, 0)
    outs, kept, others = region(outs, kept, others)
    h2 = joined(h2, others)

    received = [hop(v, j) for v, j in zip(outs, early)]
    (h2_all, gates, ups, hidden_all), outs = mlp(
        [h2[j] for j in late], gu_w, down_w, late_types, 2, 1, kept
    )
    received, outs, h2_all, gates, ups, hidden_all, valid, goal_low = region(
        received, outs, h2_all, gates, ups, hidden_all, valid, goal_low
    )

    received = received + [hop(v, j) for v, j in zip(outs[1:], late[1:])]
    valid_float = swap(valid.reshape(rows, 1)).astype(F32)

    output = residual + add_all(outs[0], received)
    deviation = output - goal_low.astype(F32)
    grad_output = valid_float * deviation
    sums = jnp.stack([jnp.sum(grad_output * deviation), jnp.sum(valid_float)])
    sums0 = jnp.broadcast_to(sums[:, None, None], (2, 8, HD))
    sums0, grad_output, output = region(sums0, grad_output, output)

    sums = sums0
    for bits in range(1, planes):
        sums = sums + flip_ctx(sums0, bits)
    low_grad, low_output, sums = region(grad_output.astype(BF), output.astype(BF), sums)

    steps = [1 << b for b in reversed(range(2, shards.bit_length() - 1))]

    def halve(part, axis, bit, move, bits):
        half = part.shape[axis] // 2
        take = lambda k: lax.dynamic_slice_in_dim(part, k * half, half, axis)
        away = move(take(1 - bit), bits)
        return (take(bit).astype(F32) + away.astype(F32)).astype(BF)

    def parts(whole):
        return whole.reshape(2, near, shards // 4, 2, 2, unit, whole.shape[1])

    def across_y(part, axis):
        for step in steps:
            part = halve(part, axis, f // step % 2, flip, step)
        return part

    def across_far(part):
        return halve(part, 0, far, flip_ctx, near)

    def place_rows(part, place):
        homes = []
        for p in range(planes):
            for s in range(shards):
                homes.append(place(s % 2, s // 4, p // near, (s // 2 % 2) * near + p % near))
        return send(part, homes).astype(F32)

    def take(v, k, axis):
        return lax.dynamic_index_in_dim(v, k, axis, keepdims=False)

    def core_away(part):
        return flip(take(part.reshape(near, 2, 2, unit, part.shape[-1]), 1 - core, 2), 1)

    def core_joined(part, away):
        keep = take(part.reshape(near, 2, 2, unit, part.shape[-1]), core, 2)
        even = core == 0
        return jnp.concatenate([jnp.where(even, keep, away), jnp.where(even, away, keep)], -1)

    def column_pieces(part):
        return [take(take(part, x ^ (j // near), 1), low ^ (j % near), 0) for j in range(planes)]

    def columns_placed(pieces):
        places = jnp.stack([group ^ j for j in range(planes)]).astype(jnp.int32)
        return assemble(places, pieces, unit).reshape(planes, unit, -1)

    dm = [low_grad] + [hop(low_grad, j) for j in early]
    for bits in [1, *(1 << b for b in range(2, shards.bit_length() - 1))]:
        sums = sums + flip(sums, bits)
    dm, sums, low_output = region(dm, sums, low_output)

    others = gather_far(dm)
    kept, backs = mlp_back([dm[j] for j in early], gates, ups, gu_w, down_w, early_types, 2, 0)
    backs, kept, others, sums, low_output = region(backs, kept, others, sums, low_output)
    dm = joined(dm, others)

    received = [hop(v, j) for v, j in zip(backs, early)]
    dm_runs = [dm[j] for j in early + late]
    away = flip(outer([hidden_all], dm_runs, 1 - core, True, None, 2), 1)
    (_, dg_all, du_all), backs = mlp_back(
        [dm[j] for j in late], gates, ups, gu_w, down_w, late_types, 2, 1, kept
    )
    g_down = outer([hidden_all], dm_runs, core, True, away, 2)
    received, backs, g_down, dg_all, du_all, h2_all, low_output = region(
        received, backs, g_down, dg_all, du_all, h2_all, low_output
    )

    received = received + [hop(v, j) for v, j in zip(backs[1:], late[1:])]
    activations = swap(low_output)
    g_down = across_y(g_down.reshape(2, shards // 4, part_ff // shards, width), 1)
    gate_half = outer([h2_all], [dg_all], 1 - core, False)
    up_half = outer([h2_all], [du_all], 1 - core, False)
    grad_two = add_all(backs[0], received)
    grad_residual = grad_output + norm_back(grad_two, normed_two, inverse_two)
    dab, gate_half, up_half, g_down, dg_all, du_all, activations = region(
        [grad_residual.astype(BF)], gate_half, up_half, g_down, dg_all, du_all, activations
    )

    dab = dab + [hop(dab[0], j) for j in early]
    gate_away, up_away = flip(gate_half, 1), flip(up_half, 1)
    g_gate = outer([h2_all], [dg_all], core, False, gate_away)
    dab, g_gate, up_away, du_all, g_down = region(dab, g_gate, up_away, du_all, g_down)

    others = gather_far(dab)
    g_gate = across_y(parts(g_gate), 2)
    g_up = outer([h2_all], [du_all], core, False, up_away)
    others, g_up, g_down = region(others, g_up, g_down)
    dab = joined(dab, others)

    up_first, up_second = jnp.split(parts(g_up), 2, -1)
    up_first = across_y(up_first, 2)
    g_down = across_far(g_down)
    (do,) = project(dab, w_out_mine, True, [BF])
    dqkv = attend_back(order, qkv, lse, do.reshape(planes, seqs, slots, blk, mine), cos, sin, heads)
    dqkv = dqkv.reshape(planes * rows, 3 * mine)
    qkv_half = outer(h1, [dqkv], 1 - core, False)
    mixed = mixed.reshape(planes * rows, mine)
    out_half = outer([mixed], dab, 1 - core, True)
    dqkv, qkv_half, out_half, g_gate, g_down, up_first, up_second, sums = region(
        dqkv, qkv_half, out_half, g_gate, g_down, up_first, up_second, sums
    )

    qkv_away, out_away = flip(qkv_half, 1), flip(out_half, 1)
    backs = project([dqkv[i * rows : (i + 1) * rows] for i in range(planes)], w_qkv, True, group_types)
    up_second = across_y(up_second, 2)
    sums = sums + flip(sums, 2)
    gate_first, gate_second = jnp.split(g_gate, 2, -1)
    gate_first = across_far(gate_first)
    backs, dqkv, qkv_away, out_away, up_second, gate_first, gate_second, sums = region(
        backs, dqkv, qkv_away, out_away, up_second, gate_first, gate_second, sums
    )

    gate_second = across_far(gate_second)
    up_parts = jnp.concatenate([up_first, up_second], -1)
    up_keep, up_away = (lax.dynamic_slice_in_dim(up_parts, k, 1, 0) for k in (far, 1 - far))
    received = reduce_far(backs)
    g_qkv = parts(outer(h1, [dqkv], core, False, qkv_away))
    g_out = outer([mixed], dab, core, True, out_away)
    received, backs, g_qkv, g_out, g_down, gate_first, gate_second, up_keep, up_away = region(
        received, backs, g_qkv, g_out, g_down, gate_first, gate_second, up_keep, up_away
    )

    own, received = reduce_near(backs, received)
    g_up = (up_keep.astype(F32) + flip_ctx(up_away, near).astype(F32)).astype(BF)
    g_out = across_y(g_out, 0)
    g_gate = jnp.concatenate([gate_first, gate_second], -1)
    g_down = place_rows(
        g_down.reshape(ff // world, width),
        lambda core, y, far, g: far * (shards // 2) * planes + (core * (shards // 4) + y) * planes + g,
    )
    grad_one = add_all(own, received)
    grad_stream = grad_residual + norm_back(grad_one, normed_one, inverse_one)
    low_stream, g_out, g_qkv, g_gate, g_up, g_down = region(
        grad_stream.astype(BF), g_out, g_qkv, g_gate, g_up, g_down
    )

    grad_low = swap(low_stream)
    g_qkv = across_y(g_qkv, 2)
    g_out = across_far(g_out)
    gate_core, up_core = core_away(g_gate), core_away(g_up)
    pieces = [column_pieces(core_joined(v, w)) for v, w in ((g_gate, gate_core), (g_up, up_core))]
    pieces = [jnp.concatenate(v, 1) for v in zip(*pieces)]
    grad_low, g_qkv, g_out, pieces = region(grad_low, g_qkv, g_out, pieces)

    g_qkv = across_far(g_qkv)
    g_out = place_rows(g_out, lambda core, y, far, g: g * shards + (core * (shards // 4) + y) * 2 + far)
    pieces = [hop(v, j) if j else v for j, v in enumerate(pieces)]
    pieces, g_qkv, g_out = region(pieces, g_qkv, g_out)
    qkv_pieces = column_pieces(core_joined(g_qkv, core_away(g_qkv)))
    qkv_pieces, pieces = region(qkv_pieces, pieces)
    qkv_pieces = [hop(v, j) if j else v for j, v in enumerate(qkv_pieces)]
    count = sums[1, 0, 0]
    loss = sums[0, 0, 0] / (count * width)
    factor = (rows * world) / count
    grad_input = grad_low.astype(F32) * factor
    ff_order = lambda v: v.reshape(planes, unit, shards, -1).transpose(1, 2, 0, 3).reshape(unit, ff)
    placed = columns_placed(pieces)
    g_gate = ff_order(placed[:, :, :part_ff]).astype(F32)
    g_up = ff_order(placed[:, :, part_ff:]).astype(F32)
    g_qkv = columns_placed(qkv_pieces).reshape(planes, unit, 3, mine).transpose(2, 1, 0, 3)
    g_qkv = g_qkv.reshape(3, unit, width).astype(F32)
    return (
        activations.reshape(tokens.shape),
        loss,
        grad_input.reshape(tokens.shape),
        g_qkv[0] * factor,
        g_qkv[1] * factor,
        g_qkv[2] * factor,
        g_out * factor,
        g_gate * factor,
        g_up * factor,
        g_down * factor,
    )


def solution(mesh):
    tokens = P("fsdp", "ctx", None, None)
    weight = P("fsdp", None)
    grad = P(("ctx", "fsdp"), None)
    in_specs = (tokens, P(), P("fsdp", "ctx", None), tokens) + (weight,) * 7
    out_specs = (tokens, P(), tokens) + (grad,) * 7
    step = functools.partial(body, mesh.shape["ctx"], mesh.shape["fsdp"])
    return jax.shard_map(step, mesh=mesh, in_specs=in_specs, out_specs=out_specs, check_vma=False)
```

```python
import functools

import jax
import jax.numpy as jnp
from jax import lax
from jax.experimental import pallas as pl
from jax.experimental.pallas import tpu as pltpu
from jax.sharding import PartitionSpec as P

HD = 128
EPS = 1e-05
BF = jnp.bfloat16
F32 = jnp.float32
NEG = -1e30


def normalize(rows):
    centered = rows - jnp.mean(rows, -1, keepdims=True)
    inverse = lax.rsqrt(jnp.mean(centered * centered, -1, keepdims=True) + EPS)
    return centered * inverse, inverse


def norm_back(gradient, normed, inverse):
    centered = gradient - jnp.mean(gradient, -1, keepdims=True)
    return inverse * (centered - normed * jnp.mean(gradient * normed, -1, keepdims=True))


def mm(left, right):
    return jnp.dot(left, right, preferred_element_type=F32)


def mm_t(left, right):
    return lax.dot_general(left, right, (((1,), (1,)), ((), ())), preferred_element_type=F32)


def mm_rows(left, right):
    return lax.dot_general(left, right, (((0,), (0,)), ((), ())), preferred_element_type=F32)


def tables(length):
    frequency = 10000.0 ** (-2.0 * jnp.arange(HD // 2, dtype=F32) / HD)
    phases = jnp.arange(length, dtype=F32)[:, None] * frequency[None, :]
    cosine, sine = jnp.cos(phases), jnp.sin(phases)
    return jnp.concatenate([cosine, cosine], 1), jnp.concatenate([-sine, sine], 1)


def fwd_kernel(heads, order, qkv, cos, sin, out, lse, q_s, k_s, v_s):
    planes, _, slots, blk, _ = qkv.shape
    blocks = planes * slots
    scale = HD ** -0.5

    def head(h, carry):
        col = pl.multiple_of(h * HD, HD)

        def load(b, carry):
            where = order[b]
            s, t = where // slots, where % slots
            row = pl.ds(pl.multiple_of(b * blk, blk), blk)
            c, n = cos[row, :], sin[row, :]
            q = qkv[s, 0, t, :, pl.ds(col, HD)]
            k = qkv[s, 0, t, :, pl.ds(pl.multiple_of(heads * HD + col, HD), HD)]
            q_s[row, :] = ((q * c + pltpu.roll(q, HD // 2, 1) * n) * scale).astype(BF)
            k_s[row, :] = (k * c + pltpu.roll(k, HD // 2, 1) * n).astype(BF)
            v_s[row, :] = qkv[s, 0, t, :, pl.ds(pl.multiple_of(2 * heads * HD + col, HD), HD)].astype(BF)
            return carry

        lax.fori_loop(0, blocks, load, 0)
        for b in range(blocks):
            keys = (b + 1) * blk
            scores = mm_t(q_s[b * blk : keys, :], k_s[0:keys, :])
            top = jnp.max(scores, -1, keepdims=True)
            raised = jnp.exp(scores - top)
            total = jnp.sum(raised, -1, keepdims=True)
            probs = (raised * (1.0 / total)).astype(BF)
            mixed = mm(probs, v_s[0:keys, :])
            where = order[b]
            s, t = where // slots, where % slots
            out[s, 0, t, :, pl.ds(col, HD)] = mixed.astype(BF)
            lse[s, 0, t, :, pl.ds(col, HD)] = jnp.broadcast_to(top + jnp.log(total), (blk, HD))
        return carry

    lax.fori_loop(0, heads, head, 0)


def bwd_kernel(heads, order, qkv, lse, grad, cos, sin, dqkv, q_s, k_s, v_s, g_s, l_s, dk_s, dv_s):
    planes, _, slots, blk, _ = qkv.shape
    blocks = planes * slots
    scale = HD ** -0.5

    def head(h, carry):
        col = pl.multiple_of(h * HD, HD)
        kcol = pl.multiple_of(heads * HD + col, HD)
        vcol = pl.multiple_of(2 * heads * HD + col, HD)

        def load(b, carry):
            where = order[b]
            s, t = where // slots, where % slots
            row = pl.ds(pl.multiple_of(b * blk, blk), blk)
            c, n = cos[row, :], sin[row, :]
            q = qkv[s, 0, t, :, pl.ds(col, HD)]
            k = qkv[s, 0, t, :, pl.ds(kcol, HD)]
            q_s[row, :] = ((q * c + pltpu.roll(q, HD // 2, 1) * n) * scale).astype(BF)
            k_s[row, :] = (k * c + pltpu.roll(k, HD // 2, 1) * n).astype(BF)
            v_s[row, :] = qkv[s, 0, t, :, pl.ds(vcol, HD)].astype(BF)
            g_s[row, :] = grad[s, 0, t, :, pl.ds(col, HD)]
            l_s[row, :] = lse[s, 0, t, :, pl.ds(col, HD)]
            return carry

        lax.fori_loop(0, blocks, load, 0)
        dk_s[...] = jnp.zeros_like(dk_s)
        dv_s[...] = jnp.zeros_like(dv_s)
        for b in range(blocks):
            keys = (b + 1) * blk
            mine = slice(b * blk, keys)
            scores = mm_t(q_s[mine, :], k_s[0:keys, :])
            probs = jnp.exp(scores - l_s[mine, 0:1])
            dprobs = mm_t(g_s[mine, :], v_s[0:keys, :])
            delta = jnp.sum(probs * dprobs, -1, keepdims=True)
            dscores = (probs * (dprobs - delta)).astype(BF)
            dq = mm(dscores, k_s[0:keys, :]) * scale
            dk_s[0:keys, :] += mm_rows(dscores, q_s[mine, :])
            dv_s[0:keys, :] += mm_rows(probs.astype(BF), g_s[mine, :])
            where = order[b]
            s, t = where // slots, where % slots
            dq = dq * cos[mine, :] - pltpu.roll(dq, HD // 2, 1) * sin[mine, :]
            dqkv[s, 0, t, :, pl.ds(col, HD)] = dq.astype(BF)

        def store(b, carry):
            where = order[b]
            s, t = where // slots, where % slots
            row = pl.ds(pl.multiple_of(b * blk, blk), blk)
            dk = dk_s[row, :]
            dk = dk * cos[row, :] - pltpu.roll(dk, HD // 2, 1) * sin[row, :]
            dqkv[s, 0, t, :, pl.ds(kcol, HD)] = dk.astype(BF)
            dqkv[s, 0, t, :, pl.ds(vcol, HD)] = dv_s[row, :].astype(BF)
            return carry

        lax.fori_loop(0, blocks, store, 0)
        return carry

    lax.fori_loop(0, heads, head, 0)


VMEM_LIMIT = 56 * 1024 * 1024
BRIEF = pl.CostEstimate(flops=1024, bytes_accessed=1024, transcendentals=0)


def attend(order, qkv, cos, sin, heads):
    planes, seqs, slots, blk, width = qkv.shape
    length = planes * slots * blk
    spec = lambda w: pl.BlockSpec((planes, 1, slots, blk, w), lambda i, o: (0, i, 0, 0, 0))
    table = pl.BlockSpec((length, HD), lambda i, o: (0, 0))
    return pl.pallas_call(
        functools.partial(fwd_kernel, heads),
        grid_spec=pltpu.PrefetchScalarGridSpec(
            num_scalar_prefetch=1,
            grid=(seqs,),
            in_specs=[spec(width), table, table],
            out_specs=[spec(heads * HD), spec(heads * HD)],
            scratch_shapes=[pltpu.VMEM((length, HD), BF)] * 3,
        ),
        out_shape=[
            jax.ShapeDtypeStruct((planes, seqs, slots, blk, heads * HD), BF),
            jax.ShapeDtypeStruct((planes, seqs, slots, blk, heads * HD), F32),
        ],
        compiler_params=pltpu.CompilerParams(vmem_limit_bytes=VMEM_LIMIT),
        cost_estimate=BRIEF,
        name="attend",
    )(order, qkv, cos, sin)


def attend_back(order, qkv, lse, grad, cos, sin, heads):
    planes, seqs, slots, blk, width = qkv.shape
    length = planes * slots * blk
    spec = lambda w: pl.BlockSpec((planes, 1, slots, blk, w), lambda i, o: (0, i, 0, 0, 0))
    table = pl.BlockSpec((length, HD), lambda i, o: (0, 0))
    return pl.pallas_call(
        functools.partial(bwd_kernel, heads),
        grid_spec=pltpu.PrefetchScalarGridSpec(
            num_scalar_prefetch=1,
            grid=(seqs,),
            in_specs=[spec(width), spec(heads * HD), spec(heads * HD), table, table],
            out_specs=spec(width),
            scratch_shapes=[pltpu.VMEM((length, HD), BF)] * 4 + [pltpu.VMEM((length, HD), F32)] * 3,
        ),
        out_shape=jax.ShapeDtypeStruct((planes, seqs, slots, blk, width), BF),
        compiler_params=pltpu.CompilerParams(vmem_limit_bytes=VMEM_LIMIT),
        cost_estimate=BRIEF,
        name="attend_back",
    )(order, qkv, lse, grad, cos, sin)


TILE = 512


def up_kernel(count, *refs):
    hs, (wg, wu, wd) = refs[:count], refs[count : count + 3]
    refs = refs[count + 3 :]
    refs = refs[4:] if len(refs) > count + 6 else refs
    h_all, g_out, u_out, hidden_out = refs[:4]
    outs, (held, total) = refs[4 : 4 + count], refs[4 + count :]
    step = pl.program_id(0)
    rows = hs[0].shape[0]

    @pl.when(step == 0)
    def _():
        for i in range(count):
            held[i * rows : (i + 1) * rows, :] = hs[i][...]
        h_all[...] = held[...]
        total[...] = jnp.zeros_like(total)

    h = held[...]
    g, u = mm(h, wg[...]), mm(h, wu[...])
    hidden = (g * (1.0 / (1.0 + jnp.exp(-g))) * u).astype(BF)
    g_out[...], u_out[...], hidden_out[...] = g, u, hidden
    total[...] += mm(hidden, wd[...])

    @pl.when(step == pl.num_programs(0) - 1)
    def _():
        for i in range(count):
            outs[i][...] = total[i * rows : (i + 1) * rows, :].astype(outs[i].dtype)


def mlp(hs, gu_w, down_w, types, parts, which, held=None):
    rows, width = hs[0].shape
    part_ff = down_w.shape[0]
    count = len(hs)
    span = rows * count
    depth = TILE if span <= TILE else TILE // 2
    tiles = part_ff // depth
    whole = pl.BlockSpec((rows, width), lambda i: (0, 0))
    tile = pl.BlockSpec((span, depth), lambda i: (which, i))
    kept = [(width, BF), (part_ff, F32), (part_ff, F32), (part_ff, BF)]
    extra = [] if held is None else list(held)
    result = pl.pallas_call(
        functools.partial(up_kernel, count),
        grid=(tiles,),
        in_specs=[whole] * count
        + [
            pl.BlockSpec((width, depth), lambda i: (0, i)),
            pl.BlockSpec((width, depth), lambda i: (0, tiles + i)),
            pl.BlockSpec((depth, width), lambda i: (i, 0)),
        ]
        + [pl.BlockSpec(memory_space=pl.ANY)] * len(extra),
        out_specs=[pl.BlockSpec((span, width), lambda i: (which, 0)), tile, tile, tile] + [whole] * count,
        out_shape=[jax.ShapeDtypeStruct((span * parts, w), t) for w, t in kept]
        + [jax.ShapeDtypeStruct((rows, width), t) for t in types],
        scratch_shapes=[pltpu.VMEM((span, width), BF), pltpu.VMEM((span, width), F32)],
        input_output_aliases={count + 3 + i: i for i in range(len(extra))},
        compiler_params=pltpu.CompilerParams(vmem_limit_bytes=48 * 1024 * 1024),
        cost_estimate=BRIEF,
        name="mlp",
    )(*hs, gu_w, gu_w, down_w, *extra)
    return result[:4], result[4:]


def down_kernel(count, *refs):
    ds, (g_in, u_in, wg, wu, wd) = refs[:count], refs[count : count + 5]
    refs = refs[count + 5 :]
    refs = refs[3:] if len(refs) > count + 5 else refs
    d_all, dg_out, du_out = refs[:3]
    outs, (held, total) = refs[3 : 3 + count], refs[3 + count :]
    step = pl.program_id(0)
    rows = ds[0].shape[0]

    @pl.when(step == 0)
    def _():
        for i in range(count):
            held[i * rows : (i + 1) * rows, :] = ds[i][...]
        d_all[...] = held[...]
        total[...] = jnp.zeros_like(total)

    dh = mm_t(held[...], wd[...])
    g = g_in[...]
    sig = 1.0 / (1.0 + jnp.exp(-g))
    dg = (dh * u_in[...] * sig * (1.0 + g * (1.0 - sig))).astype(BF)
    du = (dh * (g * sig)).astype(BF)
    dg_out[...], du_out[...] = dg, du
    total[...] += mm_t(dg, wg[...]) + mm_t(du, wu[...])

    @pl.when(step == pl.num_programs(0) - 1)
    def _():
        for i in range(count):
            outs[i][...] = total[i * rows : (i + 1) * rows, :].astype(outs[i].dtype)


def mlp_back(ds, g, u, gu_w, down_w, types, parts, which, held=None):
    rows, width = ds[0].shape
    part_ff = down_w.shape[0]
    count = len(ds)
    span = rows * count
    depth = TILE if span <= TILE else TILE // 2
    tiles = part_ff // depth
    whole = pl.BlockSpec((rows, width), lambda i: (0, 0))
    tile = pl.BlockSpec((span, depth), lambda i: (which, i))
    kept = [(width, BF), (part_ff, BF), (part_ff, BF)]
    extra = [] if held is None else list(held)
    result = pl.pallas_call(
        functools.partial(down_kernel, count),
        grid=(tiles,),
        in_specs=[whole] * count
        + [
            tile,
            tile,
            pl.BlockSpec((width, depth), lambda i: (0, i)),
            pl.BlockSpec((width, depth), lambda i: (0, tiles + i)),
            pl.BlockSpec((depth, width), lambda i: (i, 0)),
        ]
        + [pl.BlockSpec(memory_space=pl.ANY)] * len(extra),
        out_specs=[pl.BlockSpec((span, width), lambda i: (which, 0)), tile, tile] + [whole] * count,
        out_shape=[jax.ShapeDtypeStruct((span * parts, w), t) for w, t in kept]
        + [jax.ShapeDtypeStruct((rows, width), t) for t in types],
        scratch_shapes=[pltpu.VMEM((span, width), BF), pltpu.VMEM((span, width), F32)],
        input_output_aliases={count + 5 + i: i for i in range(len(extra))},
        compiler_params=pltpu.CompilerParams(vmem_limit_bytes=48 * 1024 * 1024),
        cost_estimate=BRIEF,
        name="mlp_back",
    )(*ds, g, u, gu_w, gu_w, down_w, *extra)
    return result[:3], result[3:]


def outer(lefts, rights, which, by_rows, away=None, runs=1):
    count = max(len(lefts), len(rights))
    depth = sum(v.shape[0] for v in lefts)
    chunk = depth // count
    out_rows, out_cols = lefts[0].shape[1], rights[0].shape[1]
    out_rows, out_cols = (out_rows // 2, out_cols) if by_rows else (out_rows, out_cols // 2)
    tile = min(TILE, out_rows // runs)
    tiles = out_rows // tile
    run = tiles // runs

    def kernel(which, *refs):
        left, right = refs[: len(lefts)], refs[len(lefts) : len(lefts) + len(rights)]
        take = lambda group, i: group[i][...] if len(group) > 1 else group[0][i * chunk : (i + 1) * chunk, :]
        total = mm_rows(take(left, 0), take(right, 0))
        for i in range(1, count):
            total = total + mm_rows(take(left, i), take(right, i))
        if away is not None:
            total = total + refs[-2][...].astype(F32)
        refs[-1][...] = total.astype(BF)

    out_spec = pl.BlockSpec((tile, out_cols), lambda i, w: (i, 0))
    return pl.pallas_call(
        kernel,
        grid_spec=pltpu.PrefetchScalarGridSpec(
            num_scalar_prefetch=1,
            grid=(tiles,),
            in_specs=[
                pl.BlockSpec((v.shape[0], tile), lambda i, w: (0, (i // run + w[0]) * run + i if by_rows else i)) for v in lefts
            ]
            + [pl.BlockSpec((v.shape[0], out_cols), lambda i, w: (0, 0 if by_rows else w[0])) for v in rights]
            + ([] if away is None else [out_spec]),
            out_specs=out_spec,
        ),
        out_shape=jax.ShapeDtypeStruct((out_rows, out_cols), BF),
        compiler_params=pltpu.CompilerParams(vmem_limit_bytes=48 * 1024 * 1024),
        cost_estimate=BRIEF,
        name="outer",
    )(which.reshape(1).astype(jnp.int32), *lefts, *rights, *([] if away is None else [away]))


def project(lefts, weight, transposed, types):
    rows, depth = lefts[0].shape
    width = weight.shape[0] if transposed else weight.shape[1]
    tile = min(512, width)
    count = len(lefts)

    def kernel(*refs):
        left, (w,), outs = refs[:count], refs[count : count + 1], refs[count + 1 :]
        for i in range(count):
            result = (mm_t if transposed else mm)(left[i][...], w[...])
            if len(outs) > 1:
                outs[i][...] = result.astype(outs[i].dtype)
            else:
                outs[0][i * rows : (i + 1) * rows, :] = result.astype(outs[0].dtype)

    height = rows * count // len(types)
    return pl.pallas_call(
        kernel,
        grid=(width // tile,),
        in_specs=[pl.BlockSpec((rows, depth), lambda i: (0, 0))] * count
        + [
            pl.BlockSpec((tile, depth), lambda i: (i, 0))
            if transposed
            else pl.BlockSpec((depth, tile), lambda i: (0, i))
        ],
        out_specs=[pl.BlockSpec((height, tile), lambda i: (0, i))] * len(types),
        out_shape=[jax.ShapeDtypeStruct((height, width), t) for t in types],
        compiler_params=pltpu.CompilerParams(vmem_limit_bytes=48 * 1024 * 1024),
        cost_estimate=BRIEF,
        name="project",
    )(*lefts, weight)


def assemble(places, arrays, depth):
    width = arrays[0].shape[1]
    pieces = [(n, start) for n, v in enumerate(arrays) for start in range(0, v.shape[0], depth)]
    count = len(pieces)

    def kernel(places, *refs):
        sources, out, held, arrive, leave = refs[: len(arrays)], *refs[len(arrays) :]
        ins = [
            pltpu.make_async_copy(sources[n].at[pl.ds(start, depth), :], held.at[i], arrive.at[i])
            for i, (n, start) in enumerate(pieces)
        ]
        outs = [pltpu.make_async_copy(held.at[i], out.at[places[i]], leave.at[i]) for i in range(count)]
        for copy in ins:
            copy.start()
        for i in range(count):
            ins[i].wait()
            outs[i].start()
        for copy in outs:
            copy.wait()

    return pl.pallas_call(
        kernel,
        grid_spec=pltpu.PrefetchScalarGridSpec(
            num_scalar_prefetch=1,
            grid=(1,),
            in_specs=[pl.BlockSpec(memory_space=pl.ANY)] * len(arrays),
            out_specs=pl.BlockSpec(memory_space=pl.ANY),
            scratch_shapes=[
                pltpu.VMEM((count, depth, width), arrays[0].dtype),
                pltpu.SemaphoreType.DMA((count,)),
                pltpu.SemaphoreType.DMA((count,)),
            ],
        ),
        out_shape=jax.ShapeDtypeStruct((count, depth, width), arrays[0].dtype),
        compiler_params=pltpu.CompilerParams(vmem_limit_bytes=VMEM_LIMIT),
        cost_estimate=BRIEF,
        name="assemble",
    )(places, *arrays).reshape(count * depth, width)


def take_columns(which, arrays, groups, members):
    depth, width = arrays[0].shape
    part = width // (groups * members)
    kept = len(which)
    if part % HD:
        views = [v.reshape(depth, groups, members, part) for v in arrays]
        return [
            jnp.concatenate(
                [lax.dynamic_slice_in_dim(v, k, 1, 2).reshape(depth, groups * part) for v in views], 1
            )
            for k in which
        ]

    def kernel(which, *refs):
        sources, outs = refs[: len(arrays)], refs[len(arrays) :]
        for k in range(kept):
            for n, source in enumerate(sources):
                for i in range(groups):
                    start = pl.multiple_of(i * members * part + which[k] * part, HD)
                    outs[k][:, (n * groups + i) * part : (n * groups + i + 1) * part] = source[:, pl.ds(start, part)]

    tile = min(64, depth)
    return pl.pallas_call(
        kernel,
        grid_spec=pltpu.PrefetchScalarGridSpec(
            num_scalar_prefetch=1,
            grid=(depth // tile,),
            in_specs=[pl.BlockSpec((tile, width), lambda i, w: (i, 0))] * len(arrays),
            out_specs=[pl.BlockSpec((tile, len(arrays) * groups * part), lambda i, w: (i, 0))] * kept,
        ),
        out_shape=[jax.ShapeDtypeStruct((depth, len(arrays) * groups * part), arrays[0].dtype)] * kept,
        name="take_columns",
    )(jnp.stack(which).astype(jnp.int32), *arrays)


def body(planes, shards, tokens, pairs, valid, teacher, w_query, w_key, w_value, w_out, w_gate, w_up, w_down):
    seqs, slots, blk, width = tokens.shape
    ff = w_gate.shape[1]
    rows = seqs * slots * blk
    world = planes * shards
    near = planes // 2
    all_heads = width // HD
    heads = all_heads // planes
    mine = heads * HD
    own_rows = width // shards
    part_ff = ff // planes
    length = planes * slots * blk
    unit = width // world
    both = ("ctx", "fsdp")

    c, f = lax.axis_index("ctx"), lax.axis_index("fsdp")
    far, low = c // near, c % near
    core, x, y = f % 2, f // 2 % 2, f // 4
    group = x * near + low

    def after(array, *others):
        return lax.optimization_barrier((array, *others))[0]

    def flip(array, bits):
        return lax.ppermute(array, "fsdp", [(i, i ^ bits) for i in range(shards)])

    def flip_ctx(array, bits):
        return lax.ppermute(array, "ctx", [(i, i ^ bits) for i in range(planes)])

    def hop(array, j):
        dx, dz = j // near, j % near
        if dz == 0:
            return flip(array, 2 * dx)
        if dx == 0:
            return flip_ctx(array, dz)
        return lax.ppermute(
            array,
            both,
            [(p * shards + s, (p ^ dz) * shards + (s ^ 2)) for p in range(planes) for s in range(shards)],
        )

    def send(array, homes):
        moved = lax.ppermute(array, both, [(i, to) for i, to in enumerate(homes) if i != to])
        stays = jnp.array([i == to for i, to in enumerate(homes)])[c * shards + f]
        return jnp.where(stays, array, moved)

    def swap(array):
        homes = []
        for p in range(planes):
            for s in range(shards):
                to = (s // 2 % 2) * near + p % near
                homes.append(to * shards + (s - s // 2 % 2 * 2 + p // near * 2))
        return send(array, homes)

    cos, sin = tables(length)
    ranks = jnp.argsort(pairs.reshape(-1))
    owner = ranks // slots
    relative = ((owner // near) ^ x) * near + ((owner % near) ^ low)
    order = (relative * slots + ranks % slots).astype(jnp.int32)

    def over_y(piece):
        return [flip(piece, bits) for bits in range(4, shards, 4)]

    y_bits = list(range(4, shards, 4))

    def put(*items):
        keys = [k for _, own_keys in items for k in own_keys]
        depth = items[0][0].shape[0] // len(items[0][1])
        places = jnp.stack([f ^ k for k in keys]).astype(jnp.int32)
        return assemble(places, [v for v, _ in items], depth)

    def put_pairs(both_x, both_y, other_x, other_y):
        items = [(both_x, [0, 2]), (other_x, [1, 3])]
        for bits, v, w in zip(y_bits, both_y, other_y):
            items += [(v, [bits, bits + 2]), (w, [bits + 1, bits + 3])]
        return put(*items)

    def head_columns(g):
        return jnp.concatenate(
            [lax.dynamic_slice_in_dim(w, g * mine, mine, 1) for w in (w_query, w_key, w_value)], 1
        )

    def ff_rows(g):
        return lax.dynamic_slice_in_dim(w_down, g * (part_ff // shards), part_ff // shards, 0)

    def own_heads(weight):
        sends, spreads = [], {}
        for p in range(planes):
            for s in range(shards):
                q = s // 2
                if q % near == p % near:
                    at = s // 4 * 4 + q // near * 2 + s % 2
                    if at != s:
                        sends.append((p * shards + s, p * shards + at))
                    for d in range(4, shards, 4):
                        spreads.setdefault(d, []).append((p * shards + at, p * shards + (at ^ d)))
        q = f // 2
        stays = (q % near == low) & (f // 4 * 4 + q // near * 2 + core == f)
        first = jnp.where(stays, weight, lax.ppermute(weight, both, sends))

        def rest(first):
            found = first
            for pairs_of in spreads.values():
                found = found + lax.ppermute(first, both, pairs_of)
            return found

        return first, rest

    cut = planes // 2
    early = list(range(1, cut + 1))
    late = [0, *range(cut + 1, planes)]
    early_types = [BF] * cut
    late_types = [F32] + [BF] * (planes - cut - 1)

    def gather_far(found):
        if near != 2:
            return [hop(found[0], j) for j in late[1:]]
        half = rows // 2
        return [hop(found[1][:half], 2), hop(found[2][half:], 1)]

    def joined(found, others):
        return found + (others if near != 2 else [jnp.concatenate(others, 0)])

    def reduce_far(parts):
        if near != 2:
            return [hop(parts[j], j) for j in late[1:]]
        half = rows // 2
        return [hop(parts[3][:half], 2), hop(parts[3][half:], 1)]

    def reduce_near(parts, received):
        if near != 2:
            return add_all(parts[0], received), [hop(parts[j], j) for j in early]
        half = rows // 2
        more = lambda part, other: (part.astype(F32) + other.astype(F32)).astype(BF)
        to_low = jnp.concatenate([more(parts[1][:half], received[0]), parts[1][half:]], 0)
        to_x = jnp.concatenate([parts[2][:half], more(parts[2][half:], received[1])], 0)
        return parts[0], [hop(to_low, 1), hop(to_x, 2)]

    def add_all(total, others):
        for other in others:
            total = total + other.astype(F32)
        return total

    region = lambda *values: lax.optimization_barrier(values)

    gate_own, gate_send = take_columns([group, group ^ near], [w_gate], shards, planes)
    gate_own_y = over_y(gate_own)
    up_own, up_send = take_columns([group, group ^ near], [w_up], shards, planes)
    up_own_y = over_y(up_own)
    stream_low = swap(tokens.reshape(rows, width))
    qkv_own = head_columns(group)
    qkv_other = flip(head_columns(group ^ near), 2)
    heads_first, heads_rest = own_heads(w_out)
    stream = stream_low.astype(F32)
    normed_one, inverse_one = normalize(stream)
    qkv_both = jnp.concatenate([qkv_own, qkv_other], 0)
    gate_parts, up_parts = [gate_own, gate_send, *gate_own_y], [up_own, up_send, *up_own_y]
    h1, stream_low, qkv_both, gate_parts, up_parts, heads_first, w_down = region(
        [normed_one.astype(BF)], stream_low, qkv_both, gate_parts, up_parts, heads_first, w_down
    )
    gu_own, gu_send, *gu_own_y = [jnp.concatenate(v, 1) for v in zip(gate_parts, up_parts)]

    h1 = h1 + [hop(h1[0], j) for j in early]
    qkv_y = over_y(qkv_both)
    qkv_pair = flip(qkv_both, 1)
    found = heads_rest(heads_first)
    h1, qkv_both, qkv_pair, w_down, gu_send = region(h1, qkv_both, qkv_pair, w_down, gu_send)

    others = gather_far(h1)
    down_own = ff_rows(group)
    down_other = flip(ff_rows(group ^ near), 2)
    others, found, down_own, down_other, qkv_y, gu_send, gu_own_y, teacher = region(
        others, found, down_own, down_other, qkv_y, gu_send, gu_own_y, teacher
    )
    h1 = joined(h1, others)

    gu_other = flip(gu_send, 2)
    down_both = jnp.concatenate([down_own, down_other], 0)
    down_y = over_y(down_both)
    other = flip(found, 1)
    qkv_y_pair = [flip(v, 1) for v in qkv_y]
    w_qkv = put_pairs(qkv_both, qkv_y, qkv_pair, qkv_y_pair)
    (qkv,) = project(h1, w_qkv, False, [F32])
    qkv = qkv.reshape(planes, seqs, slots, blk, 3 * mine)
    mixed, lse = attend(order, qkv, cos, sin, heads)
    even = core == 0
    w_out_mine = jnp.concatenate([jnp.where(even, found, other), jnp.where(even, other, found)], 0)
    group_types = [F32] + [BF] * (planes - 1)
    products = project([mixed[s].reshape(rows, mine) for s in range(planes)], w_out_mine, False, group_types)
    products, gu_other, down_both, down_y, gu_own, gu_own_y, teacher = region(
        products, gu_other, down_both, down_y, gu_own, gu_own_y, teacher
    )

    received = reduce_far(products)
    gate_other_y = over_y(gu_other[:, :part_ff])
    down_pair = flip(down_both, 1)
    gu_own_pair = flip(gu_own, 1)
    received, products, down_pair, gu_other, gate_other_y, down_y, gu_own_pair, gu_own_y = region(
        received, products, down_pair, gu_other, gate_other_y, down_y, gu_own_pair, gu_own_y
    )

    own, received = reduce_near(products, received)
    up_other_y = over_y(gu_other[:, part_ff:])
    gu_other_y = [jnp.concatenate(v, 1) for v in zip(gate_other_y, up_other_y)]
    down_y_pair = [flip(v, 1) for v in down_y]
    gu_own_y_pair = [flip(v, 1) for v in gu_own_y]
    residual = stream + add_all(own, received)
    normed_two, inverse_two = normalize(residual)
    h2, gu_other_y, gu_other, down_y_pair, gu_own_y_pair, valid = region(
        [normed_two.astype(BF)], gu_other_y, gu_other, down_y_pair, gu_own_y_pair, valid
    )

    h2 = h2 + [hop(h2[0], j) for j in early]
    gu_other_pair = flip(gu_other, 1)
    gu_items = [(gu_own, [0]), (gu_own_pair, [1]), (gu_other, [2]), (gu_other_pair, [3])]
    for bits, v, w, z in zip(y_bits, gu_own_y, gu_own_y_pair, gu_other_y):
        gu_items += [(v, [bits]), (w, [bits + 1]), (z, [bits + 2]), (flip(z, 1), [bits + 3])]
    down_w = put_pairs(down_both, down_y, down_pair, down_y_pair)
    gu_w = put(*gu_items)
    h2, gu_w, down_w, valid, teacher = region(h2, gu_w, down_w, valid, teacher)

    others = gather_far(h2)
    goal_low = swap(teacher.reshape(rows, width))
    kept, outs = mlp([h2[j] for j in early], gu_w, down_w, early_types, 2, 0)
    outs, kept, others = region(outs, kept, others)
    h2 = joined(h2, others)

    received = [hop(v, j) for v, j in zip(outs, early)]
    (h2_all, gates, ups, hidden_all), outs = mlp(
        [h2[j] for j in late], gu_w, down_w, late_types, 2, 1, kept
    )
    received, outs, h2_all, gates, ups, hidden_all, valid, goal_low = region(
        received, outs, h2_all, gates, ups, hidden_all, valid, goal_low
    )

    received = received + [hop(v, j) for v, j in zip(outs[1:], late[1:])]
    valid_float = swap(valid.reshape(rows, 1)).astype(F32)

    output = residual + add_all(outs[0], received)
    deviation = output - goal_low.astype(F32)
    grad_output = valid_float * deviation
    sums = jnp.stack([jnp.sum(grad_output * deviation), jnp.sum(valid_float)])
    sums0 = jnp.broadcast_to(sums[:, None, None], (2, 8, HD))
    sums0, grad_output, output = region(sums0, grad_output, output)

    sums = sums0
    for bits in range(1, planes):
        sums = sums + flip_ctx(sums0, bits)
    low_grad, low_output, sums = region(grad_output.astype(BF), output.astype(BF), sums)

    steps = [1 << b for b in reversed(range(2, shards.bit_length() - 1))]

    def halve(part, axis, bit, move, bits):
        half = part.shape[axis] // 2
        take = lambda k: lax.dynamic_slice_in_dim(part, k * half, half, axis)
        away = move(take(1 - bit), bits)
        return (take(bit).astype(F32) + away.astype(F32)).astype(BF)

    def parts(whole):
        return whole.reshape(2, near, shards // 4, 2, 2, unit, whole.shape[1])

    def across_y(part, axis):
        for step in steps:
            part = halve(part, axis, f // step % 2, flip, step)
        return part

    def across_far(part):
        return halve(part, 0, far, flip_ctx, near)

    def place_rows(part, place):
        homes = []
        for p in range(planes):
            for s in range(shards):
                homes.append(place(s % 2, s // 4, p // near, (s // 2 % 2) * near + p % near))
        return send(part, homes).astype(F32)

    def take(v, k, axis):
        return lax.dynamic_index_in_dim(v, k, axis, keepdims=False)

    def core_away(part):
        return flip(take(part.reshape(near, 2, 2, unit, part.shape[-1]), 1 - core, 2), 1)

    def core_joined(part, away):
        keep = take(part.reshape(near, 2, 2, unit, part.shape[-1]), core, 2)
        even = core == 0
        return jnp.concatenate([jnp.where(even, keep, away), jnp.where(even, away, keep)], -1)

    def column_pieces(part):
        return [take(take(part, x ^ (j // near), 1), low ^ (j % near), 0) for j in range(planes)]

    def columns_placed(pieces):
        places = jnp.stack([group ^ j for j in range(planes)]).astype(jnp.int32)
        return assemble(places, pieces, unit).reshape(planes, unit, -1)

    dm = [low_grad] + [hop(low_grad, j) for j in early]
    for bits in [1, *(1 << b for b in range(2, shards.bit_length() - 1))]:
        sums = sums + flip(sums, bits)
    dm, sums, low_output = region(dm, sums, low_output)

    others = gather_far(dm)
    kept, backs = mlp_back([dm[j] for j in early], gates, ups, gu_w, down_w, early_types, 2, 0)
    backs, kept, others, sums, low_output = region(backs, kept, others, sums, low_output)
    dm = joined(dm, others)

    received = [hop(v, j) for v, j in zip(backs, early)]
    dm_runs = [dm[j] for j in early + late]
    away = flip(outer([hidden_all], dm_runs, 1 - core, True, None, 2), 1)
    (_, dg_all, du_all), backs = mlp_back(
        [dm[j] for j in late], gates, ups, gu_w, down_w, late_types, 2, 1, kept
    )
    g_down = outer([hidden_all], dm_runs, core, True, away, 2)
    received, backs, g_down, dg_all, du_all, h2_all, low_output = region(
        received, backs, g_down, dg_all, du_all, h2_all, low_output
    )

    received = received + [hop(v, j) for v, j in zip(backs[1:], late[1:])]
    activations = swap(low_output)
    g_down = across_y(g_down.reshape(2, shards // 4, part_ff // shards, width), 1)
    gate_half = outer([h2_all], [dg_all], 1 - core, False)
    up_half = outer([h2_all], [du_all], 1 - core, False)
    grad_two = add_all(backs[0], received)
    grad_residual = grad_output + norm_back(grad_two, normed_two, inverse_two)
    dab, gate_half, up_half, g_down, dg_all, du_all, activations = region(
        [grad_residual.astype(BF)], gate_half, up_half, g_down, dg_all, du_all, activations
    )

    dab = dab + [hop(dab[0], j) for j in early]
    gate_away, up_away = flip(gate_half, 1), flip(up_half, 1)
    g_gate = outer([h2_all], [dg_all], core, False, gate_away)
    dab, g_gate, up_away, du_all, g_down = region(dab, g_gate, up_away, du_all, g_down)

    others = gather_far(dab)
    g_gate = across_y(parts(g_gate), 2)
    g_up = outer([h2_all], [du_all], core, False, up_away)
    others, g_up, g_down = region(others, g_up, g_down)
    dab = joined(dab, others)

    up_first, up_second = jnp.split(parts(g_up), 2, -1)
    up_first = across_y(up_first, 2)
    g_down = across_far(g_down)
    (do,) = project(dab, w_out_mine, True, [BF])
    dqkv = attend_back(order, qkv, lse, do.reshape(planes, seqs, slots, blk, mine), cos, sin, heads)
    dqkv = dqkv.reshape(planes * rows, 3 * mine)
    qkv_half = outer(h1, [dqkv], 1 - core, False)
    mixed = mixed.reshape(planes * rows, mine)
    out_half = outer([mixed], dab, 1 - core, True)
    dqkv, qkv_half, out_half, g_gate, g_down, up_first, up_second, sums = region(
        dqkv, qkv_half, out_half, g_gate, g_down, up_first, up_second, sums
    )

    qkv_away, out_away = flip(qkv_half, 1), flip(out_half, 1)
    backs = project([dqkv[i * rows : (i + 1) * rows] for i in range(planes)], w_qkv, True, group_types)
    up_second = across_y(up_second, 2)
    sums = sums + flip(sums, 2)
    gate_first, gate_second = jnp.split(g_gate, 2, -1)
    gate_first = across_far(gate_first)
    backs, dqkv, qkv_away, out_away, up_second, gate_first, gate_second, sums = region(
        backs, dqkv, qkv_away, out_away, up_second, gate_first, gate_second, sums
    )

    gate_second = across_far(gate_second)
    g_up = jnp.concatenate([up_first, up_second], -1)
    received = reduce_far(backs)
    g_qkv = parts(outer(h1, [dqkv], core, False, qkv_away))
    g_out = outer([mixed], dab, core, True, out_away)
    received, backs, g_qkv, g_out, g_down, gate_first, gate_second, g_up = region(
        received, backs, g_qkv, g_out, g_down, gate_first, gate_second, g_up
    )

    own, received = reduce_near(backs, received)
    g_up = across_far(g_up)
    g_out = across_y(g_out, 0)
    g_gate = jnp.concatenate([gate_first, gate_second], -1)
    g_down = place_rows(
        g_down.reshape(ff // world, width),
        lambda core, y, far, g: far * (shards // 2) * planes + (core * (shards // 4) + y) * planes + g,
    )
    grad_one = add_all(own, received)
    grad_stream = grad_residual + norm_back(grad_one, normed_one, inverse_one)
    low_stream, g_out, g_qkv, g_gate, g_up, g_down = region(
        grad_stream.astype(BF), g_out, g_qkv, g_gate, g_up, g_down
    )

    grad_low = swap(low_stream)
    g_qkv = across_y(g_qkv, 2)
    g_out = across_far(g_out)
    gate_core, up_core = core_away(g_gate), core_away(g_up)
    pieces = [column_pieces(core_joined(v, w)) for v, w in ((g_gate, gate_core), (g_up, up_core))]
    pieces = [jnp.concatenate(v, 1) for v in zip(*pieces)]
    grad_low, g_qkv, g_out, pieces = region(grad_low, g_qkv, g_out, pieces)

    g_qkv = across_far(g_qkv)
    g_out = place_rows(g_out, lambda core, y, far, g: g * shards + (core * (shards // 4) + y) * 2 + far)
    pieces = [hop(v, j) if j else v for j, v in enumerate(pieces)]
    pieces, g_qkv, g_out = region(pieces, g_qkv, g_out)
    qkv_pieces = column_pieces(core_joined(g_qkv, core_away(g_qkv)))
    qkv_pieces, pieces = region(qkv_pieces, pieces)
    qkv_pieces = [hop(v, j) if j else v for j, v in enumerate(qkv_pieces)]
    count = sums[1, 0, 0]
    loss = sums[0, 0, 0] / (count * width)
    factor = (rows * world) / count
    grad_input = grad_low.astype(F32) * factor
    ff_order = lambda v: v.reshape(planes, unit, shards, -1).transpose(1, 2, 0, 3).reshape(unit, ff)
    placed, qkv_pieces = region(columns_placed(pieces), qkv_pieces)
    g_gate = ff_order(placed[:, :, :part_ff]).astype(F32)
    g_up = ff_order(placed[:, :, part_ff:]).astype(F32)
    g_qkv = columns_placed(qkv_pieces).reshape(planes, unit, 3, mine).transpose(2, 1, 0, 3)
    g_qkv = g_qkv.reshape(3, unit, width).astype(F32)
    return (
        activations.reshape(tokens.shape),
        loss,
        grad_input.reshape(tokens.shape),
        g_qkv[0] * factor,
        g_qkv[1] * factor,
        g_qkv[2] * factor,
        g_out * factor,
        g_gate * factor,
        g_up * factor,
        g_down * factor,
    )


def solution(mesh):
    tokens = P("fsdp", "ctx", None, None)
    weight = P("fsdp", None)
    grad = P(("ctx", "fsdp"), None)
    in_specs = (tokens, P(), P("fsdp", "ctx", None), tokens) + (weight,) * 7
    out_specs = (tokens, P(), tokens) + (grad,) * 7
    step = functools.partial(body, mesh.shape["ctx"], mesh.shape["fsdp"])
    return jax.shard_map(step, mesh=mesh, in_specs=in_specs, out_specs=out_specs, check_vma=False)
```
